32 devices in a mesh: img: 8 (over z, y), win: 4 (over x, core).
Axes of the slice: x: 2, y: 2, z: 4, core: 2. Of those that a mesh axis runs over, the one named last changes fastest.
Arguments:
- tokens: bfloat16 [256, 4, 49, 384], P('img', 'win'), may hold values from -6 to 6
- cotangent: bfloat16 [256, 4, 49, 384], P('img', 'win'), may hold values from -6 to 6
- crop_counts: int32 [8], P('img'), may hold values from 8 to 32, as said below
- crop_extent: int32 [256, 2], P('img'), may hold values from 10 to 14
- norm_gain: float32 [2, 2, 384], replicated, may hold values from 0.1 to 1.9
- norm_bias: float32 [2, 2, 384], replicated, may hold values from -3 to 3
- qkv_weight: bfloat16 [2, 384, 1152], replicated, may hold values from -0.3125 to 0.3125
- qv_bias: float32 [2, 2, 384], replicated, may hold values from -3 to 3
- rel_table: float32 [2, 169, 12], replicated, may hold values from -5 to 5
- proj_weight: bfloat16 [2, 384, 384], replicated, may hold values from -1.25 to 1.25
- out_bias: float32 [2, 2, 384], replicated, may hold values from -3 to 3
- fc1_weight: bfloat16 [2, 384, 1536], replicated, may hold values from -0.3125 to 0.3125
- fc1_bias: float32 [2, 1536], replicated, may hold values from -3 to 3
- fc2_weight: bfloat16 [2, 1536, 384], replicated, may hold values from -0.15625 to 0.15625
Outputs:
- output: bfloat16 [256, 4, 49, 384], P('img', 'win')
- input_grad: bfloat16 [256, 4, 49, 384], P('img', 'win')
- grad_norm_gain: float32 [2, 2, 384], replicated
- grad_norm_bias: float32 [2, 2, 384], replicated
- grad_qkv_weight: float32 [2, 384, 1152], replicated
- grad_qv_bias: float32 [2, 2, 384], replicated
- grad_rel_table: float32 [2, 169, 12], replicated
- grad_proj_weight: float32 [2, 384, 384], replicated
- grad_out_bias: float32 [2, 2, 384], replicated
- grad_fc1_weight: float32 [2, 384, 1536], replicated
- grad_fc1_bias: float32 [2, 1536], replicated
- grad_fc2_weight: float32 [2, 1536, 384], replicated
The draws below stay inside these ranges and needn't reach their ends.
Inputs may be any that keep to these rules, and one draw needn't show every extreme that they name: `crop_counts`: slots of an image group from this count on are empty; in every draw some group is full.
All inputs are finite; a program needn't handle non-finite values.
Results may differ from the reference program's by a relative error of at most 0.017.
Values may be sent and summed in bfloat16 or wider, within the bound.
A program may use at most 256 MiB of HBM per device.

```python
import math
import jax
import jax.numpy as jnp
from jax import lax

D = 384
HEADS = 12
HEAD_DIM = 32
FF = 1536
WINDOW = 7
SHIFT = 3
CROPS_DEV = 32
SLOTS = 256
N_IMG = 8
N_WIN = 4


def draw_crop_counts(key, part):
    key = jax.random.fold_in(key, 11)
    count_key, full_key = jax.random.split(key)
    lowest = max(CROPS_DEV // 4, 1)
    counts = jax.random.randint(count_key, (N_IMG,), lowest, CROPS_DEV + 1)
    full_group = jax.random.randint(full_key, (), 0, N_IMG)
    return jnp.where(jnp.arange(N_IMG) == full_group, CROPS_DEV, counts).astype(jnp.int32)


def set_ends(values, key, smallest, top_value):
    spot = [jax.random.randint(jax.random.fold_in(key, axis), (), 0, length) for axis, length in enumerate(values.shape)]
    widest = values.shape.index(max(values.shape))
    next_to = spot[:widest] + [(spot[widest] + 1) % values.shape[widest]] + spot[widest + 1:]
    return values.at[tuple(spot)].set(smallest).at[tuple(next_to)].set(top_value)


def block_scale(key, shape, shards, least, high):
    def one(dim, shards_of):
        steps = jax.random.uniform(jax.random.fold_in(jax.random.fold_in(key, 6), dim), (shards_of,), jnp.float32, least / len(shards), high / len(shards))
        return jnp.repeat(jnp.exp(steps), shape[dim] // shards_of).reshape((-1,) + (1,) * (len(shape) - dim - 1))

    level = one(*shards[0])
    for cut in shards[1:]:
        level = level * one(*cut)
    return level


def normal_values(rng, shape, width, limit, pieces=(), held_as=jnp.bfloat16):
    level = block_scale(rng, shape, pieces, -0.22, 0.18) if pieces else 1.0
    values = jax.random.normal(rng, shape, jnp.float32) * width * level
    return jnp.minimum(jnp.maximum(values, -limit), limit).astype(held_as)


def setup_inputs(seed: int = 0) -> dict:
    key_list = jax.random.split(jax.random.key(seed), 15)
    return {
        "tokens": normal_values(key_list[0], (SLOTS, N_WIN, WINDOW * WINDOW, D), 1.0, 6.0, ((0, 8), (1, 4))),
        "cotangent": normal_values(key_list[1], (SLOTS, N_WIN, WINDOW * WINDOW, D), 1.0, 6.0, ((0, 8), (1, 4))),
        "crop_counts": draw_crop_counts(jax.random.fold_in(key_list[14], 71), 0),
        "crop_extent": set_ends(jax.random.randint(key_list[3], (SLOTS, 2), 10, 15), jax.random.fold_in(key_list[3], 1), 10, 14).astype(jnp.int32),
        "norm_gain": jnp.clip(1.0 + 0.18 * jax.random.normal(key_list[4], (2, 2, D), jnp.float32), 0.1, 1.9),
        "norm_bias": normal_values(key_list[5], (2, 2, D), 0.5, 3.0, (), jnp.float32),
        "qkv_weight": normal_values(key_list[6], (2, D, 3 * D), D ** -0.5, 0.3125),
        "qv_bias": normal_values(key_list[7], (2, 2, D), 0.5, 3.0, (), jnp.float32),
        "rel_table": normal_values(key_list[8], (2, (2 * WINDOW - 1) * (2 * WINDOW - 1), HEADS), 1.0, 5.0, (), jnp.float32),
        "proj_weight": normal_values(key_list[9], (2, D, D), (D // 16) ** -0.5, 1.25),
        "out_bias": normal_values(key_list[10], (2, 2, D), 0.5, 3.0, (), jnp.float32),
        "fc1_weight": normal_values(key_list[11], (2, D, FF), D ** -0.5, 0.3125),
        "fc1_bias": normal_values(key_list[12], (2, FF), 0.5, 3.0, (), jnp.float32),
        "fc2_weight": normal_values(key_list[13], (2, FF, D), FF ** -0.5, 0.15625),
    }


@jax.custom_vjp
def low(v):
    return lax.optimization_barrier(v.astype(jnp.bfloat16)).astype(jnp.float32)

@jax.custom_vjp
def low_back(v):
    return v

def low_keep(v):
    return (low(v), None)

def low_pass(kept, grad):
    return (grad,)

def back_keep(v):
    return (v, None)

def back_low(kept, grad):
    return (low(grad),)
low.defvjp(low_keep, low_pass)
low_back.defvjp(back_keep, back_low)
highest = lax.Precision.HIGHEST
norm_eps = 1e-05

def layer_norm(values, gains, shifts):
    row_mean = lax.optimization_barrier(jnp.mean(values, -1, keepdims=True))
    centred = values - row_mean
    row_var = lax.optimization_barrier(jnp.mean(centred * centred, -1, keepdims=True))
    return centred * lax.rsqrt(row_var + norm_eps) * gains + shifts

def to_grid(windows):
    crops_here = windows.shape[0]
    parted = windows.reshape(crops_here, 2, 2, WINDOW, WINDOW, windows.shape[-1])
    return parted.transpose(0, 1, 3, 2, 4, 5).reshape(crops_here, 2 * WINDOW, 2 * WINDOW, windows.shape[-1])

def to_windows(grid_cells):
    crops_here = grid_cells.shape[0]
    parted = grid_cells.reshape(crops_here, 2, WINDOW, 2, WINDOW, grid_cells.shape[-1])
    return parted.transpose(0, 1, 3, 2, 4, 5).reshape(crops_here, 4, WINDOW * WINDOW, grid_cells.shape[-1])

def position_bias(rel_bias_table):
    places = jnp.arange(WINDOW * WINDOW).astype(jnp.int32)
    row_part = places // WINDOW
    col_part = places % WINDOW
    table_side = 2 * WINDOW - 1
    rel_index = (row_part[:, None] - row_part[None, :] + WINDOW - 1) * table_side + col_part[:, None] - col_part[None, :] + WINDOW - 1
    return jnp.transpose(rel_bias_table[rel_index.astype(jnp.int32)], (2, 0, 1))

def block(tokens_in, group_ids, params):
    gains, shifts, w_qkv, qv_biases, rel_bias_table, w_proj, bias_pair, w_up, up_bias, w_down = params
    crops_here = tokens_in.shape[0]
    normed = low(layer_norm(tokens_in, gains[0], shifts[0]))
    projected = jnp.einsum('nwtd,de->nwte', normed, w_qkv, precision=highest)
    queries = low(low_back(projected[..., :D] + qv_biases[0]))
    keys_low = low(low_back(projected[..., D:2 * D]))
    values = low(low_back(projected[..., 2 * D:] + qv_biases[1]))
    head_shape = (crops_here, 4, WINDOW * WINDOW, HEADS, HEAD_DIM)
    scores = jnp.einsum('nwihe,nwjhe->nwhij', queries.reshape(head_shape), keys_low.reshape(head_shape), precision=highest)
    scores = scores * HEAD_DIM ** (-0.5) + position_bias(rel_bias_table)
    allowed = group_ids[:, :, None, :, None] == group_ids[:, :, None, None, :]
    scores = low_back(jnp.where(allowed, scores, -1e+30))
    row_top = lax.optimization_barrier(jnp.max(scores, -1, keepdims=True))
    exp_terms = jnp.exp(scores - row_top)
    attn_probs = low(exp_terms / lax.optimization_barrier(jnp.sum(exp_terms, -1, keepdims=True)))
    mixed_heads = jnp.einsum('nwhij,nwjhe->nwihe', attn_probs, values.reshape(head_shape), precision=highest)
    mixed_heads = low(low_back(mixed_heads.reshape(tokens_in.shape)))
    branch_out = jnp.einsum('nwtd,de->nwte', mixed_heads, w_proj, precision=highest) + bias_pair[0]
    middle = tokens_in + low_back(branch_out)
    normed_two = low(layer_norm(middle, gains[1], shifts[1]))
    inner_pre = low_back(jnp.einsum('nwtd,df->nwtf', normed_two, w_up, precision=highest) + up_bias)
    hidden = low(jax.nn.gelu(inner_pre, approximate=False))
    down_out = jnp.einsum('nwtf,fd->nwtd', hidden, w_down, precision=highest) + bias_pair[1]
    return middle + low_back(down_out)

def crop_layers(weights, tokens_in, extent):
    block_one = tuple((weight[0] for weight in weights))
    block_two = tuple((weight[1] for weight in weights))
    grid_side = 2 * WINDOW
    places = jnp.arange(grid_side).astype(jnp.int32)
    valid_grid = (places[None, :, None] < extent[:, 0, None, None]) & (places[None, None, :] < extent[:, 1, None, None])
    plain_ids = to_windows(valid_grid.astype(jnp.int32)[..., None])[..., 0]
    first_out = low(low_back(block(tokens_in, plain_ids, block_one)))
    rolled_in = to_windows(jnp.roll(to_grid(first_out), (-SHIFT, -SHIFT), (1, 2)))
    region = (places >= grid_side - WINDOW).astype(jnp.int32) + (places >= grid_side - SHIFT).astype(jnp.int32)
    valid_rolled = jnp.roll(valid_grid, (-SHIFT, -SHIFT), (1, 2)).astype(jnp.int32)
    shift_grid = 2 * (3 * region[:, None] + region[None, :])[None] + valid_rolled
    shift_ids = to_windows(shift_grid[..., None])[..., 0]
    second_out = block(rolled_in, shift_ids, block_two)
    return to_windows(jnp.roll(to_grid(second_out), (SHIFT, SHIFT), (1, 2)))

def reference(tokens, cotangent, crop_counts, crop_extent, norm_gain, norm_bias, qkv_weight, qv_bias, rel_table, proj_weight, out_bias, fc1_weight, fc1_bias, fc2_weight):
    weights = (norm_gain.astype(jnp.float32), norm_bias.astype(jnp.float32), qkv_weight.astype(jnp.float32), qv_bias.astype(jnp.float32), rel_table.astype(jnp.float32), proj_weight.astype(jnp.float32), out_bias.astype(jnp.float32), fc1_weight.astype(jnp.float32), fc1_bias.astype(jnp.float32), fc2_weight.astype(jnp.float32))
    slot_index = jnp.arange(SLOTS).astype(jnp.int32)
    live_slot = (slot_index % CROPS_DEV < crop_counts[slot_index // CROPS_DEV]).astype(jnp.float32)[:, None, None, None]
    group_size = math.gcd(SLOTS, 8)

    def forward(params, tokens_in):

        def one_group(pair_args):
            return crop_layers(params, pair_args[0], pair_args[1])
        shaped = tokens_in.reshape(SLOTS // group_size, group_size, 4, WINDOW * WINDOW, D)
        extents = crop_extent.reshape(SLOTS // group_size, group_size, 2)
        result = lax.map(jax.checkpoint(one_group), (shaped, extents))
        return result.reshape(tokens_in.shape)
    result, pullback = jax.vjp(forward, weights, tokens.astype(jnp.float32))
    gradients, input_grad = pullback(cotangent.astype(jnp.float32) * live_slot)
    output = (result * live_slot).astype(jnp.bfloat16)
    return (output, input_grad.astype(jnp.bfloat16), gradients[0], gradients[1], gradients[2], gradients[3], gradients[4], gradients[5], gradients[6], gradients[7], gradients[8], gradients[9])
```

```python
import jax
import jax.numpy as jnp
from jax import lax
from jax.experimental import pallas as pl
from jax.experimental.pallas import tpu as pltpu
from jax.sharding import PartitionSpec as P

D = 384
FF = 1536
HEADS = 12
HEAD_DIM = 32
WINDOW = 7
SHIFT = 3
CELLS = WINDOW * WINDOW
SIDE = 2 * WINDOW
HALF = 16
ROWS = CELLS * HALF
LANES = 128
GROUPS = 3
KEYS = 56
SLOT = 64
SLABS = 12
NEG = -1e30
LOG2E = 1.4426950408889634
SCALE = HEAD_DIM**-0.5
MESH = pl.DeviceIdType.MESH

bf16 = jnp.bfloat16
f32 = jnp.float32
VMEM = pltpu.VMEM


def mm(a, b):
    return lax.dot_general(a, b, (((1,), (0,)), ((), ())), preferred_element_type=f32)


def mm_bt(a, b):
    return lax.dot_general(a, b, (((1,), (1,)), ((), ())), preferred_element_type=f32)


def mm_at(a, b):
    return lax.dot_general(a, b, (((0,), (0,)), ((), ())), preferred_element_type=f32)


def norm(x):
    centred = x - jnp.mean(x, -1, keepdims=True)
    rstd = lax.rsqrt(jnp.mean(centred * centred, -1, keepdims=True) + 1e-5)
    return centred * rstd, rstd


def norm_back(xh, rstd, dn, gain):
    e = dn * gain
    mean_e = jnp.mean(e, -1, keepdims=True)
    mean_ex = jnp.mean(e * xh, -1, keepdims=True)
    dx = rstd * (e - mean_e - xh * mean_ex)
    return dx, jnp.sum(dn * xh, 0, keepdims=True), jnp.sum(dn, 0, keepdims=True)


def gelu(u):
    phi = 0.5 + 0.5 * lax.erf(u * 0.7071067811865476)
    return u * phi, phi


def gelu_slope(u, phi):
    return phi + u * jnp.exp2(u * u * (-0.5 * LOG2E)) * 0.3989422804014327


def spread(rows):
    head = lax.broadcasted_iota(jnp.int32, rows.shape, 1) // HEAD_DIM
    zero = jnp.zeros_like(rows)
    return jnp.concatenate([jnp.where(head == h, rows, zero) for h in range(4)], 0)


def gather_heads(rows):
    head = lax.broadcasted_iota(jnp.int32, (KEYS, LANES), 1) // HEAD_DIM
    out = rows[:KEYS]
    for h in range(1, 4):
        out = jnp.where(head == h, rows[SLOT * h : SLOT * h + KEYS], out)
    return out


def to_windows(ref, slot, part):
    parted = part.reshape(CELLS, 2, 8, LANES)
    for cg in range(2):
        ref[cg, slot, 0 : CELLS * 8, :] = parted[:, cg].reshape(CELLS * 8, LANES)


def from_windows(ref, slot):
    parts = [ref[cg, slot, 0 : CELLS * 8, :].reshape(CELLS, 1, 8, LANES) for cg in range(2)]
    return jnp.concatenate(parts, 1).reshape(ROWS, LANES)


def cells(shifted):
    win = lax.axis_index("win")
    j = lax.broadcasted_iota(jnp.int32, (KEYS, LANES), 0)
    i = lax.broadcasted_iota(jnp.int32, (KEYS, LANES), 1) % SLOT
    top, left = WINDOW * (win // 2), WINDOW * (win % 2)
    places = [top + j // WINDOW, left + j % WINDOW, top + i // WINDOW, left + i % WINDOW]
    if not shifted:
        return places, None
    region = [(v >= SIDE - WINDOW).astype(jnp.int32) + (v >= SIDE - SHIFT).astype(jnp.int32) for v in places]
    apart = (region[0] != region[2]) | (region[1] != region[3])
    moved = [jnp.where(v + SHIFT >= SIDE, v + SHIFT - SIDE, v + SHIFT) for v in places]
    return moved, jnp.where(apart, NEG, 0.0)


def forward(step, block, shifted, x, refs, keep_n1=None, keep_n2=None, keep_gelu=None, keep_u=None):
    (ext, gain, beta, wqkv, qvb, bias, wp, ob, w1, b1, w2, xs, qw, ss, pr, os, o16, mid) = refs
    xh, _ = norm(x)
    n1 = (xh * gain[block, 0:1, :] + beta[block, 0:1, :]).astype(bf16)
    if keep_n1 is not None:
        keep_n1[step] = n1
    proj = mm(n1, wqkv[...])
    q = (proj[:, :D] + qvb[block, 0:1, :]) * (SCALE * LOG2E)
    k = proj[:, D : 2 * D]
    v = proj[:, 2 * D :] + qvb[block, 1:2, :]
    for g in range(GROUPS):
        cut = slice(LANES * g, LANES * (g + 1))
        to_windows(xs, g, q[:, cut])
        to_windows(xs, GROUPS + g, k[:, cut])
        to_windows(xs, 2 * GROUPS + g, v[:, cut])
    places, apart = cells(shifted)
    if apart is not None:
        apart = jnp.concatenate([apart, apart], 1)

    def scores(w, carry):
        cg, c = w // 8, w % 8
        rows, cols = ext[step * HALF + w, 0], ext[step * HALF + w, 1]
        valid_j = (places[0] < rows) & (places[1] < cols)
        valid_i = (places[2] < rows) & (places[3] < cols)
        mask = jnp.where(valid_i == valid_j, 0.0, NEG)
        mask = jnp.concatenate([mask, mask], 1)
        if apart is not None:
            mask = mask + apart
        for g in range(GROUPS):
            qs, ks, vs = (
                xs[cg, GROUPS * n + g, pl.ds(c, SLOT, stride=8), :].astype(bf16) for n in range(3)
            )
            qw[w, g] = qs
            qw[w, GROUPS + g] = ks
            qw[w, 2 * GROUPS + g] = vs
            ss[w, g] = mm_bt(ks[:KEYS], spread(qs)) + bias[g] + mask
        return carry

    lax.fori_loop(0, HALF, scores, 0, unroll=2)

    def softmax(w, carry):
        for g in range(GROUPS):
            s = ss[w, g]
            e = jnp.exp2(s - jnp.max(s, 0, keepdims=True))
            pr[w, g] = (e * (1.0 / jnp.sum(e, 0, keepdims=True))).astype(bf16)
        return carry

    lax.fori_loop(0, HALF, softmax, 0)

    def mix(w, carry):
        cg, c = w // 8, w % 8
        for g in range(GROUPS):
            os[cg, g, pl.ds(c, KEYS, stride=8), :] = gather_heads(
                mm_at(pr[w, g], qw[w, 2 * GROUPS + g][:KEYS])
            )
        return carry

    lax.fori_loop(0, HALF, mix, 0)
    for g in range(GROUPS):
        o16[:, LANES * g : LANES * (g + 1)] = from_windows(os, g).astype(bf16)
    middle = x + (mm(o16[...], wp[...]) + ob[block, 0:1, :])
    mid[...] = middle
    xh2, _ = norm(middle)
    n2 = (xh2 * gain[block, 1:2, :] + beta[block, 1:2, :]).astype(bf16)
    if keep_n2 is not None:
        keep_n2[step] = n2
    y = middle + ob[block, 1:2, :]
    for part in range(3):
        cut = slice(512 * part, 512 * (part + 1))
        u = mm(n2, w1[:, cut]) + b1[block : block + 1, cut]
        if keep_u is not None:
            keep_u[:, cut] = u.astype(bf16)
        z, phi = gelu(u)
        z = z.astype(bf16)
        if keep_gelu is not None:
            keep_gelu[0][step, :, cut] = z
            keep_gelu[1][:, cut] = gelu_slope(u, phi).astype(bf16)
        y = y + mm(z, w2[cut, :])
    return y


def backward(step, block, x, mid, dy, refs, slope, tick=lambda point: None):
    (gain, wqkv, wp, w1, w2, xs, qw, pr, dos, dss, dm_all, du_all, da_all, dp_all, small, dbias) = refs

    def add_small(row, value):
        small[row : row + 1, :] += value

    dm = dy.astype(bf16)
    dm_all[step] = dm
    add_small(7, jnp.sum(dm.astype(f32), 0, keepdims=True))
    dn2 = jnp.zeros((ROWS, D), f32)
    for part in range(4):
        cut = slice(384 * part, 384 * (part + 1))
        du = (mm_bt(dm, w2[cut, :]) * slope(cut)).astype(bf16)
        du_all[step, :, cut] = du
        add_small(8 + part, jnp.sum(du.astype(f32), 0, keepdims=True))
        dn2 = dn2 + mm_bt(du, w1[:, cut])
        if part % 2:
            tick(1 + part // 2)
    xh2, rstd2 = norm(mid)
    dx2, dgain, dbeta = norm_back(xh2, rstd2, dn2, gain[block, 1:2, :])
    add_small(1, dgain)
    add_small(3, dbeta)
    dmid = dy + dx2
    da = dmid.astype(bf16)
    da_all[step] = da
    add_small(6, jnp.sum(da.astype(f32), 0, keepdims=True))
    do = mm_bt(da, wp[...])
    for g in range(GROUPS):
        to_windows(dos, g, do[:, LANES * g : LANES * (g + 1)])

    tick(3)

    def probs_back(w, carry):
        cg, c = w // 8, w % 8
        for g in range(GROUPS):
            d = spread(dos[cg, g, pl.ds(c, SLOT, stride=8), :].astype(bf16))
            p16 = pr[w, g]
            p = p16.astype(f32)
            t = p * mm_bt(qw[w, 2 * GROUPS + g][:KEYS], d)
            ds = (t - p * jnp.sum(t, 0, keepdims=True)).astype(bf16)
            dss[w, g] = ds
            dbias[g] += ds.astype(f32)
            xs[cg, 2 * GROUPS + g, pl.ds(c, KEYS, stride=8), :] = mm(p16, d)
        return carry

    lax.fori_loop(0, HALF, probs_back, 0, unroll=2)

    tick(4)

    def scores_back(w, carry):
        cg, c = w // 8, w % 8
        for g in range(GROUPS):
            ds = dss[w, g]
            dk = mm(ds, spread(qw[w, g])) * (1.0 / LOG2E)
            dq = gather_heads(mm_at(ds, qw[w, GROUPS + g][:KEYS])) * SCALE
            xs[cg, g, pl.ds(c, KEYS, stride=8), :] = dq
            xs[cg, GROUPS + g, pl.ds(c, KEYS, stride=8), :] = dk
        return carry

    lax.fori_loop(0, HALF, scores_back, 0)
    tick(5)
    for n in range(3 * GROUPS):
        dp_all[step, :, LANES * n : LANES * (n + 1)] = from_windows(xs, n).astype(bf16)
    dp = dp_all[step]
    add_small(4, jnp.sum(dp[:, :D].astype(f32), 0, keepdims=True))
    add_small(5, jnp.sum(dp[:, 2 * D :].astype(f32), 0, keepdims=True))
    dn1 = mm_bt(dp, wqkv[...])
    tick(6)
    xh1, rstd1 = norm(x)
    dx1, dgain, dbeta = norm_back(xh1, rstd1, dn1, gain[block, 0:1, :])
    add_small(0, dgain)
    add_small(2, dbeta)
    return dmid + dx1


def weight_grads(n1, n2, o16, z, dm, du, da, dp, out):
    rows = 2 * ROWS

    def flat(ref, cut=slice(None)):
        return ref[:, :, cut].reshape(rows, -1)

    for j in range(2):
        up = mm_at(flat(n2), flat(du, slice(768 * j, 768 * (j + 1)))).astype(bf16)
        out[2 * D * j : 2 * D * j + D, :] = up[:, :D]
        out[2 * D * j + D : 2 * D * (j + 1), :] = up[:, D:]
    for j in range(3):
        out[4 * D + 512 * j : 4 * D + 512 * (j + 1), :] = mm_at(
            flat(z, slice(512 * j, 512 * (j + 1))), flat(dm)
        ).astype(bf16)
    qkv = mm_at(flat(n1), flat(dp)).astype(bf16)
    for j in range(3):
        out[D * (8 + j) : D * (9 + j), :] = qkv[:, D * j : D * (j + 1)]
    out[11 * D : 12 * D, :] = mm_at(flat(o16), flat(da)).astype(bf16)


def first_kernel(
    ext, x_ref, gain, beta, wqkv, qvb, bias, wp, ob, w1, b1, w2,
    y_ref, qw, pr, o16, mid, u_ref, xs, ss, os,
):
    step = pl.program_id(0)

    @pl.when(step == 0)
    def _():
        xs[...] = jnp.zeros_like(xs)

    x = x_ref[...].reshape(ROWS, D).astype(f32)
    y = forward(
        step, 0, False, x, (ext, gain, beta, wqkv, qvb, bias, wp, ob, w1, b1, w2, xs, qw, ss, pr, os, o16, mid), keep_u=u_ref
    )
    y_ref[...] = y.astype(bf16).reshape(y_ref.shape)


def second_kernel(
    ext, count, x_ref, cot_ref, gain, beta, wqkv, qvb, bias, wp, ob, w1, b1, w2,
    y_ref, dx_ref, grads, small, dbias,
    xs, qw, ss, pr, os, mid, slope, dos, dss, n1, n2, o16, z, dm, du, da, dp,
):
    step = pl.program_id(0)

    @pl.when(step == 0)
    def _():
        xs[...] = jnp.zeros_like(xs)
        dos[...] = jnp.zeros_like(dos)
        small[...] = jnp.zeros_like(small)
        dbias[...] = jnp.zeros_like(dbias)

    x = x_ref[...].reshape(ROWS, D).astype(f32)
    live = lax.broadcasted_iota(jnp.int32, (CELLS, HALF, 1), 1) + step * HALF < count[0]
    y = forward(
        step, 1, True, x,
        (ext, gain, beta, wqkv, qvb, bias, wp, ob, w1, b1, w2, xs, qw, ss, pr, os, o16.at[step], mid),
        n1, n2, (z, slope),
    )
    y_ref[...] = jnp.where(live, y.reshape(CELLS, HALF, D), 0.0).astype(bf16)
    dy = jnp.where(live, cot_ref[...].astype(f32), 0.0).reshape(ROWS, D)
    dx = backward(
        step, 1, x, mid[...], dy,
        (gain, wqkv, wp, w1, w2, xs, qw, pr, dos, dss, dm, du, da, dp, small, dbias),
        lambda cut: slope[:, cut].astype(f32),
    )
    dx_ref[...] = dx.astype(bf16).reshape(dx_ref.shape)

    @pl.when(step == 1)
    def _():
        weight_grads(n1, n2, o16, z, dm, du, da, dp, grads)


def third_kernel(
    x_ref, dy_ref, qw, pr, o_ref, mid, u_ref, gain, beta, wqkv, wp, w1, w2, other_ref,
    dx_ref, grads, small, dbias, other_out,
    xs, dos, dss, n1, n2, o16, z, dm, du, da, dp, other_sum, landing, send, recv, free, local, loads,
):
    step = pl.program_id(0)
    exchange = Exchange(other_sum, landing, send, recv, free)
    ticks = 7

    def kept(half):
        rows = pl.ds(half * ROWS, ROWS)
        return (
            pltpu.make_async_copy(u_ref.at[rows], z.at[half], loads.at[0, half]),
            pltpu.make_async_copy(o_ref.at[rows], o16.at[half], loads.at[1, half]),
        )

    def tick(point):
        for s in range(2):
            @pl.when(step == s)
            def _():
                exchange.advance(s * ticks + point)

    @pl.when(step == 0)
    def _():
        exchange.greet()
        load = pltpu.make_async_copy(other_ref, other_sum, local)
        load.start()
        for half in range(2):
            for copy in kept(half):
                copy.start()
        load.wait()

    @pl.when(step == 0)
    def _():
        xs[...] = jnp.zeros_like(xs)
        dos[...] = jnp.zeros_like(dos)
        small[...] = jnp.zeros_like(small)
        dbias[...] = jnp.zeros_like(dbias)

    tick(0)
    for half in range(2):
        @pl.when(step == half)
        def _():
            for copy in kept(half):
                copy.wait()

    x = x_ref[...].reshape(ROWS, D).astype(f32)
    xh, _ = norm(x)
    n1[step] = (xh * gain[0, 0:1, :] + beta[0, 0:1, :]).astype(bf16)
    middle = mid[...]
    xh2, _ = norm(middle)
    n2[step] = (xh2 * gain[0, 1:2, :] + beta[0, 1:2, :]).astype(bf16)

    def slope(cut):
        u = z[step, :, cut].astype(f32)
        value, phi = gelu(u)
        z[step, :, cut] = value.astype(bf16)
        return gelu_slope(u, phi)

    dx = backward(
        step, 0, x, middle, dy_ref[...].astype(f32).reshape(ROWS, D),
        (gain, wqkv, wp, w1, w2, xs, qw, pr, dos, dss, dm, du, da, dp, small, dbias),
        slope,
        tick,
    )
    dx_ref[...] = dx.astype(bf16).reshape(dx_ref.shape)

    @pl.when(step == 1)
    def _():
        weight_grads(n1, n2, o16, z, dm, du, da, dp, grads)
        for k in range(2 * ticks, exchange.stages + 1):
            exchange.advance(k)
        store = pltpu.make_async_copy(other_sum, other_out, local)
        store.start()
        store.wait()


def whole(shape):
    return pl.BlockSpec(shape, lambda s: (0,) * len(shape), pipeline_mode=pl.Buffered(1))


def of_block(block, *shape):
    return pl.BlockSpec((None,) + shape, lambda s: (block,) + (0,) * len(shape), pipeline_mode=pl.Buffered(1))


def by_half(*shape, buffers=2):
    return pl.BlockSpec(shape, lambda s: (s,) + (0,) * (len(shape) - 1), pipeline_mode=pl.Buffered(buffers))


ANY_SPEC = pl.BlockSpec(memory_space=pl.ANY)
SMEM_SPEC = pl.BlockSpec(memory_space=pltpu.SMEM)
TOKEN_SPEC = pl.BlockSpec((CELLS, HALF, D), lambda s: (0, s, 0))
XS = VMEM((2, 3 * GROUPS, 8 * SLOT, LANES), f32)
DOS = VMEM((2, GROUPS, 8 * SLOT, LANES), f32)
QW = (HALF, 3 * GROUPS, SLOT, LANES)
PR = (HALF, GROUPS, KEYS, 4 * SLOT)
OPERANDS = [VMEM((2, ROWS, width), bf16) for width in (D, D, D, FF, D, FF, D, 3 * D)]


def params():
    return pltpu.CompilerParams(vmem_limit_bytes=61 * 2**20, dimension_semantics=("arbitrary",))


def run_first(ext, x, gain, beta, wqkv, qvb, bias, wp, ob, w1, b1, w2):
    crops = x.shape[1]
    return pl.pallas_call(
        first_kernel,
        grid=(2,),
        out_shape=(
            jax.ShapeDtypeStruct(x.shape, bf16),
            jax.ShapeDtypeStruct((crops,) + QW[1:], bf16),
            jax.ShapeDtypeStruct((crops,) + PR[1:], bf16),
            jax.ShapeDtypeStruct((2 * ROWS, D), bf16),
            jax.ShapeDtypeStruct((2 * ROWS, D), f32),
            jax.ShapeDtypeStruct((2 * ROWS, FF), bf16),
        ),
        in_specs=[
            SMEM_SPEC, TOKEN_SPEC, whole(gain.shape), whole(beta.shape), of_block(0, D, 3 * D), whole(qvb.shape),
            of_block(0, GROUPS, KEYS, 4 * SLOT), of_block(0, D, D), whole(ob.shape), of_block(0, D, FF),
            whole(b1.shape), of_block(0, FF, D),
        ],
        out_specs=(TOKEN_SPEC, by_half(*QW), by_half(*PR), by_half(ROWS, D), by_half(ROWS, D), by_half(ROWS, FF)),
        scratch_shapes=[XS, VMEM(PR, f32), VMEM((2, GROUPS, 8 * KEYS, LANES), f32)],
        compiler_params=params(),
        name="first_forward",
    )(ext, x, gain, beta, wqkv, qvb, bias, wp, ob, w1, b1, w2)


GRAD_SHAPES = (
    jax.ShapeDtypeStruct((SLABS * D, D), bf16),
    jax.ShapeDtypeStruct((16, D), f32),
    jax.ShapeDtypeStruct((GROUPS, KEYS, 4 * SLOT), f32),
)
GRAD_SPECS = (whole((SLABS * D, D)), whole((16, D)), whole((GROUPS, KEYS, 4 * SLOT)))


def run_second(ext, count, x, cot, gain, beta, wqkv, qvb, bias, wp, ob, w1, b1, w2):
    return pl.pallas_call(
        second_kernel,
        grid=(2,),
        out_shape=(jax.ShapeDtypeStruct(x.shape, bf16), jax.ShapeDtypeStruct(x.shape, bf16)) + GRAD_SHAPES,
        in_specs=[
            SMEM_SPEC, SMEM_SPEC, TOKEN_SPEC, TOKEN_SPEC, whole(gain.shape), whole(beta.shape), of_block(1, D, 3 * D),
            whole(qvb.shape), of_block(1, GROUPS, KEYS, 4 * SLOT), of_block(1, D, D), whole(ob.shape),
            of_block(1, D, FF), whole(b1.shape), of_block(1, FF, D),
        ],
        out_specs=(TOKEN_SPEC, TOKEN_SPEC) + GRAD_SPECS,
        scratch_shapes=[
            XS, VMEM(QW, bf16), VMEM(PR, f32), VMEM(PR, bf16), VMEM((2, GROUPS, 8 * KEYS, LANES), f32),
            VMEM((ROWS, D), f32), VMEM((ROWS, FF), bf16), DOS, VMEM(PR, bf16),
        ] + OPERANDS,
        compiler_params=params(),
        name="second_block",
    )(ext, count, x, cot, gain, beta, wqkv, qvb, bias, wp, ob, w1, b1, w2)


def run_third(x, dy, qw, pr, o16, mid, u, gain, beta, wqkv, wp, w1, w2, other):
    return pl.pallas_call(
        third_kernel,
        grid=(2,),
        out_shape=(jax.ShapeDtypeStruct(x.shape, bf16),) + GRAD_SHAPES + GRAD_SHAPES[:1],
        in_specs=[
            TOKEN_SPEC, TOKEN_SPEC, by_half(*QW), by_half(*PR, buffers=1), ANY_SPEC, by_half(ROWS, D), ANY_SPEC,
            whole(gain.shape), whole(beta.shape), of_block(0, D, 3 * D), of_block(0, D, D), of_block(0, D, FF),
            of_block(0, FF, D), ANY_SPEC,
        ],
        out_specs=(TOKEN_SPEC,) + GRAD_SPECS + (ANY_SPEC,),
        scratch_shapes=[XS, DOS, VMEM(PR, bf16)] + OPERANDS + [VMEM((SLABS * D, D), bf16)] + exchange_scratch() + [
            pltpu.SemaphoreType.DMA(()), pltpu.SemaphoreType.DMA((2, 2)),
        ],
        compiler_params=pltpu.CompilerParams(
            vmem_limit_bytes=63 * 2**20, dimension_semantics=("arbitrary",), collective_id=0, has_side_effects=True
        ),
        name="first_backward",
    )(x, dy, qw, pr, o16, mid, u, gain, beta, wqkv, wp, w1, w2, other)


def partner(value, apart):
    pairs = [(source, source ^ 2**apart) for source in range(lax.axis_size("win"))]
    return lax.ppermute(value, "win", pairs)


def shift_in(cells_here):
    grid = cells_here.reshape((WINDOW, WINDOW) + cells_here.shape[1:])
    widened = jnp.concatenate([grid[:, SHIFT:], partner(grid[:, :SHIFT], 0)], 1)
    return jnp.concatenate([widened[SHIFT:], partner(widened[:SHIFT], 1)], 0).reshape(cells_here.shape)


def shift_out(cells_here):
    keep = WINDOW - SHIFT
    grid = cells_here.reshape((WINDOW, WINDOW) + cells_here.shape[1:])
    widened = jnp.concatenate([partner(grid[:, keep:], 0), grid[:, :keep]], 1)
    return jnp.concatenate([partner(widened[keep:], 1), widened[:keep]], 0).reshape(cells_here.shape)


def orders():
    n_img, n_win = lax.axis_size("img"), lax.axis_size("win")
    core = [("win", 0)]
    across = [("win", b) for b in range(1, n_win.bit_length() - 1)]
    img = [("img", b) for b in range(n_img.bit_length() - 1)]
    return [core + across + img, core + img[:1] + across + img[1:], core + img[1:] + across + img[:1]]


class Exchange:
    def __init__(self, buf, landing, send, recv, free):
        self.buf, self.landing, self.send, self.recv, self.free = buf, landing, send, recv, free
        chains = orders()
        self.bits = len(chains[0])
        self.stages = 2 * self.bits
        self.index = {axis: lax.axis_index(axis) for axis in ("img", "win")}
        rows = buf.shape[0] // len(chains)
        self.plans, land = [], 0
        for c, chain in enumerate(chains):
            start, size, plan = c * rows, rows, []
            for axis, bit in chain:
                mine = (self.index[axis] // 2**bit) % 2
                halve = size % 32 == 0
                if halve:
                    size = size // 2
                keep, give = (start + mine * size, start + (1 - mine) * size) if halve else (start, start)
                to = {axis: self.index[axis] + 2**bit - 2 ** (bit + 1) * mine}
                plan.append((keep, give, size, land, halve, to))
                start, land = keep, land + size
            self.plans.append(plan)

    def greet(self):
        barrier = pltpu.get_barrier_semaphore()
        for plan in self.plans[:1]:
            for *_, to in plan:
                pl.semaphore_signal(barrier, inc=1, device_id=to, device_id_type=MESH)
            pl.semaphore_wait(barrier, len(plan))

    def copy(self, c, k):
        n = min(k, self.stages - 1 - k)
        keep, give, size, land, halve, to = self.plans[c][n]
        if k >= self.bits and not halve:
            return None
        if k < self.bits:
            source, target = self.buf.at[pl.ds(pl.multiple_of(give, 16), size)], self.landing.at[pl.ds(land, size)]
        else:
            source = target = self.buf.at[pl.ds(pl.multiple_of(keep, 16), size)]
        return pltpu.make_async_remote_copy(
            source, target, self.send.at[c, k], self.recv.at[c, k], device_id=to, device_id_type=MESH
        )

    def start(self, k):
        for c in range(len(self.plans)):
            copy = self.copy(c, k)
            if copy is not None:
                if k >= self.bits:
                    pl.semaphore_wait(self.free.at[c, self.stages - 1 - k], 1)
                copy.start()

    def finish(self, k):
        for c in range(len(self.plans)):
            copy = self.copy(c, k)
            if copy is None:
                continue
            copy.wait()
            if k >= self.bits:
                continue
            keep, _, size, land, halve, to = self.plans[c][k]
            if halve:
                pl.semaphore_signal(self.free.at[c, k], inc=1, device_id=to, device_id_type=MESH)
            tile = 96 if size % 96 == 0 else 16

            def add(i, carry, keep=keep, land=land, tile=tile):
                here = pl.ds(pl.multiple_of(keep + i * tile, 16), tile)
                there = pl.ds(pl.multiple_of(land + i * tile, 16), tile)
                self.buf[here, :] = (self.buf[here, :].astype(f32) + self.landing[there, :].astype(f32)).astype(bf16)
                return carry

            lax.fori_loop(0, size // tile, add, 0)

    def advance(self, k):
        if 1 <= k <= self.stages:
            self.finish(k - 1)
        if k < self.stages:
            self.start(k)


def exchange_scratch():
    landing = 0
    for chain in orders():
        size = SLABS * D // 3
        for _ in chain:
            size = size // 2 if size % 32 == 0 else size
            landing += size
    stages = 2 * len(orders()[0])
    dma = pltpu.SemaphoreType.DMA((3, stages))
    return [VMEM((landing, D), bf16), dma, dma, pltpu.SemaphoreType.REGULAR((3, stages // 2))]


def sum_kernel(g_ref, s_ref, out, s_out, landing, send, recv, free, s_land, s_send, s_recv):
    exchange = Exchange(out, landing, send, recv, free)
    exchange.greet()
    out[...] = g_ref[...]
    s_out[...] = s_ref[...]
    exchange.start(0)
    for n, (*_, to) in enumerate(exchange.plans[0]):
        small = pltpu.make_async_remote_copy(
            s_out, s_land.at[n], s_send.at[n], s_recv.at[n], device_id=to, device_id_type=MESH
        )
        small.start()
        exchange.advance(n + 1)
        small.wait()
        s_out[...] += s_land[n]
    for k in range(exchange.bits + 1, exchange.stages + 1):
        exchange.advance(k)


def sum_all(grads, small):
    bits = len(orders()[0])
    return pl.pallas_call(
        sum_kernel,
        out_shape=(jax.ShapeDtypeStruct(grads.shape, bf16), jax.ShapeDtypeStruct(small.shape, f32)),
        in_specs=[pl.BlockSpec(memory_space=VMEM)] * 2,
        out_specs=(pl.BlockSpec(memory_space=VMEM),) * 2,
        scratch_shapes=exchange_scratch() + [
            VMEM((bits,) + small.shape, f32), pltpu.SemaphoreType.DMA((bits,)), pltpu.SemaphoreType.DMA((bits,)),
        ],
        compiler_params=pltpu.CompilerParams(
            collective_id=1, has_side_effects=True, vmem_limit_bytes=30 * 2**20
        ),
        name="sum_gradients",
    )(grads, small)


def finish_kernel(*refs):
    ins, outs = refs[:8], refs[8:]
    for n, out in enumerate(outs):
        for block in range(2):
            out[block] = ins[2 * n + block][...].astype(f32)


def finish(grads_one, grads_two):
    slabs = [lambda j: (j, 0), lambda j: (4 + j, 0), lambda j: (8 + jnp.minimum(j, 2), 0), lambda j: (11, 0)]
    targets = [lambda j: (0, 0, j), lambda j: (0, j, 0), lambda j: (0, 0, jnp.minimum(j, 2)), lambda j: (0, 0, 0)]
    return pl.pallas_call(
        finish_kernel,
        grid=(4,),
        out_shape=tuple(jax.ShapeDtypeStruct((2,) + s, f32) for s in ((D, FF), (FF, D), (D, 3 * D), (D, D))),
        in_specs=[pl.BlockSpec((D, D), index) for index in slabs for _ in range(2)],
        out_specs=tuple(pl.BlockSpec((2, D, D), index) for index in targets),
        compiler_params=params(),
        name="finish_gradients",
    )(*[grads_one, grads_two] * 4)


def position_lookup():
    j = jnp.arange(KEYS)[:, None]
    i = jnp.arange(SLOT)[None, :]
    side = SIDE - 1
    index = (i // WINDOW - j // WINDOW + WINDOW - 1) * side + i % WINDOW - j % WINDOW + WINDOW - 1
    index = jnp.where((i < CELLS) & (j < CELLS), index, -1).reshape(-1)
    return (jnp.arange(side * side)[:, None] == index[None, :]).astype(f32)


def on_device(
    tokens, cotangent, crop_counts, crop_extent, norm_gain, norm_bias, qkv_weight, qv_bias, rel_table, proj_weight,
    out_bias, fc1_weight, fc1_bias, fc2_weight,
):
    crops = tokens.shape[0]
    x = tokens.reshape(crops, CELLS, D).transpose(1, 0, 2)
    cot = cotangent.reshape(crops, CELLS, D).transpose(1, 0, 2)
    lookup = position_lookup()
    highest = lax.Precision.HIGHEST
    bias = jnp.einsum("bkh,kp->bhp", rel_table, lookup, precision=highest) * LOG2E
    bias = bias.reshape(2, GROUPS, 4, KEYS, SLOT).transpose(0, 1, 3, 2, 4)
    bias = jnp.where(jnp.arange(KEYS)[:, None, None] < CELLS, bias, NEG).reshape(2, GROUPS, KEYS, 4 * SLOT)

    cot_shifted = shift_in(cot)
    x1, qw, pr, o16, mid, u = run_first(
        crop_extent, x, norm_gain, norm_bias, qkv_weight, qv_bias, bias, proj_weight, out_bias, fc1_weight, fc1_bias,
        fc2_weight,
    )
    x1 = shift_in(x1)
    y2, dr, grads_two, small_two, dbias_two = run_second(
        crop_extent, crop_counts, x1, cot_shifted, norm_gain, norm_bias, qkv_weight, qv_bias, bias, proj_weight,
        out_bias, fc1_weight, fc1_bias, fc2_weight,
    )
    output = shift_out(y2)
    dx1 = shift_out(dr)
    dx, grads_one, small_one, dbias_one, sum_two = run_third(
        x, dx1, qw, pr, o16, mid, u, norm_gain, norm_bias, qkv_weight, proj_weight, fc1_weight, fc2_weight, grads_two
    )
    dbias = jnp.stack([dbias_one, dbias_two]).reshape(2, GROUPS, KEYS, 4, SLOT).transpose(0, 1, 3, 2, 4)
    table = jnp.einsum("hp,kp->hk", dbias.reshape(2 * HEADS, KEYS * SLOT), lookup, precision=highest)
    table = jnp.pad(table, ((0, 0), (0, D - table.shape[1])))
    small = jnp.concatenate([small_one, small_two, table], 0)
    sum_one, small = sum_all(grads_one, small)

    fc1, fc2, qkv, proj = finish(sum_one, sum_two)
    rows = small[:32].reshape(2, 16, D)
    table = small[32:, : rel_table.shape[1]].reshape(2, HEADS, -1).transpose(0, 2, 1)
    back = lambda v: v.transpose(1, 0, 2).reshape(tokens.shape)
    return (
        back(output), back(dx), rows[:, 0:2], rows[:, 2:4], qkv, rows[:, 4:6], table, proj, rows[:, 6:8], fc1,
        rows[:, 8:12].reshape(2, FF), fc2,
    )


def solution(mesh):
    split = P("img", "win", None, None)
    return jax.shard_map(
        on_device,
        mesh=mesh,
        in_specs=(split, split, P("img"), P("img", None)) + (P(),) * 10,
        out_specs=(split, split) + (P(),) * 10,
        check_vma=False,
    )
```

```python
import jax
import jax.numpy as jnp
from jax import lax
from jax.experimental import pallas as pl
from jax.experimental.pallas import tpu as pltpu
from jax.sharding import PartitionSpec as P

D = 384
FF = 1536
HEADS = 12
HEAD_DIM = 32
WINDOW = 7
SHIFT = 3
CELLS = WINDOW * WINDOW
SIDE = 2 * WINDOW
HALF = 16
ROWS = CELLS * HALF
LANES = 128
GROUPS = 3
KEYS = 56
SLOT = 64
SLABS = 12
SMALL = 16
TABLE = GROUPS * KEYS
SUMS = SLABS * D + 256
GROUPED = ((0, 1), (2, 3), (4, 5, 6))
NEG = -1e30
LOG2E = 1.4426950408889634
SCALE = HEAD_DIM**-0.5
MESH = pl.DeviceIdType.MESH

bf16 = jnp.bfloat16
f32 = jnp.float32
VMEM = pltpu.VMEM


def mm(a, b):
    return lax.dot_general(a, b, (((1,), (0,)), ((), ())), preferred_element_type=f32)


def mm_bt(a, b):
    return lax.dot_general(a, b, (((1,), (1,)), ((), ())), preferred_element_type=f32)


def mm_at(a, b):
    return lax.dot_general(a, b, (((0,), (0,)), ((), ())), preferred_element_type=f32)


def norm(x):
    centred = x - jnp.mean(x, -1, keepdims=True)
    rstd = lax.rsqrt(jnp.mean(centred * centred, -1, keepdims=True) + 1e-5)
    return centred * rstd, rstd


def norm_back(xh, rstd, dn, gain):
    e = dn * gain
    mean_e = jnp.mean(e, -1, keepdims=True)
    mean_ex = jnp.mean(e * xh, -1, keepdims=True)
    dx = rstd * (e - mean_e - xh * mean_ex)
    return dx, jnp.sum(dn * xh, 0, keepdims=True), jnp.sum(dn, 0, keepdims=True)


def gelu(u):
    phi = 0.5 + 0.5 * lax.erf(u * 0.7071067811865476)
    return u * phi, phi


def gelu_slope(u, phi):
    return phi + u * jnp.exp2(u * u * (-0.5 * LOG2E)) * 0.3989422804014327


def spread(rows):
    head = lax.broadcasted_iota(jnp.int32, rows.shape, 1) // HEAD_DIM
    zero = jnp.zeros_like(rows)
    return jnp.concatenate([jnp.where(head == h, rows, zero) for h in range(4)], 0)


def gather_heads(rows):
    head = lax.broadcasted_iota(jnp.int32, (KEYS, LANES), 1) // HEAD_DIM
    out = rows[:KEYS]
    for h in range(1, 4):
        out = jnp.where(head == h, rows[SLOT * h : SLOT * h + KEYS], out)
    return out


def to_windows(ref, slot, part):
    parted = part.reshape(CELLS, 2, 8, LANES)
    for cg in range(2):
        ref[cg, slot, 0 : CELLS * 8, :] = parted[:, cg].reshape(CELLS * 8, LANES)


def from_windows(ref, slot):
    parts = [ref[cg, slot, 0 : CELLS * 8, :].reshape(CELLS, 1, 8, LANES) for cg in range(2)]
    return jnp.concatenate(parts, 1).reshape(ROWS, LANES)


def cells(shifted):
    win = lax.axis_index("win")
    j = lax.broadcasted_iota(jnp.int32, (KEYS, LANES), 0)
    i = lax.broadcasted_iota(jnp.int32, (KEYS, LANES), 1) % SLOT
    top, left = WINDOW * (win // 2), WINDOW * (win % 2)
    places = [top + j // WINDOW, left + j % WINDOW, top + i // WINDOW, left + i % WINDOW]
    if not shifted:
        return places, None
    region = [(v >= SIDE - WINDOW).astype(jnp.int32) + (v >= SIDE - SHIFT).astype(jnp.int32) for v in places]
    apart = (region[0] != region[2]) | (region[1] != region[3])
    moved = [jnp.where(v + SHIFT >= SIDE, v + SHIFT - SIDE, v + SHIFT) for v in places]
    return moved, jnp.where(apart, NEG, 0.0)


def forward(step, block, shifted, x, refs, keep_n1=None, keep_n2=None, keep_gelu=None, keep_u=None):
    (ext, gain, beta, wqkv, qvb, bias, wp, ob, w1, b1, w2, xs, qw, ss, pr, os, o16, mid) = refs
    xh, _ = norm(x)
    n1 = (xh * gain[block, 0:1, :] + beta[block, 0:1, :]).astype(bf16)
    if keep_n1 is not None:
        keep_n1[step] = n1
    proj = mm(n1, wqkv[...])
    q = (proj[:, :D] + qvb[block, 0:1, :]) * (SCALE * LOG2E)
    k = proj[:, D : 2 * D]
    v = proj[:, 2 * D :] + qvb[block, 1:2, :]
    for g in range(GROUPS):
        cut = slice(LANES * g, LANES * (g + 1))
        to_windows(xs, g, q[:, cut])
        to_windows(xs, GROUPS + g, k[:, cut])
        to_windows(xs, 2 * GROUPS + g, v[:, cut])
    places, apart = cells(shifted)
    if apart is not None:
        apart = jnp.concatenate([apart, apart], 1)

    def scores(w, carry):
        cg, c = w // 8, w % 8
        rows, cols = ext[step * HALF + w, 0], ext[step * HALF + w, 1]
        valid_j = (places[0] < rows) & (places[1] < cols)
        valid_i = (places[2] < rows) & (places[3] < cols)
        mask = jnp.where(valid_i == valid_j, 0.0, NEG)
        mask = jnp.concatenate([mask, mask], 1)
        if apart is not None:
            mask = mask + apart
        for g in range(GROUPS):
            qs, ks, vs = (
                xs[cg, GROUPS * n + g, pl.ds(c, SLOT, stride=8), :].astype(bf16) for n in range(3)
            )
            qw[w, g] = qs
            qw[w, GROUPS + g] = ks
            qw[w, 2 * GROUPS + g] = vs
            ss[w, g] = mm_bt(ks[:KEYS], spread(qs)) + bias[g] + mask
        return carry

    lax.fori_loop(0, HALF, scores, 0, unroll=2)

    def softmax(w, carry):
        for g in range(GROUPS):
            s = ss[w, g]
            e = jnp.exp2(s - jnp.max(s, 0, keepdims=True))
            pr[w, g] = (e * (1.0 / jnp.sum(e, 0, keepdims=True))).astype(bf16)
        return carry

    lax.fori_loop(0, HALF, softmax, 0)

    def mix(w, carry):
        cg, c = w // 8, w % 8
        for g in range(GROUPS):
            os[cg, g, pl.ds(c, KEYS, stride=8), :] = gather_heads(
                mm_at(pr[w, g], qw[w, 2 * GROUPS + g][:KEYS])
            )
        return carry

    lax.fori_loop(0, HALF, mix, 0)
    for g in range(GROUPS):
        o16[:, LANES * g : LANES * (g + 1)] = from_windows(os, g).astype(bf16)
    middle = x + (mm(o16[...], wp[...]) + ob[block, 0:1, :])
    mid[...] = middle
    xh2, _ = norm(middle)
    n2 = (xh2 * gain[block, 1:2, :] + beta[block, 1:2, :]).astype(bf16)
    if keep_n2 is not None:
        keep_n2[step] = n2
    y = middle + ob[block, 1:2, :]
    for part in range(3):
        cut = slice(512 * part, 512 * (part + 1))
        u = mm(n2, w1[:, cut]) + b1[block : block + 1, cut]
        if keep_u is not None:
            keep_u[:, cut] = u.astype(bf16)
        z, phi = gelu(u)
        z = z.astype(bf16)
        if keep_gelu is not None:
            keep_gelu[0][step, :, cut] = z
            keep_gelu[1][:, cut] = gelu_slope(u, phi).astype(bf16)
        y = y + mm(z, w2[cut, :])
    return y


def no_tick(point):
    pass


def mlp_back(step, block, mid, dy, refs, slope, keep_n2=None, beta=None, tick=no_tick):
    (gain, wp, w1, w2, dos, dm_all, du_all, da_all, small) = refs

    def add_small(row, value):
        small[row : row + 1, :] += value

    dm = dy.astype(bf16)
    dm_all[step] = dm
    add_small(7, jnp.sum(dm.astype(f32), 0, keepdims=True))
    dn2 = jnp.zeros((ROWS, D), f32)
    for part in range(4):
        cut = slice(384 * part, 384 * (part + 1))
        du = (mm_bt(dm, w2[cut, :]) * slope(cut)).astype(bf16)
        du_all[step, :, cut] = du
        add_small(8 + part, jnp.sum(du.astype(f32), 0, keepdims=True))
        dn2 = dn2 + mm_bt(du, w1[:, cut])
        tick(part)
    xh, rstd = norm(mid)
    if keep_n2 is not None:
        keep_n2[step] = (xh * gain[block, 1:2, :] + beta[block, 1:2, :]).astype(bf16)
    dx, dgain, dbeta = norm_back(xh, rstd, dn2, gain[block, 1:2, :])
    add_small(1, dgain)
    add_small(3, dbeta)
    dmid = dy + dx
    da = dmid.astype(bf16)
    da_all[step] = da
    add_small(6, jnp.sum(da.astype(f32), 0, keepdims=True))
    do = mm_bt(da, wp[...])
    for g in range(GROUPS):
        to_windows(dos, g, do[:, LANES * g : LANES * (g + 1)])
    tick(4)
    return dmid


def attention_back(step, block, x, dmid, refs, keep_n1=None, beta=None, tick=no_tick):
    (gain, wqkv, xs, qw, pr, dos, dss, dp_all, small, dbias) = refs

    def add_small(row, value):
        small[row : row + 1, :] += value

    def probs_back(w, carry):
        cg, c = w // 8, w % 8
        for g in range(GROUPS):
            d = spread(dos[cg, g, pl.ds(c, SLOT, stride=8), :].astype(bf16))
            p16 = pr[w, g]
            p = p16.astype(f32)
            t = p * mm_bt(qw[w, 2 * GROUPS + g][:KEYS], d)
            ds = (t - p * jnp.sum(t, 0, keepdims=True)).astype(bf16)
            dss[w, g] = ds
            dbias[g] += ds.astype(f32)
            xs[cg, 2 * GROUPS + g, pl.ds(c, KEYS, stride=8), :] = mm(p16, d)
        return carry

    def scores_back(w, carry):
        cg, c = w // 8, w % 8
        for g in range(GROUPS):
            ds = dss[w, g]
            dk = mm(ds, spread(qw[w, g])) * (1.0 / LOG2E)
            dq = gather_heads(mm_at(ds, qw[w, GROUPS + g][:KEYS])) * SCALE
            xs[cg, g, pl.ds(c, KEYS, stride=8), :] = dq
            xs[cg, GROUPS + g, pl.ds(c, KEYS, stride=8), :] = dk
        return carry

    for part in range(2):
        lax.fori_loop(8 * part, 8 * (part + 1), probs_back, 0, unroll=2)
        tick(part)
    for part in range(2):
        lax.fori_loop(8 * part, 8 * (part + 1), scores_back, 0)
        tick(2 + part)
    for n in range(3 * GROUPS):
        dp_all[step, :, LANES * n : LANES * (n + 1)] = from_windows(xs, n).astype(bf16)
    dp = dp_all[step, :, : 3 * D]
    add_small(4, jnp.sum(dp[:, :D].astype(f32), 0, keepdims=True))
    add_small(5, jnp.sum(dp[:, 2 * D :].astype(f32), 0, keepdims=True))
    dn1 = mm_bt(dp, wqkv[...])
    tick(4)
    xh, rstd = norm(x)
    if keep_n1 is not None:
        keep_n1[step] = (xh * gain[block, 0:1, :] + beta[block, 0:1, :]).astype(bf16)
    dx, dgain, dbeta = norm_back(xh, rstd, dn1, gain[block, 0:1, :])
    add_small(0, dgain)
    add_small(2, dbeta)
    tick(5)
    return dmid() + dx


def flat(ref, cut=slice(None)):
    return ref[:, :, cut].reshape(2 * ROWS, -1)


def put_slabs(out, first, value):
    for j in range(value.shape[1] // D):
        out[D * (first + j) : D * (first + j + 1), :] = value[:, D * j : D * (j + 1)].astype(bf16)


def fc_grads(n2, z, dm, du, out, tick=no_tick):
    for first, left, right in ((0, n2, du), (4, dm, z)):
        for j in range(2):
            put_slabs(out, first + 2 * j, mm_at(flat(left), flat(right, slice(768 * j, 768 * (j + 1)))))
        tick(first // 4)


def attention_grads(n1, o16, da, dp, out):
    put_slabs(out, 8, mm_at(flat(n1), flat(dp, slice(3 * D))))
    put_slabs(out, 11, mm_at(flat(o16), flat(da)))


def small_grads(small, dbias, out):
    base = SLABS * D
    out[base : base + SMALL, :] = small[...].astype(bf16)
    out[base + SMALL : SUMS, :] = jnp.zeros((SUMS - base - SMALL, D), bf16)
    out[base + SMALL : base + SMALL + TABLE, : 4 * SLOT] = dbias[...].reshape(TABLE, 4 * SLOT).astype(bf16)


KEEP = WINDOW - SHIFT
NEAR, FAR = slice(0, KEEP), slice(KEEP, WINDOW)
HERE, THERE = slice(SHIFT, WINDOW), slice(0, SHIFT)


def shift_peers():
    win = lax.axis_index("win")
    beside = 1 - 2 * (win % 2)
    below = 2 - 4 * (win // 2 % 2)
    return [{"win": win + beside}, {"win": win + below}, {"win": win + beside + below}]


def shift_copies(source, target, send, recv, back=False):
    plain = [(HERE, HERE), (HERE, THERE), (THERE, HERE), (THERE, THERE)]
    moved = [(NEAR, NEAR), (NEAR, FAR), (FAR, NEAR), (FAR, FAR)]
    if back:
        plain, moved = moved, plain
    out = [pltpu.make_async_copy(source.at[plain[0]], target.at[moved[0]], send.at[3])]
    for n, to in enumerate(shift_peers()):
        out.append(
            pltpu.make_async_remote_copy(
                source.at[plain[n + 1]], target.at[moved[n + 1]], send.at[n], recv.at[n], device_id=to, device_id_type=MESH
            )
        )
    return out


def start_all(copies):
    for copy in copies:
        copy.start()


def wait_all(copies):
    for copy in copies:
        copy.wait()


def greet(peers):
    barrier = pltpu.get_barrier_semaphore()
    for to in peers:
        pl.semaphore_signal(barrier, inc=1, device_id=to, device_id_type=MESH)
    pl.semaphore_wait(barrier, len(peers))


def first_kernel(
    ext, x_ref, cot, gain, beta, wqkv, qvb, bias, wp, ob, w1, b1, w2,
    y_shifted, y_last, cot_shifted, qw, pr, o16, mid, u_ref, xs, ss, os, y_first, send, recv,
):
    step = pl.program_id(0)
    cot_copies = shift_copies(cot, cot_shifted, send.at[0], recv.at[0])
    y_copies = shift_copies(y_first, y_shifted, send.at[1], recv.at[1])

    @pl.when(step == 0)
    def _():
        greet(shift_peers())
        start_all(cot_copies)
        xs[...] = jnp.zeros_like(xs)

    x = x_ref[...].reshape(ROWS, D).astype(f32)
    y = forward(
        step, 0, False, x, (ext, gain, beta, wqkv, qvb, bias, wp, ob, w1, b1, w2, xs, qw, ss, pr, os, o16, mid), keep_u=u_ref
    )
    y = y.astype(bf16).reshape(WINDOW, WINDOW, HALF, D)

    @pl.when(step == 0)
    def _():
        y_first[...] = y
        start_all(y_copies)

    @pl.when(step == 1)
    def _():
        y_last[...] = y
        wait_all(y_copies)
        wait_all(cot_copies)


def second_kernel(
    ext, count, x_first, x_last, cot_ref, gain, beta, wqkv, qvb, bias, wp, ob, w1, b1, w2,
    y_ref, dx_shifted, dx_last, grads,
    xs, qw, ss, pr, os, mid, slope, dos, dss, small, dbias, n1, n2, o16, z, dm, du, da, dp, x_both, dx_first, send, recv, local,
):
    step = pl.program_id(0)
    x_copies = shift_copies(x_last, x_both.at[1], send.at[0], recv.at[0])
    dx_copies = shift_copies(dx_first, dx_shifted, send.at[1], recv.at[1], back=True)

    @pl.when(step == 0)
    def _():
        load = pltpu.make_async_copy(x_first, x_both.at[0], local)
        load.start()
        greet(shift_peers())
        start_all(x_copies)
        load.wait()
        xs[...] = jnp.zeros_like(xs)
        dos[...] = jnp.zeros_like(dos)
        small[...] = jnp.zeros_like(small)
        dbias[...] = jnp.zeros_like(dbias)

    @pl.when(step == 1)
    def _():
        wait_all(x_copies)

    x = x_both[step].reshape(ROWS, D).astype(f32)
    live = lax.broadcasted_iota(jnp.int32, (CELLS, HALF, 1), 1) + step * HALF < count[0]
    y = forward(
        step, 1, True, x,
        (ext, gain, beta, wqkv, qvb, bias, wp, ob, w1, b1, w2, xs, qw, ss, pr, os, o16.at[step], mid),
        n1, n2, (z, slope),
    )
    y_ref[...] = jnp.where(live, y.reshape(CELLS, HALF, D), 0.0).astype(bf16)
    dy = jnp.where(live, cot_ref[...].astype(f32), 0.0).reshape(ROWS, D)
    mid[...] = mlp_back(
        step, 1, mid[...], dy, (gain, wp, w1, w2, dos, dm, du, da, small), lambda cut: slope[:, cut].astype(f32)
    )
    dx = attention_back(
        step, 1, x, lambda: mid[...], (gain, wqkv, xs, qw, pr, dos, dss, dp, small, dbias)
    )
    dx = dx.astype(bf16).reshape(WINDOW, WINDOW, HALF, D)

    @pl.when(step == 0)
    def _():
        dx_first[...] = dx
        start_all(dx_copies)

    @pl.when(step == 1)
    def _():
        dx_last[...] = dx
        fc_grads(n2, z, dm, du, grads)
        attention_grads(n1, o16, da, dp, grads)
        small_grads(small, dbias, grads)
        wait_all(dx_copies)


def third_kernel(
    x_ref, dy_first, dy_last, y_ref, qw, pr, o_ref, mid, u_ref, gain, beta, wqkv, wp, w1, w2, two_ref,
    dx_ref, one_out, two_out, y_out,
    xs, dos, dss, small, dbias, dmid, n2, o16, z, dm, du, da,
    one, two, land_one, send_one, recv_one, free_one, land_two, send_two, recv_two, free_two, local, loads, dy_both, send, recv,
):
    step = pl.program_id(0)
    first = Exchange(one, land_one, send_one, recv_one, free_one)
    second = Exchange(two, land_two, send_two, recv_two, free_two)
    dy_copies = shift_copies(dy_last, dy_both.at[1], send.at[0], recv.at[0], back=True)
    y_copies = shift_copies(y_ref, y_out, send.at[1], recv.at[1], back=True)
    last = 24
    moves = [[] for _ in range(last + 1)]
    late = []
    for exchange, group, begin, every in ((second, 0, 0, 3), (second, 1, 1, 3), (second, 2, 2, 3), (first, 0, 12, 2), (first, 1, 13, 2)):
        for k in range(exchange.stages + 1):
            n = begin + every * k
            (moves[n] if n <= last else late).append((exchange, group, k))

    def tick(n):
        for exchange, group, k in moves[n]:
            exchange.advance(GROUPED[group], k)

    def tick_at(steps, base, per_step):
        def ticker(point):
            for s in steps:
                pl.when(step == s)(lambda s=s: tick(base + (s - steps[0]) * per_step + point))

        return ticker

    def kept(half):
        rows = pl.ds(half * ROWS, ROWS)
        return (
            pltpu.make_async_copy(u_ref.at[rows], z.at[half], loads.at[0, half]),
            pltpu.make_async_copy(o_ref.at[rows], o16.at[half], loads.at[1, half]),
        )

    @pl.when(step == 0)
    def _():
        load = pltpu.make_async_copy(two_ref, two, local.at[0])
        load.start()
        load_dy = pltpu.make_async_copy(dy_first, dy_both.at[0], local.at[1])
        load_dy.start()
        for half in range(2):
            start_all(kept(half))
        greet(second.peers() + shift_peers()[2:])
        start_all(dy_copies)
        xs[...] = jnp.zeros_like(xs)
        dos[...] = jnp.zeros_like(dos)
        small[...] = jnp.zeros_like(small)
        dbias[...] = jnp.zeros_like(dbias)
        load.wait()
        tick(0)
        start_all(y_copies)
        load_dy.wait()

    for half in range(2):

        @pl.when(step == half)
        def _():
            wait_all(kept(half))
            if half:
                wait_all(dy_copies)

    @pl.when(step < 2)
    def _():
        def slope(cut):
            u = z[step, :, cut].astype(f32)
            value, phi = gelu(u)
            z[step, :, cut] = value.astype(bf16)
            return gelu_slope(u, phi)

        dmid[step] = mlp_back(
            step, 0, mid[...], dy_both[step].astype(f32).reshape(ROWS, D),
            (gain, wp, w1, w2, dos.at[step], dm, du, da, small), slope, n2, beta, tick_at((0, 1), 1, 5),
        )

    @pl.when(step == 1)
    def _():
        fc_grads(n2, z, dm, du, one, lambda point: tick(11 + point))

    @pl.when(step >= 2)
    def _():
        half = step - 2
        dx = attention_back(
            half, 0, x_ref[...].reshape(ROWS, D).astype(f32), lambda: dmid[half],
            (gain, wqkv, xs, qw, pr, dos.at[half], dss, du, small, dbias), n2, beta, tick_at((2, 3), 13, 6),
        )
        dx_ref[...] = dx.astype(bf16).reshape(dx_ref.shape)

    @pl.when(step == 3)
    def _():
        for exchange, group, k in late:
            if exchange is second:
                exchange.advance(GROUPED[group], k)
        store_two = pltpu.make_async_copy(two, two_out, local.at[0])
        store_two.start()
        attention_grads(n2, o16, da, du, one)
        small_grads(small, dbias, one)
        first.advance(GROUPED[2], 0)
        for exchange, group, k in late:
            if exchange is first:
                exchange.advance(GROUPED[group], k)
        for k in range(1, first.stages + 1):
            first.advance(GROUPED[2], k)
        store_one = pltpu.make_async_copy(one, one_out, local.at[1])
        store_one.start()
        wait_all(y_copies)
        store_one.wait()
        store_two.wait()


def whole(shape):
    return pl.BlockSpec(shape, lambda s: (0,) * len(shape), pipeline_mode=pl.Buffered(1))


def of_block(block, *shape):
    return pl.BlockSpec((None,) + shape, lambda s: (block,) + (0,) * len(shape), pipeline_mode=pl.Buffered(1))


def by_half(*shape, buffers=2):
    return pl.BlockSpec(shape, lambda s: (s,) + (0,) * (len(shape) - 1), pipeline_mode=pl.Buffered(buffers))


ANY_SPEC = pl.BlockSpec(memory_space=pl.ANY)
SMEM_SPEC = pl.BlockSpec(memory_space=pltpu.SMEM)
TOKEN_SPEC = pl.BlockSpec((CELLS, HALF, D), lambda s: (0, s, 0))
XS = VMEM((2, 3 * GROUPS, 8 * SLOT, LANES), f32)
DOS = VMEM((2, GROUPS, 8 * SLOT, LANES), f32)
QW = (HALF, 3 * GROUPS, SLOT, LANES)
PR = (HALF, GROUPS, KEYS, 4 * SLOT)


def params(collective_id=None, mib=61):
    return pltpu.CompilerParams(
        vmem_limit_bytes=mib * 2**20, dimension_semantics=("arbitrary",), collective_id=collective_id,
        has_side_effects=collective_id is not None,
    )


CELL = (WINDOW, WINDOW)
PART = jax.ShapeDtypeStruct(CELL + (HALF, D), bf16)
SHIFTS = [pltpu.SemaphoreType.DMA((2, 4)), pltpu.SemaphoreType.DMA((2, 4))]


def run_first(ext, x, cot, gain, beta, wqkv, qvb, bias, wp, ob, w1, b1, w2):
    crops = x.shape[1]
    return pl.pallas_call(
        first_kernel,
        grid=(2,),
        out_shape=(
            PART,
            PART,
            jax.ShapeDtypeStruct(cot.shape, bf16),
            jax.ShapeDtypeStruct((crops,) + QW[1:], bf16),
            jax.ShapeDtypeStruct((crops,) + PR[1:], bf16),
            jax.ShapeDtypeStruct((2 * ROWS, D), bf16),
            jax.ShapeDtypeStruct((2 * ROWS, D), f32),
            jax.ShapeDtypeStruct((2 * ROWS, FF), bf16),
        ),
        in_specs=[
            SMEM_SPEC, TOKEN_SPEC, ANY_SPEC, whole(gain.shape), whole(beta.shape), of_block(0, D, 3 * D), whole(qvb.shape),
            of_block(0, GROUPS, KEYS, 4 * SLOT), of_block(0, D, D), whole(ob.shape), of_block(0, D, FF),
            whole(b1.shape), of_block(0, FF, D),
        ],
        out_specs=(
            ANY_SPEC, whole(PART.shape), ANY_SPEC, by_half(*QW), by_half(*PR), by_half(ROWS, D), by_half(ROWS, D),
            by_half(ROWS, FF),
        ),
        scratch_shapes=[
            XS, VMEM(PR, f32), VMEM((2, GROUPS, 8 * KEYS, LANES), f32), VMEM(PART.shape, bf16),
        ] + SHIFTS,
        compiler_params=params(1),
        name="first_forward",
    )(ext, x, cot, gain, beta, wqkv, qvb, bias, wp, ob, w1, b1, w2)


GRADS = jax.ShapeDtypeStruct((SUMS, D), bf16)
SMALLS = [VMEM((SMALL, D), f32), VMEM((GROUPS, KEYS, 4 * SLOT), f32)]


def run_second(ext, count, x_first, x_last, cot, gain, beta, wqkv, qvb, bias, wp, ob, w1, b1, w2):
    return pl.pallas_call(
        second_kernel,
        grid=(2,),
        out_shape=(jax.ShapeDtypeStruct(cot.shape, bf16), PART, PART, GRADS),
        in_specs=[
            SMEM_SPEC, SMEM_SPEC, ANY_SPEC, ANY_SPEC, TOKEN_SPEC, whole(gain.shape), whole(beta.shape), of_block(1, D, 3 * D),
            whole(qvb.shape), of_block(1, GROUPS, KEYS, 4 * SLOT), of_block(1, D, D), whole(ob.shape),
            of_block(1, D, FF), whole(b1.shape), of_block(1, FF, D),
        ],
        out_specs=(TOKEN_SPEC, ANY_SPEC, whole(PART.shape), whole(GRADS.shape)),
        scratch_shapes=[
            XS, VMEM(QW, bf16), VMEM(PR, f32), VMEM(PR, bf16), VMEM((2, GROUPS, 8 * KEYS, LANES), f32),
            VMEM((ROWS, D), f32), VMEM((ROWS, FF), bf16), DOS, VMEM(PR, bf16),
        ] + SMALLS + [VMEM((2, ROWS, width), bf16) for width in (D, D, D, FF, D, FF, D, 3 * D)]
        + [VMEM((2,) + PART.shape, bf16), VMEM(PART.shape, bf16)] + SHIFTS + [pltpu.SemaphoreType.DMA(())],
        compiler_params=params(2, 63),
        name="second_block",
    )(ext, count, x_first, x_last, cot, gain, beta, wqkv, qvb, bias, wp, ob, w1, b1, w2)


def in_steps(first, *shape, axis=0, buffers=2):
    def index(s):
        return tuple(jnp.clip(s - first, 0, 1) if n == axis else 0 for n in range(len(shape)))

    return pl.BlockSpec(shape, index, pipeline_mode=pl.Buffered(buffers))


def run_third(x, dy_first, dy_last, y, qw, pr, o16, mid, u, gain, beta, wqkv, wp, w1, w2, two):
    tokens = (CELLS, HALF, D)
    return pl.pallas_call(
        third_kernel,
        grid=(4,),
        out_shape=(jax.ShapeDtypeStruct(x.shape, bf16), GRADS, GRADS, jax.ShapeDtypeStruct(y.shape, bf16)),
        in_specs=[
            in_steps(2, *tokens, axis=1), ANY_SPEC, ANY_SPEC, ANY_SPEC, in_steps(2, *QW, buffers=1),
            in_steps(2, *PR, buffers=1), ANY_SPEC, in_steps(0, ROWS, D), ANY_SPEC,
            whole(gain.shape), whole(beta.shape), of_block(0, D, 3 * D), of_block(0, D, D), of_block(0, D, FF),
            of_block(0, FF, D), ANY_SPEC,
        ],
        out_specs=(in_steps(2, *tokens, axis=1), ANY_SPEC, ANY_SPEC, ANY_SPEC),
        scratch_shapes=[XS, VMEM((2,) + DOS.shape, f32), VMEM(PR, bf16)] + SMALLS + [VMEM((2, ROWS, D), f32)]
        + [VMEM((2, ROWS, width), bf16) for width in (D, D, FF, D, FF, D)]
        + [VMEM(GRADS.shape, bf16)] * 2 + exchange_scratch() * 2
        + [pltpu.SemaphoreType.DMA((2,)), pltpu.SemaphoreType.DMA((2, 2)), VMEM((2,) + PART.shape, bf16)] + SHIFTS,
        compiler_params=params(0, 63),
        name="first_backward",
    )(x, dy_first, dy_last, y, qw, pr, o16, mid, u, gain, beta, wqkv, wp, w1, w2, two)


def jobs():
    n_img, n_win = lax.axis_size("img"), lax.axis_size("win")
    bits = [("win", b) for b in range(1, n_win.bit_length() - 1)] + [("img", b) for b in range(n_img.bit_length() - 1)]
    pairs = [bits[n : n + 2] for n in range(0, len(bits), 2)]
    orders = [[[("win", 0)]] + pairs, [[("win", 0)]] + pairs[::-1]]
    out = []
    for group in range(3):
        out += [(1536 * group, 1024, orders[0]), (1536 * group + 1024, 512, orders[1])]
    return out + [(SLABS * D, SUMS - SLABS * D, orders[0])]


def plan_sizes(size, order):
    out = []
    for group in order:
        ways = 2 ** len(group)
        cut = ways if size % (16 * ways) == 0 else 1
        size //= cut
        out.append((ways, cut, size))
    return out


class Exchange:
    def __init__(self, buf, landing, send, recv, free):
        self.buf, self.landing, self.send, self.recv, self.free = buf, landing, send, recv, free
        index = {axis: lax.axis_index(axis) for axis in ("img", "win")}
        self.plans, land = [], 0
        for start, rows, order in jobs():
            plan = []
            for group, (ways, cut, size) in zip(order, plan_sizes(rows, order)):
                own = [(index[axis] // 2**bit) % 2 for axis, bit in group]
                peers = []
                for apart in range(1, ways):
                    to, piece = {}, 0
                    for n, (axis, bit) in enumerate(group):
                        here = own[n]
                        if apart >> n & 1:
                            to[axis] = to.get(axis, index[axis]) + 2**bit - 2 ** (bit + 1) * here
                            here = 1 - here
                        piece = piece + here * 2**n
                    peers.append((to, start + piece * size if cut > 1 else start, land))
                    land += size
                if cut > 1:
                    start = start + sum(here * 2**n for n, here in enumerate(own)) * size
                plan.append((start, size, cut, peers))
            self.plans.append(plan)
        self.bits = len(self.plans[0])
        self.stages = 2 * self.bits

    def peers(self):
        return [to for *_, peers in self.plans[0] for to, _, _ in peers]

    def copies(self, c, k):
        n = min(k, self.stages - 1 - k)
        keep, size, cut, peers = self.plans[c][n]
        if k >= self.bits and cut == 1:
            return []
        out = []
        for p, (to, give, land) in enumerate(peers):
            if k < self.bits:
                source, target = self.buf.at[pl.ds(pl.multiple_of(give, 16), size)], self.landing.at[pl.ds(land, size)]
            else:
                source = target = self.buf.at[pl.ds(pl.multiple_of(keep, 16), size)]
            out.append(
                pltpu.make_async_remote_copy(
                    source, target, self.send.at[c, k, p], self.recv.at[c, k, p], device_id=to, device_id_type=MESH
                )
            )
        return out

    def start(self, c, k):
        copies = self.copies(c, k)
        if copies and k >= self.bits:
            pl.semaphore_wait(self.free.at[c, self.stages - 1 - k], len(copies))
        for copy in copies:
            copy.start()

    def finish(self, c, k):
        for copy in self.copies(c, k):
            copy.wait()
        if k >= self.bits:
            return
        keep, size, cut, peers = self.plans[c][k]
        if cut > 1:
            for to, _, _ in peers:
                pl.semaphore_signal(self.free.at[c, k], inc=1, device_id=to, device_id_type=MESH)
        tile = max(t for t in (16, 32, 48, 64) if size % t == 0)

        def add(i, carry):
            here = pl.ds(pl.multiple_of(keep + i * tile, 16), tile)
            total = self.buf[here, :].astype(f32)
            for _, _, land in peers:
                total = total + self.landing[pl.ds(pl.multiple_of(land + i * tile, 16), tile), :].astype(f32)
            self.buf[here, :] = total.astype(bf16)
            return carry

        lax.fori_loop(0, size // tile, add, 0)

    def advance(self, which, k):
        for c in which:
            if 1 <= k <= self.stages:
                self.finish(c, k - 1)
            if k < self.stages:
                self.start(c, k)


def exchange_scratch():
    landing, most = 0, 0
    for _, rows, order in jobs():
        for ways, _, size in plan_sizes(rows, order):
            landing += size * (ways - 1)
            most = max(most, ways - 1)
    n, bits = len(jobs()), len(jobs()[0][2])
    dma = pltpu.SemaphoreType.DMA((n, 2 * bits, most))
    return [VMEM((landing, D), bf16), dma, dma, pltpu.SemaphoreType.REGULAR((n, bits))]


def finish_kernel(*refs):
    ins, outs = refs[:8], refs[8:]
    for n, out in enumerate(outs):
        for block in range(2):
            value = ins[2 * n + block][...].astype(f32)
            out[block] = value.T if n == 1 else value


def finish(grads_one, grads_two):
    slabs = [lambda j: (j, 0), lambda j: (4 + j, 0), lambda j: (8 + jnp.minimum(j, 2), 0), lambda j: (11, 0)]
    targets = [lambda j: (0, 0, j), lambda j: (0, j, 0), lambda j: (0, 0, jnp.minimum(j, 2)), lambda j: (0, 0, 0)]
    return pl.pallas_call(
        finish_kernel,
        grid=(4,),
        out_shape=tuple(jax.ShapeDtypeStruct((2,) + s, f32) for s in ((D, FF), (FF, D), (D, 3 * D), (D, D))),
        in_specs=[pl.BlockSpec((D, D), index) for index in slabs for _ in range(2)],
        out_specs=tuple(pl.BlockSpec((2, D, D), index) for index in targets),
        compiler_params=params(),
        name="finish_gradients",
    )(*[grads_one, grads_two] * 4)


def position_lookup():
    j = jnp.arange(KEYS)[:, None]
    i = jnp.arange(SLOT)[None, :]
    side = SIDE - 1
    index = (i // WINDOW - j // WINDOW + WINDOW - 1) * side + i % WINDOW - j % WINDOW + WINDOW - 1
    index = jnp.where((i < CELLS) & (j < CELLS), index, -1).reshape(-1)
    return (jnp.arange(side * side)[:, None] == index[None, :]).astype(f32)


def on_device(
    tokens, cotangent, crop_counts, crop_extent, norm_gain, norm_bias, qkv_weight, qv_bias, rel_table, proj_weight,
    out_bias, fc1_weight, fc1_bias, fc2_weight,
):
    crops = tokens.shape[0]
    x = tokens.reshape(crops, CELLS, D).transpose(1, 0, 2)
    cot = cotangent.reshape(crops, CELLS, D).transpose(1, 0, 2)
    lookup = position_lookup()
    highest = lax.Precision.HIGHEST
    bias = jnp.einsum("bkh,kp->bhp", rel_table, lookup, precision=highest) * LOG2E
    bias = bias.reshape(2, GROUPS, 4, KEYS, SLOT).transpose(0, 1, 3, 2, 4)
    bias = jnp.where(jnp.arange(KEYS)[:, None, None] < CELLS, bias, NEG).reshape(2, GROUPS, KEYS, 4 * SLOT)

    cells_of = lambda v: v.reshape(CELL + v.shape[1:])
    rows_of = lambda v: v.reshape((CELLS,) + v.shape[2:])
    x_first, x_last, cot_shifted, qw, pr, o16, mid, u = run_first(
        crop_extent, x, cells_of(cot), norm_gain, norm_bias, qkv_weight, qv_bias, bias, proj_weight, out_bias,
        fc1_weight, fc1_bias, fc2_weight,
    )
    y, dx_first, dx_last, grads_two = run_second(
        crop_extent, crop_counts, x_first, x_last, rows_of(cot_shifted), norm_gain, norm_bias, qkv_weight, qv_bias,
        bias, proj_weight, out_bias, fc1_weight, fc1_bias, fc2_weight,
    )
    dx, sum_one, sum_two, output = run_third(
        x, dx_first, dx_last, cells_of(y), qw, pr, o16, mid, u, norm_gain, norm_bias, qkv_weight, proj_weight,
        fc1_weight, fc2_weight, grads_two,
    )
    fc1, fc2, qkv, proj = finish(sum_one, sum_two)
    rows = jnp.stack([sum_one[SLABS * D :], sum_two[SLABS * D :]]).astype(f32)
    dbias = rows[:, SMALL : SMALL + TABLE, : 4 * SLOT].reshape(2, GROUPS, KEYS, 4, SLOT).transpose(0, 1, 3, 2, 4)
    table = jnp.einsum("hp,kp->kh", dbias.reshape(2 * HEADS, KEYS * SLOT), lookup, precision=highest)
    table = table.reshape(-1, 2, HEADS).transpose(1, 0, 2)
    back = lambda v: v.transpose(1, 0, 2).reshape(tokens.shape)
    return (
        back(rows_of(output)), back(dx), rows[:, 0:2], rows[:, 2:4], qkv, rows[:, 4:6], table, proj, rows[:, 6:8], fc1,
        rows[:, 8:12].reshape(2, FF), fc2,
    )


def solution(mesh):
    split = P("img", "win", None, None)
    return jax.shard_map(
        on_device,
        mesh=mesh,
        in_specs=(split, split, P("img"), P("img", None)) + (P(),) * 10,
        out_specs=(split, split) + (P(),) * 10,
        check_vma=False,
    )
```

```python
import jax
import jax.numpy as jnp
from jax import lax
from jax.experimental import pallas as pl
from jax.experimental.pallas import tpu as pltpu
from jax.sharding import PartitionSpec as P

D = 384
FF = 1536
HEADS = 12
HEAD_DIM = 32
WINDOW = 7
SHIFT = 3
CELLS = WINDOW * WINDOW
SIDE = 2 * WINDOW
HALF = 16
ROWS = CELLS * HALF
LANES = 128
GROUPS = 3
KEYS = 56
SLOT = 64
SLABS = 12
SMALL = 16
TABLE = GROUPS * KEYS
SUMS = SLABS * D + 256
GROUPED = ((0, 1), (2, 3), (4, 5, 6))
NEG = -1e30
LOG2E = 1.4426950408889634
SCALE = HEAD_DIM**-0.5
MESH = pl.DeviceIdType.MESH

bf16 = jnp.bfloat16
f32 = jnp.float32
VMEM = pltpu.VMEM


def mm(a, b):
    return lax.dot_general(a, b, (((1,), (0,)), ((), ())), preferred_element_type=f32)


def mm_bt(a, b):
    return lax.dot_general(a, b, (((1,), (1,)), ((), ())), preferred_element_type=f32)


def mm_at(a, b):
    return lax.dot_general(a, b, (((0,), (0,)), ((), ())), preferred_element_type=f32)


def norm(x):
    centred = x - jnp.mean(x, -1, keepdims=True)
    rstd = lax.rsqrt(jnp.mean(centred * centred, -1, keepdims=True) + 1e-5)
    return centred * rstd, rstd


def norm_back(xh, rstd, dn, gain):
    e = dn * gain
    mean_e = jnp.mean(e, -1, keepdims=True)
    mean_ex = jnp.mean(e * xh, -1, keepdims=True)
    dx = rstd * (e - mean_e - xh * mean_ex)
    return dx, jnp.sum(dn * xh, 0, keepdims=True), jnp.sum(dn, 0, keepdims=True)


def gelu(u):
    phi = 0.5 + 0.5 * lax.erf(u * 0.7071067811865476)
    return u * phi, phi


def gelu_slope(u, phi):
    return phi + u * jnp.exp2(u * u * (-0.5 * LOG2E)) * 0.3989422804014327


def spread(rows):
    head = lax.broadcasted_iota(jnp.int32, rows.shape, 1) // HEAD_DIM
    zero = jnp.zeros_like(rows)
    return jnp.concatenate([jnp.where(head == h, rows, zero) for h in range(4)], 0)


def gather_heads(rows):
    head = lax.broadcasted_iota(jnp.int32, (KEYS, LANES), 1) // HEAD_DIM
    out = rows[:KEYS]
    for h in range(1, 4):
        out = jnp.where(head == h, rows[SLOT * h : SLOT * h + KEYS], out)
    return out


def to_windows(ref, slot, part):
    parted = part.reshape(CELLS, 2, 8, LANES)
    for cg in range(2):
        ref[cg, slot, 0 : CELLS * 8, :] = parted[:, cg].reshape(CELLS * 8, LANES)


def from_windows(ref, slot):
    parts = [ref[cg, slot, 0 : CELLS * 8, :].reshape(CELLS, 1, 8, LANES) for cg in range(2)]
    return jnp.concatenate(parts, 1).reshape(ROWS, LANES)


def cells(shifted):
    win = lax.axis_index("win")
    j = lax.broadcasted_iota(jnp.int32, (KEYS, LANES), 0)
    i = lax.broadcasted_iota(jnp.int32, (KEYS, LANES), 1) % SLOT
    top, left = WINDOW * (win // 2), WINDOW * (win % 2)
    places = [top + j // WINDOW, left + j % WINDOW, top + i // WINDOW, left + i % WINDOW]
    if not shifted:
        return places, None
    region = [(v >= SIDE - WINDOW).astype(jnp.int32) + (v >= SIDE - SHIFT).astype(jnp.int32) for v in places]
    apart = (region[0] != region[2]) | (region[1] != region[3])
    moved = [jnp.where(v + SHIFT >= SIDE, v + SHIFT - SIDE, v + SHIFT) for v in places]
    return moved, jnp.where(apart, NEG, 0.0)


def forward(step, block, shifted, x, refs, keep_n1=None, keep_n2=None, keep_gelu=None, keep_u=None):
    (ext, gain, beta, wqkv, qvb, bias, wp, ob, w1, b1, w2, xs, qw, ss, pr, os, o16, mid) = refs
    xh, _ = norm(x)
    n1 = (xh * gain[block, 0:1, :] + beta[block, 0:1, :]).astype(bf16)
    if keep_n1 is not None:
        keep_n1[step] = n1
    proj = mm(n1, wqkv[...])
    q = (proj[:, :D] + qvb[block, 0:1, :]) * (SCALE * LOG2E)
    k = proj[:, D : 2 * D]
    v = proj[:, 2 * D :] + qvb[block, 1:2, :]
    for g in range(GROUPS):
        cut = slice(LANES * g, LANES * (g + 1))
        to_windows(xs, g, q[:, cut])
        to_windows(xs, GROUPS + g, k[:, cut])
        to_windows(xs, 2 * GROUPS + g, v[:, cut])
    places, apart = cells(shifted)
    if apart is not None:
        apart = jnp.concatenate([apart, apart], 1)

    def scores(w, carry):
        cg, c = w // 8, w % 8
        rows, cols = ext[step * HALF + w, 0], ext[step * HALF + w, 1]
        valid_j = (places[0] < rows) & (places[1] < cols)
        valid_i = (places[2] < rows) & (places[3] < cols)
        mask = jnp.where(valid_i == valid_j, 0.0, NEG)
        mask = jnp.concatenate([mask, mask], 1)
        if apart is not None:
            mask = mask + apart
        for g in range(GROUPS):
            qs, ks, vs = (
                xs[cg, GROUPS * n + g, pl.ds(c, SLOT, stride=8), :].astype(bf16) for n in range(3)
            )
            qw[w, g] = qs
            qw[w, GROUPS + g] = ks
            qw[w, 2 * GROUPS + g] = vs
            ss[w, g] = mm_bt(ks[:KEYS], spread(qs)) + bias[g] + mask
        return carry

    lax.fori_loop(0, HALF, scores, 0, unroll=8)

    def mix(w, carry):
        cg, c = w // 8, w % 8
        for g in range(GROUPS):
            s = ss[w, g]
            e = jnp.exp2(s - jnp.max(s, 0, keepdims=True))
            p = (e * (1.0 / jnp.sum(e, 0, keepdims=True))).astype(bf16)
            pr[w, g] = p
            os[cg, g, pl.ds(c, KEYS, stride=8), :] = gather_heads(mm_at(p, qw[w, 2 * GROUPS + g][:KEYS]))
        return carry

    lax.fori_loop(0, HALF, mix, 0, unroll=8)
    for g in range(GROUPS):
        o16[:, LANES * g : LANES * (g + 1)] = from_windows(os, g).astype(bf16)
    middle = x + (mm(o16[...], wp[...]) + ob[block, 0:1, :])
    mid[...] = middle
    xh2, _ = norm(middle)
    n2 = (xh2 * gain[block, 1:2, :] + beta[block, 1:2, :]).astype(bf16)
    if keep_n2 is not None:
        keep_n2[step] = n2
    y = middle + ob[block, 1:2, :]
    for part in range(3):
        cut = slice(512 * part, 512 * (part + 1))
        u = mm(n2, w1[:, cut]) + b1[block : block + 1, cut]
        if keep_u is not None:
            keep_u[:, cut] = u.astype(bf16)
        z, phi = gelu(u)
        z = z.astype(bf16)
        if keep_gelu is not None:
            keep_gelu[0][step, :, cut] = z
            keep_gelu[1][:, cut] = gelu_slope(u, phi).astype(bf16)
        y = y + mm(z, w2[cut, :])
    return y


def no_tick(point, when=True):
    pass


def mlp_back(step, block, mid, dy, refs, slope, keep_n2=None, beta=None, tick=no_tick):
    (gain, wp, w1, w2, dos, dm_all, du_all, da_all, small) = refs

    def add_small(row, value):
        small[row : row + 1, :] += value

    dm = dy.astype(bf16)
    dm_all[step] = dm
    add_small(7, jnp.sum(dm.astype(f32), 0, keepdims=True))
    dn2 = jnp.zeros((ROWS, D), f32)
    for part in range(4):
        cut = slice(384 * part, 384 * (part + 1))
        du = (mm_bt(dm, w2[cut, :]) * slope(cut)).astype(bf16)
        du_all[step, :, cut] = du
        add_small(8 + part, jnp.sum(du.astype(f32), 0, keepdims=True))
        dn2 = dn2 + mm_bt(du, w1[:, cut])
        tick(part)
    xh, rstd = norm(mid)
    if keep_n2 is not None:
        keep_n2[step] = (xh * gain[block, 1:2, :] + beta[block, 1:2, :]).astype(bf16)
    dx, dgain, dbeta = norm_back(xh, rstd, dn2, gain[block, 1:2, :])
    add_small(1, dgain)
    add_small(3, dbeta)
    dmid = dy + dx
    da = dmid.astype(bf16)
    da_all[step] = da
    add_small(6, jnp.sum(da.astype(f32), 0, keepdims=True))
    do = mm_bt(da, wp[...])
    for g in range(GROUPS):
        to_windows(dos, g, do[:, LANES * g : LANES * (g + 1)])
    tick(4)
    return dmid


def attention_back(step, block, x, dmid, refs, keep_n1=None, beta=None, tick=no_tick):
    (gain, wqkv, xs, qw, pr, dos, dp_all, small, dbias) = refs

    def add_small(row, value):
        small[row : row + 1, :] += value

    def window_back(w, carry):
        cg, c = w // 8, w % 8
        for g in range(GROUPS):
            d = spread(dos[cg, g, pl.ds(c, SLOT, stride=8), :].astype(bf16))
            p16 = pr[w, g]
            p = p16.astype(f32)
            t = p * mm_bt(qw[w, 2 * GROUPS + g][:KEYS], d)
            ds = (t - p * jnp.sum(t, 0, keepdims=True)).astype(bf16)
            dbias[g] += ds.astype(f32)
            dq = gather_heads(mm_at(ds, qw[w, GROUPS + g][:KEYS])) * SCALE
            dk = mm(ds, spread(qw[w, g])) * (1.0 / LOG2E)
            for n, value in enumerate((dq, dk, mm(p16, d))):
                xs[cg, GROUPS * n + g, pl.ds(c, KEYS, stride=8), :] = value
        return carry

    def four_back(part, carry):
        for n in range(4):
            window_back(4 * part + n, carry)
        for n in range(4):
            tick(n, part == n)
        return carry

    lax.fori_loop(0, 4, four_back, 0)
    for n in range(3 * GROUPS):
        dp_all[step, :, LANES * n : LANES * (n + 1)] = from_windows(xs, n).astype(bf16)
    dp = dp_all[step, :, : 3 * D]
    add_small(4, jnp.sum(dp[:, :D].astype(f32), 0, keepdims=True))
    add_small(5, jnp.sum(dp[:, 2 * D :].astype(f32), 0, keepdims=True))
    dn1 = mm_bt(dp, wqkv[...])
    tick(4)
    xh, rstd = norm(x)
    if keep_n1 is not None:
        keep_n1[step] = (xh * gain[block, 0:1, :] + beta[block, 0:1, :]).astype(bf16)
    dx, dgain, dbeta = norm_back(xh, rstd, dn1, gain[block, 0:1, :])
    add_small(0, dgain)
    add_small(2, dbeta)
    tick(5)
    return dmid() + dx


def flat(ref, cut=slice(None)):
    return ref[:, :, cut].reshape(2 * ROWS, -1)


def put_slabs(out, first, value):
    for j in range(value.shape[1] // D):
        out[D * (first + j) : D * (first + j + 1), :] = value[:, D * j : D * (j + 1)].astype(bf16)


def fc_grads(n2, z, dm, du, out, tick=no_tick):
    for first, left, right in ((0, n2, du), (4, dm, z)):
        for j in range(2):
            put_slabs(out, first + 2 * j, mm_at(flat(left), flat(right, slice(768 * j, 768 * (j + 1)))))
        tick(first // 4)


def attention_grads(n1, o16, da, dp, out):
    put_slabs(out, 8, mm_at(flat(n1), flat(dp, slice(3 * D))))
    put_slabs(out, 11, mm_at(flat(o16), flat(da)))


def small_grads(small, dbias, out):
    base = SLABS * D
    out[base : base + SMALL, :] = small[...].astype(bf16)
    out[base + SMALL : SUMS, :] = jnp.zeros((SUMS - base - SMALL, D), bf16)
    out[base + SMALL : base + SMALL + TABLE, : 4 * SLOT] = dbias[...].reshape(TABLE, 4 * SLOT).astype(bf16)


KEEP = WINDOW - SHIFT
NEAR, FAR = slice(0, KEEP), slice(KEEP, WINDOW)
HERE, THERE = slice(SHIFT, WINDOW), slice(0, SHIFT)


def shift_peers():
    win = lax.axis_index("win")
    beside = 1 - 2 * (win % 2)
    below = 2 - 4 * (win // 2 % 2)
    return [{"win": win + beside}, {"win": win + below}, {"win": win + beside + below}]


def shift_copies(source, target, send, recv, back=False):
    plain = [(HERE, HERE), (HERE, THERE), (THERE, HERE), (THERE, THERE)]
    moved = [(NEAR, NEAR), (NEAR, FAR), (FAR, NEAR), (FAR, FAR)]
    if back:
        plain, moved = moved, plain
    out = [pltpu.make_async_copy(source.at[plain[0]], target.at[moved[0]], send.at[3])]
    for n, to in enumerate(shift_peers()):
        out.append(
            pltpu.make_async_remote_copy(
                source.at[plain[n + 1]], target.at[moved[n + 1]], send.at[n], recv.at[n], device_id=to, device_id_type=MESH
            )
        )
    return out


def start_all(copies):
    for copy in copies:
        copy.start()


def wait_all(copies):
    for copy in copies:
        copy.wait()


def greet(peers):
    barrier = pltpu.get_barrier_semaphore()
    for to in peers:
        pl.semaphore_signal(barrier, inc=1, device_id=to, device_id_type=MESH)
    pl.semaphore_wait(barrier, len(peers))


def first_kernel(
    ext, x_ref, cot, gain, beta, wqkv, qvb, bias, wp, ob, w1, b1, w2,
    y_shifted, y_last, cot_shifted, qw, pr, o16, mid, u_ref, xs, ss, os, y_first, send, recv,
):
    step = pl.program_id(0)
    cot_copies = shift_copies(cot, cot_shifted, send.at[0], recv.at[0])
    y_copies = shift_copies(y_first, y_shifted, send.at[1], recv.at[1])

    @pl.when(step == 0)
    def _():
        greet(shift_peers())
        start_all(cot_copies)
        xs[...] = jnp.zeros_like(xs)

    x = x_ref[...].reshape(ROWS, D).astype(f32)
    y = forward(
        step, 0, False, x, (ext, gain, beta, wqkv, qvb, bias, wp, ob, w1, b1, w2, xs, qw, ss, pr, os, o16, mid), keep_u=u_ref
    )
    y = y.astype(bf16).reshape(WINDOW, WINDOW, HALF, D)

    @pl.when(step == 0)
    def _():
        y_first[...] = y
        start_all(y_copies)

    @pl.when(step == 1)
    def _():
        y_last[...] = y
        wait_all(y_copies)
        wait_all(cot_copies)


def second_kernel(
    ext, count, x_first, x_last, cot_ref, gain, beta, wqkv, qvb, bias, wp, ob, w1, b1, w2,
    y_ref, dx_shifted, dx_last, grads,
    xs, qw, ss, pr, os, mid, slope, dos, small, dbias, n1, n2, o16, z, dm, du, da, dp, x_both, dx_first, send, recv, local,
):
    step = pl.program_id(0)
    x_copies = shift_copies(x_last, x_both.at[1], send.at[0], recv.at[0])
    dx_copies = shift_copies(dx_first, dx_shifted, send.at[1], recv.at[1], back=True)

    @pl.when(step == 0)
    def _():
        load = pltpu.make_async_copy(x_first, x_both.at[0], local)
        load.start()
        greet(shift_peers())
        start_all(x_copies)
        load.wait()
        xs[...] = jnp.zeros_like(xs)
        dos[...] = jnp.zeros_like(dos)
        small[...] = jnp.zeros_like(small)
        dbias[...] = jnp.zeros_like(dbias)

    @pl.when(step == 1)
    def _():
        wait_all(x_copies)

    x = x_both[step].reshape(ROWS, D).astype(f32)
    live = lax.broadcasted_iota(jnp.int32, (CELLS, HALF, 1), 1) + step * HALF < count[0]
    y = forward(
        step, 1, True, x,
        (ext, gain, beta, wqkv, qvb, bias, wp, ob, w1, b1, w2, xs, qw, ss, pr, os, o16.at[step], mid),
        n1, n2, (z, slope),
    )
    y_ref[...] = jnp.where(live, y.reshape(CELLS, HALF, D), 0.0).astype(bf16)
    dy = jnp.where(live, cot_ref[...].astype(f32), 0.0).reshape(ROWS, D)
    mid[...] = mlp_back(
        step, 1, mid[...], dy, (gain, wp, w1, w2, dos, dm, du, da, small), lambda cut: slope[:, cut].astype(f32)
    )
    dx = attention_back(
        step, 1, x, lambda: mid[...], (gain, wqkv, xs, qw, pr, dos, dp, small, dbias)
    )
    dx = dx.astype(bf16).reshape(WINDOW, WINDOW, HALF, D)

    @pl.when(step == 0)
    def _():
        dx_first[...] = dx
        start_all(dx_copies)

    @pl.when(step == 1)
    def _():
        dx_last[...] = dx
        fc_grads(n2, z, dm, du, grads)
        attention_grads(n1, o16, da, dp, grads)
        small_grads(small, dbias, grads)
        wait_all(dx_copies)


LAST = 24
PACE = {
    (0, 0): (0.7, 1.2, 7.0, 9.9, 21.7, 30.9, 33.3),
    (0, 1): (1.9, 2.5, 19.4, 21.6, 24.6, 37.8, 43.3),
    (0, 2): (0.5, 3.1, 8.9, 11.1, 17.0, 38.1, 41.8),
    (1, 0): (20.4, 23.4, 30.3, 34.0, 38.6, 40.3, 46.2),
    (1, 1): (12.8, 20.1, 26.6, 27.5, 33.4, 38.6, 46.7),
    (1, 2): (26.5, 26.9, 32.8, 35.9, 38.9, 44.4, 51.2),
}


def schedule(*exchanges):
    out = []
    for (which, group), places in PACE.items():
        exchange = exchanges[which]
        if exchange.stages + 1 != len(places):
            first = LAST + 1 if which and group == 2 else places[0]
            places = [first + 4 * k + 0.1 * group for k in range(exchange.stages + 1)]
        out += [(place, exchange, group, k) for k, place in enumerate(places)]
    return sorted(out, key=lambda item: item[0])


def third_kernel(
    x_ref, dy_first, dy_last, y_ref, qw, pr, o_ref, mid, u_ref, gain, beta, wqkv, wp, w1, w2, two_ref,
    dx_ref, one_out, two_out, y_out,
    xs, dos, small, dbias, dmid, n2, o16, z, dm, du, da,
    one, two, land_one, send_one, recv_one, free_one, land_two, send_two, recv_two, free_two, local, loads, dy_both, send, recv,
):
    step = pl.program_id(0)
    first = Exchange(one, land_one, send_one, recv_one, free_one)
    second = Exchange(two, land_two, send_two, recv_two, free_two)
    dy_copies = shift_copies(dy_last, dy_both.at[1], send.at[0], recv.at[0], back=True)
    y_copies = shift_copies(y_ref, y_out, send.at[1], recv.at[1], back=True)
    moves = [[] for _ in range(LAST + 1)]
    late = []
    for place, exchange, group, k in schedule(second, first):
        (moves[int(place)] if place < LAST + 1 else late).append((exchange, group, k))

    def tick(n):
        if n == 8:
            start_all(y_copies)
        for exchange, group, k in moves[n]:
            exchange.advance(GROUPED[group], k)

    def tick_at(steps, base, per_step):
        def ticker(point, when=True):
            for s in steps:
                pl.when((step == s) & when)(lambda s=s: tick(base + (s - steps[0]) * per_step + point))

        return ticker

    def kept(half):
        rows = pl.ds(half * ROWS, ROWS)
        return (
            pltpu.make_async_copy(u_ref.at[rows], z.at[half], loads.at[0, half]),
            pltpu.make_async_copy(o_ref.at[rows], o16.at[half], loads.at[1, half]),
        )

    @pl.when(step == 0)
    def _():
        load = pltpu.make_async_copy(two_ref, two, local.at[0])
        load.start()
        load_dy = pltpu.make_async_copy(dy_first, dy_both.at[0], local.at[1])
        load_dy.start()
        for half in range(2):
            start_all(kept(half))
        greet(second.peers() + shift_peers()[2:])
        start_all(dy_copies)
        xs[...] = jnp.zeros_like(xs)
        dos[...] = jnp.zeros_like(dos)
        small[...] = jnp.zeros_like(small)
        dbias[...] = jnp.zeros_like(dbias)
        load.wait()
        tick(0)
        load_dy.wait()

    for half in range(2):

        @pl.when(step == half)
        def _():
            wait_all(kept(half))
            if half:
                wait_all(dy_copies)

    @pl.when(step < 2)
    def _():
        def slope(cut):
            u = z[step, :, cut].astype(f32)
            value, phi = gelu(u)
            z[step, :, cut] = value.astype(bf16)
            return gelu_slope(u, phi)

        dmid[step] = mlp_back(
            step, 0, mid[...], dy_both[step].astype(f32).reshape(ROWS, D),
            (gain, wp, w1, w2, dos.at[step], dm, du, da, small), slope, n2, beta, tick_at((0, 1), 1, 5),
        )

    @pl.when(step == 1)
    def _():
        fc_grads(n2, z, dm, du, one, lambda point: tick(11 + point))

    @pl.when(step >= 2)
    def _():
        half = step - 2
        dx = attention_back(
            half, 0, x_ref[...].reshape(ROWS, D).astype(f32), lambda: dmid[half],
            (gain, wqkv, xs, qw, pr, dos.at[half], du, small, dbias), n2, beta, tick_at((2, 3), 13, 6),
        )
        dx_ref[...] = dx.astype(bf16).reshape(dx_ref.shape)

    @pl.when(step == 3)
    def _():
        attention_grads(n2, o16, da, du, one)
        small_grads(small, dbias, one)
        for n, (exchange, group, k) in enumerate(late):
            exchange.advance(GROUPED[group], k)
            if all(other is not second for other, _, _ in late[n + 1 :]) and (exchange is second or n == 0):
                store_two = pltpu.make_async_copy(two, two_out, local.at[0])
                store_two.start()
        store_one = pltpu.make_async_copy(one, one_out, local.at[1])
        store_one.start()
        wait_all(y_copies)
        store_one.wait()
        store_two.wait()


def whole(shape):
    return pl.BlockSpec(shape, lambda s: (0,) * len(shape), pipeline_mode=pl.Buffered(1))


def of_block(block, *shape):
    return pl.BlockSpec((None,) + shape, lambda s: (block,) + (0,) * len(shape), pipeline_mode=pl.Buffered(1))


def by_half(*shape, buffers=2):
    return pl.BlockSpec(shape, lambda s: (s,) + (0,) * (len(shape) - 1), pipeline_mode=pl.Buffered(buffers))


ANY_SPEC = pl.BlockSpec(memory_space=pl.ANY)
SMEM_SPEC = pl.BlockSpec(memory_space=pltpu.SMEM)
TOKEN_SPEC = pl.BlockSpec((CELLS, HALF, D), lambda s: (0, s, 0))
XS = VMEM((2, 3 * GROUPS, 8 * SLOT, LANES), f32)
DOS = VMEM((2, GROUPS, 8 * SLOT, LANES), f32)
QW = (HALF, 3 * GROUPS, SLOT, LANES)
PR = (HALF, GROUPS, KEYS, 4 * SLOT)


def params(collective_id=None, mib=61):
    return pltpu.CompilerParams(
        vmem_limit_bytes=mib * 2**20, dimension_semantics=("arbitrary",), collective_id=collective_id,
        has_side_effects=collective_id is not None,
    )


CELL = (WINDOW, WINDOW)
PART = jax.ShapeDtypeStruct(CELL + (HALF, D), bf16)
SHIFTS = [pltpu.SemaphoreType.DMA((2, 4)), pltpu.SemaphoreType.DMA((2, 4))]


def run_first(ext, x, cot, gain, beta, wqkv, qvb, bias, wp, ob, w1, b1, w2):
    crops = x.shape[1]
    return pl.pallas_call(
        first_kernel,
        grid=(2,),
        out_shape=(
            PART,
            PART,
            jax.ShapeDtypeStruct(cot.shape, bf16),
            jax.ShapeDtypeStruct((crops,) + QW[1:], bf16),
            jax.ShapeDtypeStruct((crops,) + PR[1:], bf16),
            jax.ShapeDtypeStruct((2 * ROWS, D), bf16),
            jax.ShapeDtypeStruct((2 * ROWS, D), f32),
            jax.ShapeDtypeStruct((2 * ROWS, FF), bf16),
        ),
        in_specs=[
            SMEM_SPEC, TOKEN_SPEC, ANY_SPEC, whole(gain.shape), whole(beta.shape), of_block(0, D, 3 * D), whole(qvb.shape),
            of_block(0, GROUPS, KEYS, 4 * SLOT), of_block(0, D, D), whole(ob.shape), of_block(0, D, FF),
            whole(b1.shape), of_block(0, FF, D),
        ],
        out_specs=(
            ANY_SPEC, whole(PART.shape), ANY_SPEC, by_half(*QW), by_half(*PR), by_half(ROWS, D), by_half(ROWS, D),
            by_half(ROWS, FF),
        ),
        scratch_shapes=[
            XS, VMEM(PR, f32), VMEM((2, GROUPS, 8 * KEYS, LANES), f32), VMEM(PART.shape, bf16),
        ] + SHIFTS,
        compiler_params=params(1),
        name="first_forward",
    )(ext, x, cot, gain, beta, wqkv, qvb, bias, wp, ob, w1, b1, w2)


GRADS = jax.ShapeDtypeStruct((SUMS, D), bf16)
SMALLS = [VMEM((SMALL, D), f32), VMEM((GROUPS, KEYS, 4 * SLOT), f32)]


def run_second(ext, count, x_first, x_last, cot, gain, beta, wqkv, qvb, bias, wp, ob, w1, b1, w2):
    return pl.pallas_call(
        second_kernel,
        grid=(2,),
        out_shape=(jax.ShapeDtypeStruct(cot.shape, bf16), PART, PART, GRADS),
        in_specs=[
            SMEM_SPEC, SMEM_SPEC, ANY_SPEC, ANY_SPEC, TOKEN_SPEC, whole(gain.shape), whole(beta.shape), of_block(1, D, 3 * D),
            whole(qvb.shape), of_block(1, GROUPS, KEYS, 4 * SLOT), of_block(1, D, D), whole(ob.shape),
            of_block(1, D, FF), whole(b1.shape), of_block(1, FF, D),
        ],
        out_specs=(TOKEN_SPEC, ANY_SPEC, whole(PART.shape), whole(GRADS.shape)),
        scratch_shapes=[
            XS, VMEM(QW, bf16), VMEM(PR, f32), VMEM(PR, bf16), VMEM((2, GROUPS, 8 * KEYS, LANES), f32),
            VMEM((ROWS, D), f32), VMEM((ROWS, FF), bf16), DOS,
        ] + SMALLS + [VMEM((2, ROWS, width), bf16) for width in (D, D, D, FF, D, FF, D, 3 * D)]
        + [VMEM((2,) + PART.shape, bf16), VMEM(PART.shape, bf16)] + SHIFTS + [pltpu.SemaphoreType.DMA(())],
        compiler_params=params(2, 63),
        name="second_block",
    )(ext, count, x_first, x_last, cot, gain, beta, wqkv, qvb, bias, wp, ob, w1, b1, w2)


def in_steps(first, *shape, axis=0, buffers=2):
    def index(s):
        return tuple(jnp.clip(s - first, 0, 1) if n == axis else 0 for n in range(len(shape)))

    return pl.BlockSpec(shape, index, pipeline_mode=pl.Buffered(buffers))


def run_third(x, dy_first, dy_last, y, qw, pr, o16, mid, u, gain, beta, wqkv, wp, w1, w2, two):
    tokens = (CELLS, HALF, D)
    return pl.pallas_call(
        third_kernel,
        grid=(4,),
        out_shape=(jax.ShapeDtypeStruct(x.shape, bf16), GRADS, GRADS, jax.ShapeDtypeStruct(y.shape, bf16)),
        in_specs=[
            in_steps(2, *tokens, axis=1), ANY_SPEC, ANY_SPEC, ANY_SPEC, in_steps(2, *QW, buffers=1),
            in_steps(2, *PR, buffers=1), ANY_SPEC, in_steps(0, ROWS, D), ANY_SPEC,
            whole(gain.shape), whole(beta.shape), of_block(0, D, 3 * D), of_block(0, D, D), of_block(0, D, FF),
            of_block(0, FF, D), ANY_SPEC,
        ],
        out_specs=(in_steps(2, *tokens, axis=1), ANY_SPEC, ANY_SPEC, ANY_SPEC),
        scratch_shapes=[XS, VMEM((2,) + DOS.shape, f32)] + SMALLS + [VMEM((2, ROWS, D), f32)]
        + [VMEM((2, ROWS, width), bf16) for width in (D, D, FF, D, FF, D)]
        + [VMEM(GRADS.shape, bf16)] * 2 + exchange_scratch() * 2
        + [pltpu.SemaphoreType.DMA((2,)), pltpu.SemaphoreType.DMA((2, 2)), VMEM((2,) + PART.shape, bf16)] + SHIFTS,
        compiler_params=params(0, 63),
        name="first_backward",
    )(x, dy_first, dy_last, y, qw, pr, o16, mid, u, gain, beta, wqkv, wp, w1, w2, two)


def jobs():
    n_img, n_win = lax.axis_size("img"), lax.axis_size("win")
    bits = [("win", b) for b in range(1, n_win.bit_length() - 1)] + [("img", b) for b in range(n_img.bit_length() - 1)]
    pairs = [bits[n : n + 2] for n in range(0, len(bits), 2)]
    orders = [[[("win", 0)]] + pairs, [[("win", 0)]] + pairs[::-1]]
    out = []
    for group in range(3):
        out += [(1536 * group, 1024, orders[0]), (1536 * group + 1024, 512, orders[1])]
    return out + [(SLABS * D, SUMS - SLABS * D, orders[0])]


def plan_sizes(size, order):
    out = []
    for group in order:
        ways = 2 ** len(group)
        cut = ways if size % (16 * ways) == 0 else 1
        size //= cut
        out.append((ways, cut, size))
    return out


class Exchange:
    def __init__(self, buf, landing, send, recv, free):
        self.buf, self.landing, self.send, self.recv, self.free = buf, landing, send, recv, free
        index = {axis: lax.axis_index(axis) for axis in ("img", "win")}
        self.plans, land = [], 0
        for start, rows, order in jobs():
            plan = []
            for group, (ways, cut, size) in zip(order, plan_sizes(rows, order)):
                own = [(index[axis] // 2**bit) % 2 for axis, bit in group]
                peers = []
                for apart in range(1, ways):
                    to, piece = {}, 0
                    for n, (axis, bit) in enumerate(group):
                        here = own[n]
                        if apart >> n & 1:
                            to[axis] = to.get(axis, index[axis]) + 2**bit - 2 ** (bit + 1) * here
                            here = 1 - here
                        piece = piece + here * 2**n
                    peers.append((to, start + piece * size if cut > 1 else start, land))
                    land += size
                if cut > 1:
                    start = start + sum(here * 2**n for n, here in enumerate(own)) * size
                plan.append((start, size, cut, peers))
            self.plans.append(plan)
        self.bits = len(self.plans[0])
        self.stages = 2 * self.bits

    def peers(self):
        return [to for *_, peers in self.plans[0] for to, _, _ in peers]

    def copies(self, c, k):
        n = min(k, self.stages - 1 - k)
        keep, size, cut, peers = self.plans[c][n]
        if k >= self.bits and cut == 1:
            return []
        out = []
        for p, (to, give, land) in enumerate(peers):
            if k < self.bits:
                source, target = self.buf.at[pl.ds(pl.multiple_of(give, 16), size)], self.landing.at[pl.ds(land, size)]
            else:
                source = target = self.buf.at[pl.ds(pl.multiple_of(keep, 16), size)]
            out.append(
                pltpu.make_async_remote_copy(
                    source, target, self.send.at[c, k, p], self.recv.at[c, k, p], device_id=to, device_id_type=MESH
                )
            )
        return out

    def start(self, c, k):
        copies = self.copies(c, k)
        if copies and k >= self.bits:
            pl.semaphore_wait(self.free.at[c, self.stages - 1 - k], len(copies))
        for copy in copies:
            copy.start()

    def finish(self, c, k):
        for copy in self.copies(c, k):
            copy.wait()
        if k >= self.bits:
            return
        keep, size, cut, peers = self.plans[c][k]
        if cut > 1:
            for to, _, _ in peers:
                pl.semaphore_signal(self.free.at[c, k], inc=1, device_id=to, device_id_type=MESH)
        tile = max(t for t in (16, 32, 48, 64) if size % t == 0)

        def add(i, carry):
            here = pl.ds(pl.multiple_of(keep + i * tile, 16), tile)
            total = self.buf[here, :].astype(f32)
            for _, _, land in peers:
                total = total + self.landing[pl.ds(pl.multiple_of(land + i * tile, 16), tile), :].astype(f32)
            self.buf[here, :] = total.astype(bf16)
            return carry

        lax.fori_loop(0, size // tile, add, 0)

    def advance(self, which, k):
        for c in which:
            if 1 <= k <= self.stages:
                self.finish(c, k - 1)
            if k < self.stages:
                self.start(c, k)


def exchange_scratch():
    landing, most = 0, 0
    for _, rows, order in jobs():
        for ways, _, size in plan_sizes(rows, order):
            landing += size * (ways - 1)
            most = max(most, ways - 1)
    n, bits = len(jobs()), len(jobs()[0][2])
    dma = pltpu.SemaphoreType.DMA((n, 2 * bits, most))
    return [VMEM((landing, D), bf16), dma, dma, pltpu.SemaphoreType.REGULAR((n, bits))]


def finish_kernel(*refs):
    ins, outs = refs[:8], refs[8:]
    for n, out in enumerate(outs):
        for block in range(2):
            value = ins[2 * n + block][...].astype(f32)
            out[block] = value.T if n == 1 else value


def finish(grads_one, grads_two):
    slabs = [lambda j: (j, 0), lambda j: (4 + j, 0), lambda j: (8 + jnp.minimum(j, 2), 0), lambda j: (11, 0)]
    targets = [lambda j: (0, 0, j), lambda j: (0, j, 0), lambda j: (0, 0, jnp.minimum(j, 2)), lambda j: (0, 0, 0)]
    return pl.pallas_call(
        finish_kernel,
        grid=(4,),
        out_shape=tuple(jax.ShapeDtypeStruct((2,) + s, f32) for s in ((D, FF), (FF, D), (D, 3 * D), (D, D))),
        in_specs=[pl.BlockSpec((D, D), index) for index in slabs for _ in range(2)],
        out_specs=tuple(pl.BlockSpec((2, D, D), index) for index in targets),
        compiler_params=params(),
        name="finish_gradients",
    )(*[grads_one, grads_two] * 4)


def position_lookup():
    j = jnp.arange(KEYS)[:, None]
    i = jnp.arange(SLOT)[None, :]
    side = SIDE - 1
    index = (i // WINDOW - j // WINDOW + WINDOW - 1) * side + i % WINDOW - j % WINDOW + WINDOW - 1
    index = jnp.where((i < CELLS) & (j < CELLS), index, -1).reshape(-1)
    return (jnp.arange(side * side)[:, None] == index[None, :]).astype(f32)


def on_device(
    tokens, cotangent, crop_counts, crop_extent, norm_gain, norm_bias, qkv_weight, qv_bias, rel_table, proj_weight,
    out_bias, fc1_weight, fc1_bias, fc2_weight,
):
    crops = tokens.shape[0]
    x = tokens.reshape(crops, CELLS, D).transpose(1, 0, 2)
    cot = cotangent.reshape(crops, CELLS, D).transpose(1, 0, 2)
    lookup = position_lookup()
    highest = lax.Precision.HIGHEST
    bias = jnp.einsum("bkh,kp->bhp", rel_table, lookup, precision=highest) * LOG2E
    bias = bias.reshape(2, GROUPS, 4, KEYS, SLOT).transpose(0, 1, 3, 2, 4)
    bias = jnp.where(jnp.arange(KEYS)[:, None, None] < CELLS, bias, NEG).reshape(2, GROUPS, KEYS, 4 * SLOT)

    cells_of = lambda v: v.reshape(CELL + v.shape[1:])
    rows_of = lambda v: v.reshape((CELLS,) + v.shape[2:])
    x_first, x_last, cot_shifted, qw, pr, o16, mid, u = run_first(
        crop_extent, x, cells_of(cot), norm_gain, norm_bias, qkv_weight, qv_bias, bias, proj_weight, out_bias,
        fc1_weight, fc1_bias, fc2_weight,
    )
    y, dx_first, dx_last, grads_two = run_second(
        crop_extent, crop_counts, x_first, x_last, rows_of(cot_shifted), norm_gain, norm_bias, qkv_weight, qv_bias,
        bias, proj_weight, out_bias, fc1_weight, fc1_bias, fc2_weight,
    )
    dx, sum_one, sum_two, output = run_third(
        x, dx_first, dx_last, cells_of(y), qw, pr, o16, mid, u, norm_gain, norm_bias, qkv_weight, proj_weight,
        fc1_weight, fc2_weight, grads_two,
    )
    fc1, fc2, qkv, proj = finish(sum_one, sum_two)
    rows = jnp.stack([sum_one[SLABS * D :], sum_two[SLABS * D :]]).astype(f32)
    dbias = rows[:, SMALL : SMALL + TABLE, : 4 * SLOT].reshape(2, GROUPS, KEYS, 4, SLOT).transpose(0, 1, 3, 2, 4)
    table = jnp.einsum("hp,kp->kh", dbias.reshape(2 * HEADS, KEYS * SLOT), lookup, precision=highest)
    table = table.reshape(-1, 2, HEADS).transpose(1, 0, 2)
    back = lambda v: v.transpose(1, 0, 2).reshape(tokens.shape)
    return (
        back(rows_of(output)), back(dx), rows[:, 0:2], rows[:, 2:4], qkv, rows[:, 4:6], table, proj, rows[:, 6:8], fc1,
        rows[:, 8:12].reshape(2, FF), fc2,
    )


def solution(mesh):
    split = P("img", "win", None, None)
    return jax.shard_map(
        on_device,
        mesh=mesh,
        in_specs=(split, split, P("img"), P("img", None)) + (P(),) * 10,
        out_specs=(split, split) + (P(),) * 10,
        check_vma=False,
    )
```

```python
import jax
import jax.numpy as jnp
from jax import lax
from jax.experimental import pallas as pl
from jax.experimental.pallas import tpu as pltpu
from jax.sharding import PartitionSpec as P

D = 384
FF = 1536
HEADS = 12
HEAD_DIM = 32
WINDOW = 7
SHIFT = 3
CELLS = WINDOW * WINDOW
SIDE = 2 * WINDOW
HALF = 16
ROWS = CELLS * HALF
LANES = 128
GROUPS = 3
KEYS = 56
SLOT = 64
SLABS = 12
SMALL = 16
TABLE = GROUPS * KEYS
SUMS = SLABS * D + 256
GROUPED = ((0, 1), (2, 3), (4, 5, 6))
NEG = -1e30
LOG2E = 1.4426950408889634
SCALE = HEAD_DIM**-0.5
MESH = pl.DeviceIdType.MESH

bf16 = jnp.bfloat16
f32 = jnp.float32
VMEM = pltpu.VMEM


def mm(a, b):
    return lax.dot_general(a, b, (((1,), (0,)), ((), ())), preferred_element_type=f32)


def mm_bt(a, b):
    return lax.dot_general(a, b, (((1,), (1,)), ((), ())), preferred_element_type=f32)


def mm_at(a, b):
    return lax.dot_general(a, b, (((0,), (0,)), ((), ())), preferred_element_type=f32)


def norm(x):
    centred = x - jnp.mean(x, -1, keepdims=True)
    rstd = lax.rsqrt(jnp.mean(centred * centred, -1, keepdims=True) + 1e-5)
    return centred * rstd, rstd


def norm_back(xh, rstd, dn, gain):
    e = dn * gain
    mean_e = jnp.mean(e, -1, keepdims=True)
    mean_ex = jnp.mean(e * xh, -1, keepdims=True)
    dx = rstd * (e - mean_e - xh * mean_ex)
    return dx, jnp.sum(dn * xh, 0, keepdims=True), jnp.sum(dn, 0, keepdims=True)


def gelu(u):
    phi = 0.5 + 0.5 * lax.erf(u * 0.7071067811865476)
    return u * phi, phi


def gelu_slope(u, phi):
    return phi + u * jnp.exp2(u * u * (-0.5 * LOG2E)) * 0.3989422804014327


def spread(rows):
    head = lax.broadcasted_iota(jnp.int32, rows.shape, 1) // HEAD_DIM
    zero = jnp.zeros_like(rows)
    return jnp.concatenate([jnp.where(head == h, rows, zero) for h in range(4)], 0)


def gather_heads(rows):
    head = lax.broadcasted_iota(jnp.int32, (KEYS, LANES), 1) // HEAD_DIM
    out = rows[:KEYS]
    for h in range(1, 4):
        out = jnp.where(head == h, rows[SLOT * h : SLOT * h + KEYS], out)
    return out


def to_windows(ref, slot, part):
    parted = part.reshape(CELLS, 2, 8, LANES)
    for cg in range(2):
        ref[cg, slot, 0 : CELLS * 8, :] = parted[:, cg].reshape(CELLS * 8, LANES)


def from_windows(ref, slot):
    parts = [ref[cg, slot, 0 : CELLS * 8, :].reshape(CELLS, 1, 8, LANES) for cg in range(2)]
    return jnp.concatenate(parts, 1).reshape(ROWS, LANES)


def cells(shifted):
    win = lax.axis_index("win")
    j = lax.broadcasted_iota(jnp.int32, (KEYS, LANES), 0)
    i = lax.broadcasted_iota(jnp.int32, (KEYS, LANES), 1) % SLOT
    top, left = WINDOW * (win // 2), WINDOW * (win % 2)
    places = [top + j // WINDOW, left + j % WINDOW, top + i // WINDOW, left + i % WINDOW]
    if not shifted:
        return places, None
    region = [(v >= SIDE - WINDOW).astype(jnp.int32) + (v >= SIDE - SHIFT).astype(jnp.int32) for v in places]
    apart = (region[0] != region[2]) | (region[1] != region[3])
    moved = [jnp.where(v + SHIFT >= SIDE, v + SHIFT - SIDE, v + SHIFT) for v in places]
    return moved, jnp.where(apart, NEG, 0.0)


def forward(step, block, shifted, x, refs, keep_n1=None, keep_n2=None, keep_gelu=None, keep_u=None):
    (ext, gain, beta, wqkv, qvb, bias, wp, ob, w1, b1, w2, xs, qw, pr, os, o16, mid) = refs
    xh, _ = norm(x)
    n1 = (xh * gain[block, 0:1, :] + beta[block, 0:1, :]).astype(bf16)
    if keep_n1 is not None:
        keep_n1[step] = n1
    proj = mm(n1, wqkv[...])
    q = (proj[:, :D] + qvb[block, 0:1, :]) * (SCALE * LOG2E)
    k = proj[:, D : 2 * D]
    v = proj[:, 2 * D :] + qvb[block, 1:2, :]
    for g in range(GROUPS):
        cut = slice(LANES * g, LANES * (g + 1))
        to_windows(xs, g, q[:, cut])
        to_windows(xs, GROUPS + g, k[:, cut])
        to_windows(xs, 2 * GROUPS + g, v[:, cut])
    places, apart = cells(shifted)
    if apart is not None:
        apart = jnp.concatenate([apart, apart], 1)

    def windows(part, carry):
        masks = []
        for w in [8 * part + n for n in range(8)]:
            rows, cols = ext[step * HALF + w, 0], ext[step * HALF + w, 1]
            valid_j = (places[0] < rows) & (places[1] < cols)
            valid_i = (places[2] < rows) & (places[3] < cols)
            mask = jnp.where(valid_i == valid_j, 0.0, NEG)
            mask = jnp.concatenate([mask, mask], 1)
            masks.append(mask if apart is None else mask + apart)
        for g in range(GROUPS):
            for n in range(8):
                w = 8 * part + n
                qs, ks, vs = (xs[part, GROUPS * m + g, pl.ds(n, SLOT, stride=8), :].astype(bf16) for m in range(3))
                for m, value in enumerate((qs, ks, vs)):
                    qw[w, GROUPS * m + g] = value
                s = mm_bt(ks[:KEYS], spread(qs)) + bias[g] + masks[n]
                e = jnp.exp2(s - jnp.max(s, 0, keepdims=True))
                p = (e * (1.0 / jnp.sum(e, 0, keepdims=True))).astype(bf16)
                pr[w, g] = p
                os[part, g, pl.ds(n, KEYS, stride=8), :] = gather_heads(mm_at(p, vs[:KEYS]))
        return carry

    lax.fori_loop(0, 2, windows, 0)
    for g in range(GROUPS):
        o16[:, LANES * g : LANES * (g + 1)] = from_windows(os, g).astype(bf16)
    middle = x + (mm(o16[...], wp[...]) + ob[block, 0:1, :])
    mid[...] = middle
    xh2, _ = norm(middle)
    n2 = (xh2 * gain[block, 1:2, :] + beta[block, 1:2, :]).astype(bf16)
    if keep_n2 is not None:
        keep_n2[step] = n2
    y = middle + ob[block, 1:2, :]
    for part in range(3):
        cut = slice(512 * part, 512 * (part + 1))
        u = mm(n2, w1[:, cut]) + b1[block : block + 1, cut]
        if keep_u is not None:
            keep_u[:, cut] = u.astype(bf16)
        z, phi = gelu(u)
        z = z.astype(bf16)
        if keep_gelu is not None:
            keep_gelu[0][step, :, cut] = z
            keep_gelu[1][:, cut] = gelu_slope(u, phi).astype(bf16)
        y = y + mm(z, w2[cut, :])
    return y


def no_tick(point, when=True):
    pass


def mlp_back(step, block, mid, dy, refs, slope, keep_n2=None, beta=None, tick=no_tick):
    (gain, wp, w1, w2, dos, dm_all, du_all, da_all, small) = refs

    def add_small(row, value):
        small[row : row + 1, :] += value

    dm = dy.astype(bf16)
    dm_all[step] = dm
    add_small(7, jnp.sum(dm.astype(f32), 0, keepdims=True))
    sums = []
    for part in range(3):
        cut = slice(512 * part, 512 * (part + 1))
        du = (mm_bt(dm, w2[cut, :]) * slope(cut)).astype(bf16)
        du_all[step, :, cut] = du
        sums.append(jnp.sum(du.astype(f32), 0, keepdims=True))
        tick(part)
    sums = jnp.concatenate(sums, 1)
    for part in range(4):
        add_small(8 + part, sums[:, D * part : D * (part + 1)])
    dn2 = mm_bt(du_all[step], w1[...])
    tick(3)
    xh, rstd = norm(mid)
    if keep_n2 is not None:
        keep_n2[step] = (xh * gain[block, 1:2, :] + beta[block, 1:2, :]).astype(bf16)
    dx, dgain, dbeta = norm_back(xh, rstd, dn2, gain[block, 1:2, :])
    add_small(1, dgain)
    add_small(3, dbeta)
    dmid = dy + dx
    da = dmid.astype(bf16)
    da_all[step] = da
    add_small(6, jnp.sum(da.astype(f32), 0, keepdims=True))
    do = mm_bt(da, wp[...])
    for g in range(GROUPS):
        to_windows(dos, g, do[:, LANES * g : LANES * (g + 1)])
    tick(4)
    return dmid


def attention_back(step, block, x, dmid, refs, keep_n1=None, beta=None, tick=no_tick):
    (gain, wqkv, xs, qw, pr, dos, dp_all, small, dbias) = refs

    def add_small(row, value):
        small[row : row + 1, :] += value

    def windows_back(part, carry):
        units = [(n, g) for n in range(8) for g in range(GROUPS)]
        grad, scores = {}, {}
        for n, g in units:
            grad[n, g] = spread(dos[part, g, pl.ds(n, SLOT, stride=8), :].astype(bf16))
        dprobs = {(n, g): mm_bt(qw[8 * part + n, 2 * GROUPS + g][:KEYS], grad[n, g]) for n, g in units}
        for g in range(GROUPS):
            total = jnp.zeros((KEYS, 4 * SLOT), f32)
            for n in range(8):
                p = pr[8 * part + n, g].astype(f32)
                t = p * dprobs[n, g]
                ds = t - p * jnp.sum(t, 0, keepdims=True)
                total = total + ds
                scores[n, g] = ds.astype(bf16)
            dbias[g] += total
        for n, g in units:
            w, ds = 8 * part + n, scores[n, g]
            dv = mm(pr[w, g], grad[n, g])
            dk = mm(ds, spread(qw[w, g])) * (1.0 / LOG2E)
            dq = gather_heads(mm_at(ds, qw[w, GROUPS + g][:KEYS])) * SCALE
            for m, value in enumerate((dq, dk, dv)):
                xs[part, GROUPS * m + g, pl.ds(n, KEYS, stride=8), :] = value
        for n in range(4):
            tick(n, part == n // 2)
        return carry

    lax.fori_loop(0, 2, windows_back, 0)
    for n in range(3 * GROUPS):
        dp_all[step, :, LANES * n : LANES * (n + 1)] = from_windows(xs, n).astype(bf16)
    dp = dp_all[step, :, : 3 * D]
    add_small(4, jnp.sum(dp[:, :D].astype(f32), 0, keepdims=True))
    add_small(5, jnp.sum(dp[:, 2 * D :].astype(f32), 0, keepdims=True))
    dn1 = mm_bt(dp, wqkv[...])
    tick(4)
    xh, rstd = norm(x)
    if keep_n1 is not None:
        keep_n1[step] = (xh * gain[block, 0:1, :] + beta[block, 0:1, :]).astype(bf16)
    dx, dgain, dbeta = norm_back(xh, rstd, dn1, gain[block, 0:1, :])
    add_small(0, dgain)
    add_small(2, dbeta)
    tick(5)
    return dmid() + dx


def flat(ref, cut=slice(None)):
    return ref[:, :, cut].reshape(2 * ROWS, -1)


def put_slabs(out, first, value):
    for j in range(value.shape[1] // D):
        out[D * (first + j) : D * (first + j + 1), :] = value[:, D * j : D * (j + 1)].astype(bf16)


def fc_grads(n2, z, dm, du, out, tick=no_tick):
    for first, left, right in ((0, n2, du), (4, dm, z)):
        for j in range(2):
            put_slabs(out, first + 2 * j, mm_at(flat(left), flat(right, slice(768 * j, 768 * (j + 1)))))
        tick(first // 4)


def attention_grads(n1, o16, da, dp, out):
    put_slabs(out, 8, mm_at(flat(n1), flat(dp, slice(3 * D))))
    put_slabs(out, 11, mm_at(flat(o16), flat(da)))


def small_grads(small, dbias, out):
    base = SLABS * D
    out[base : base + SMALL, :] = small[...].astype(bf16)
    out[base + SMALL : SUMS, :] = jnp.zeros((SUMS - base - SMALL, D), bf16)
    out[base + SMALL : base + SMALL + TABLE, : 4 * SLOT] = dbias[...].reshape(TABLE, 4 * SLOT).astype(bf16)


KEEP = WINDOW - SHIFT
NEAR, FAR = slice(0, KEEP), slice(KEEP, WINDOW)
HERE, THERE = slice(SHIFT, WINDOW), slice(0, SHIFT)


def shift_peers():
    win = lax.axis_index("win")
    beside = 1 - 2 * (win % 2)
    below = 2 - 4 * (win // 2 % 2)
    return [{"win": win + beside}, {"win": win + below}, {"win": win + beside + below}]


def shift_copies(source, target, send, recv, back=False):
    plain = [(HERE, HERE), (HERE, THERE), (THERE, HERE), (THERE, THERE)]
    moved = [(NEAR, NEAR), (NEAR, FAR), (FAR, NEAR), (FAR, FAR)]
    if back:
        plain, moved = moved, plain
    out = [pltpu.make_async_copy(source.at[plain[0]], target.at[moved[0]], send.at[3])]
    for n, to in enumerate(shift_peers()):
        out.append(
            pltpu.make_async_remote_copy(
                source.at[plain[n + 1]], target.at[moved[n + 1]], send.at[n], recv.at[n], device_id=to, device_id_type=MESH
            )
        )
    return out


def start_all(copies):
    for copy in copies:
        copy.start()


def wait_all(copies):
    for copy in copies:
        copy.wait()


def greet(peers):
    barrier = pltpu.get_barrier_semaphore()
    for to in peers:
        pl.semaphore_signal(barrier, inc=1, device_id=to, device_id_type=MESH)
    pl.semaphore_wait(barrier, len(peers))


def first_kernel(
    ext, x_ref, cot, gain, beta, wqkv, qvb, bias, wp, ob, w1, b1, w2,
    y_shifted, y_last, cot_shifted, qw, pr, o16, mid, u_ref, xs, os, y_first, send, recv,
):
    step = pl.program_id(0)
    cot_copies = shift_copies(cot, cot_shifted, send.at[0], recv.at[0])
    y_copies = shift_copies(y_first, y_shifted, send.at[1], recv.at[1])

    @pl.when(step == 0)
    def _():
        greet(shift_peers())
        start_all(cot_copies)
        xs[...] = jnp.zeros_like(xs)

    x = x_ref[...].reshape(ROWS, D).astype(f32)
    y = forward(
        step, 0, False, x, (ext, gain, beta, wqkv, qvb, bias, wp, ob, w1, b1, w2, xs, qw, pr, os, o16, mid), keep_u=u_ref
    )
    y = y.astype(bf16).reshape(WINDOW, WINDOW, HALF, D)

    @pl.when(step == 0)
    def _():
        y_first[...] = y
        start_all(y_copies)

    @pl.when(step == 1)
    def _():
        y_last[...] = y
        wait_all(y_copies)
        wait_all(cot_copies)


def second_kernel(
    ext, count, x_first, x_last, cot_ref, gain, beta, wqkv, qvb, bias, wp, ob, w1, b1, w2,
    y_ref, dx_shifted, dx_last, grads,
    xs, qw, pr, os, mid, slope, dos, small, dbias, n1, n2, o16, z, dm, du, da, dp, x_both, dx_first, send, recv, local,
):
    step = pl.program_id(0)
    x_copies = shift_copies(x_last, x_both.at[1], send.at[0], recv.at[0])
    dx_copies = shift_copies(dx_first, dx_shifted, send.at[1], recv.at[1], back=True)

    @pl.when(step == 0)
    def _():
        load = pltpu.make_async_copy(x_first, x_both.at[0], local)
        load.start()
        greet(shift_peers())
        start_all(x_copies)
        load.wait()
        xs[...] = jnp.zeros_like(xs)
        dos[...] = jnp.zeros_like(dos)
        small[...] = jnp.zeros_like(small)
        dbias[...] = jnp.zeros_like(dbias)

    @pl.when(step == 1)
    def _():
        wait_all(x_copies)

    x = x_both[step].reshape(ROWS, D).astype(f32)
    live = lax.broadcasted_iota(jnp.int32, (CELLS, HALF, 1), 1) + step * HALF < count[0]
    y = forward(
        step, 1, True, x,
        (ext, gain, beta, wqkv, qvb, bias, wp, ob, w1, b1, w2, xs, qw, pr, os, o16.at[step], mid),
        n1, n2, (z, slope),
    )
    y_ref[...] = jnp.where(live, y.reshape(CELLS, HALF, D), 0.0).astype(bf16)
    dy = jnp.where(live, cot_ref[...].astype(f32), 0.0).reshape(ROWS, D)
    mid[...] = mlp_back(
        step, 1, mid[...], dy, (gain, wp, w1, w2, dos, dm, du, da, small), lambda cut: slope[:, cut].astype(f32)
    )
    dx = attention_back(
        step, 1, x, lambda: mid[...], (gain, wqkv, xs, qw, pr, dos, dp, small, dbias)
    )
    dx = dx.astype(bf16).reshape(WINDOW, WINDOW, HALF, D)

    @pl.when(step == 0)
    def _():
        dx_first[...] = dx
        start_all(dx_copies)

    @pl.when(step == 1)
    def _():
        dx_last[...] = dx
        fc_grads(n2, z, dm, du, grads)
        attention_grads(n1, o16, da, dp, grads)
        small_grads(small, dbias, grads)
        wait_all(dx_copies)


LAST = 24
PACE = {
    (0, 0): (4.2, 6.0, 13.5, 17.1, 21.7, 32.9, 50.5),
    (0, 1): (1.9, 3.9, 9.1, 12.7, 16.3, 31.4, 37.3),
    (0, 2): (2.6, 4.5, 10.1, 13.9, 20.1, 40.0, 52.1),
    (1, 0): (30.7, 33.8, 38.5, 44.6, 47.5, 59.9, 73.1),
    (1, 1): (13.1, 17.1, 29.9, 42.0, 56.9, 72.9, 95.6),
    (1, 2): (29.3, 30.4, 38.3, 39.8, 46.6, 57.1, 68.4),
}


def schedule(*exchanges):
    out = []
    for (which, group), places in PACE.items():
        exchange = exchanges[which]
        if exchange.stages + 1 != len(places):
            first = LAST + 1 if which and group == 2 else places[0]
            places = [first + 4 * k + 0.1 * group for k in range(exchange.stages + 1)]
        out += [(place, exchange, group, k) for k, place in enumerate(places)]
    return sorted(out, key=lambda item: item[0])


def third_kernel(
    x_ref, dy_first, dy_last, y_ref, qw, pr, o_ref, mid, u_ref, gain, beta, wqkv, wp, w1, w2, two_ref,
    dx_ref, one_out, two_out, y_out,
    xs, dos, small, dbias, dmid, n2, o16, z, dm, du, da,
    one, two, land_one, send_one, recv_one, free_one, land_two, send_two, recv_two, free_two, local, loads, dy_both, send, recv,
):
    step = pl.program_id(0)
    first = Exchange(one, land_one, send_one, recv_one, free_one)
    second = Exchange(two, land_two, send_two, recv_two, free_two)
    dy_copies = shift_copies(dy_last, dy_both.at[1], send.at[0], recv.at[0], back=True)
    y_copies = shift_copies(y_ref, y_out, send.at[1], recv.at[1], back=True)
    moves = [[] for _ in range(LAST + 1)]
    late = []
    for place, exchange, group, k in schedule(second, first):
        (moves[int(place)] if place < LAST + 1 else late).append((exchange, group, k))

    def tick(n):
        if n == 14:
            start_all(y_copies)
        for exchange, group, k in moves[n]:
            exchange.advance(GROUPED[group], k)

    def tick_at(steps, base, per_step):
        def ticker(point, when=True):
            for s in steps:
                pl.when((step == s) & when)(lambda s=s: tick(base + (s - steps[0]) * per_step + point))

        return ticker

    def kept(half):
        rows = pl.ds(half * ROWS, ROWS)
        return (
            pltpu.make_async_copy(u_ref.at[rows], z.at[half], loads.at[0, half]),
            pltpu.make_async_copy(o_ref.at[rows], o16.at[half], loads.at[1, half]),
        )

    @pl.when(step == 0)
    def _():
        load = pltpu.make_async_copy(two_ref, two, local.at[0])
        load.start()
        load_dy = pltpu.make_async_copy(dy_first, dy_both.at[0], local.at[1])
        load_dy.start()
        for half in range(2):
            start_all(kept(half))
        greet(second.peers() + shift_peers()[2:])
        start_all(dy_copies)
        xs[...] = jnp.zeros_like(xs)
        dos[...] = jnp.zeros_like(dos)
        small[...] = jnp.zeros_like(small)
        dbias[...] = jnp.zeros_like(dbias)
        load.wait()
        tick(0)
        load_dy.wait()

    for half in range(2):

        @pl.when(step == half)
        def _():
            wait_all(kept(half))
            if half:
                wait_all(dy_copies)

    @pl.when(step < 2)
    def _():
        def slope(cut):
            u = z[step, :, cut].astype(f32)
            value, phi = gelu(u)
            z[step, :, cut] = value.astype(bf16)
            return gelu_slope(u, phi)

        dmid[step] = mlp_back(
            step, 0, mid[...], dy_both[step].astype(f32).reshape(ROWS, D),
            (gain, wp, w1, w2, dos.at[step], dm, du, da, small), slope, n2, beta, tick_at((0, 1), 1, 5),
        )

    @pl.when(step == 1)
    def _():
        fc_grads(n2, z, dm, du, one, lambda point: tick(11 + point))

    @pl.when(step >= 2)
    def _():
        half = step - 2
        dx = attention_back(
            half, 0, x_ref[...].reshape(ROWS, D).astype(f32), lambda: dmid[half],
            (gain, wqkv, xs, qw, pr, dos.at[half], du, small, dbias), n2, beta, tick_at((2, 3), 13, 6),
        )
        dx_ref[...] = dx.astype(bf16).reshape(dx_ref.shape)

    @pl.when(step == 3)
    def _():
        attention_grads(n2, o16, da, du, one)
        small_grads(small, dbias, one)
        for n, (exchange, group, k) in enumerate(late):
            exchange.advance(GROUPED[group], k)
            if all(other is not second for other, _, _ in late[n + 1 :]) and (exchange is second or n == 0):
                store_two = pltpu.make_async_copy(two, two_out, local.at[0])
                store_two.start()
        store_one = pltpu.make_async_copy(one, one_out, local.at[1])
        store_one.start()
        wait_all(y_copies)
        store_one.wait()
        store_two.wait()


def whole(shape):
    return pl.BlockSpec(shape, lambda s: (0,) * len(shape), pipeline_mode=pl.Buffered(1))


def of_block(block, *shape):
    return pl.BlockSpec((None,) + shape, lambda s: (block,) + (0,) * len(shape), pipeline_mode=pl.Buffered(1))


def by_half(*shape, buffers=2):
    return pl.BlockSpec(shape, lambda s: (s,) + (0,) * (len(shape) - 1), pipeline_mode=pl.Buffered(buffers))


ANY_SPEC = pl.BlockSpec(memory_space=pl.ANY)
SMEM_SPEC = pl.BlockSpec(memory_space=pltpu.SMEM)
TOKEN_SPEC = pl.BlockSpec((CELLS, HALF, D), lambda s: (0, s, 0))
XS = VMEM((2, 3 * GROUPS, 8 * SLOT, LANES), f32)
DOS = VMEM((2, GROUPS, 8 * SLOT, LANES), f32)
QW = (HALF, 3 * GROUPS, SLOT, LANES)
PR = (HALF, GROUPS, KEYS, 4 * SLOT)


def params(collective_id=None, mib=61):
    return pltpu.CompilerParams(
        vmem_limit_bytes=mib * 2**20, dimension_semantics=("arbitrary",), collective_id=collective_id,
        has_side_effects=collective_id is not None,
    )


CELL = (WINDOW, WINDOW)
PART = jax.ShapeDtypeStruct(CELL + (HALF, D), bf16)
SHIFTS = [pltpu.SemaphoreType.DMA((2, 4)), pltpu.SemaphoreType.DMA((2, 4))]


def run_first(ext, x, cot, gain, beta, wqkv, qvb, bias, wp, ob, w1, b1, w2):
    crops = x.shape[1]
    return pl.pallas_call(
        first_kernel,
        grid=(2,),
        out_shape=(
            PART,
            PART,
            jax.ShapeDtypeStruct(cot.shape, bf16),
            jax.ShapeDtypeStruct((crops,) + QW[1:], bf16),
            jax.ShapeDtypeStruct((crops,) + PR[1:], bf16),
            jax.ShapeDtypeStruct((2 * ROWS, D), bf16),
            jax.ShapeDtypeStruct((2 * ROWS, D), f32),
            jax.ShapeDtypeStruct((2 * ROWS, FF), bf16),
        ),
        in_specs=[
            SMEM_SPEC, TOKEN_SPEC, ANY_SPEC, whole(gain.shape), whole(beta.shape), of_block(0, D, 3 * D), whole(qvb.shape),
            of_block(0, GROUPS, KEYS, 4 * SLOT), of_block(0, D, D), whole(ob.shape), of_block(0, D, FF),
            whole(b1.shape), of_block(0, FF, D),
        ],
        out_specs=(
            ANY_SPEC, whole(PART.shape), ANY_SPEC, by_half(*QW), by_half(*PR), by_half(ROWS, D), by_half(ROWS, D),
            by_half(ROWS, FF),
        ),
        scratch_shapes=[
            XS, VMEM((2, GROUPS, 8 * KEYS, LANES), f32), VMEM(PART.shape, bf16),
        ] + SHIFTS,
        compiler_params=params(1),
        name="first_forward",
    )(ext, x, cot, gain, beta, wqkv, qvb, bias, wp, ob, w1, b1, w2)


GRADS = jax.ShapeDtypeStruct((SUMS, D), bf16)
SMALLS = [VMEM((SMALL, D), f32), VMEM((GROUPS, KEYS, 4 * SLOT), f32)]


def run_second(ext, count, x_first, x_last, cot, gain, beta, wqkv, qvb, bias, wp, ob, w1, b1, w2):
    return pl.pallas_call(
        second_kernel,
        grid=(2,),
        out_shape=(jax.ShapeDtypeStruct(cot.shape, bf16), PART, PART, GRADS),
        in_specs=[
            SMEM_SPEC, SMEM_SPEC, ANY_SPEC, ANY_SPEC, TOKEN_SPEC, whole(gain.shape), whole(beta.shape), of_block(1, D, 3 * D),
            whole(qvb.shape), of_block(1, GROUPS, KEYS, 4 * SLOT), of_block(1, D, D), whole(ob.shape),
            of_block(1, D, FF), whole(b1.shape), of_block(1, FF, D),
        ],
        out_specs=(TOKEN_SPEC, ANY_SPEC, whole(PART.shape), whole(GRADS.shape)),
        scratch_shapes=[
            XS, VMEM(QW, bf16), VMEM(PR, bf16), VMEM((2, GROUPS, 8 * KEYS, LANES), f32),
            VMEM((ROWS, D), f32), VMEM((ROWS, FF), bf16), DOS,
        ] + SMALLS + [VMEM((2, ROWS, width), bf16) for width in (D, D, D, FF, D, FF, D, 3 * D)]
        + [VMEM((2,) + PART.shape, bf16), VMEM(PART.shape, bf16)] + SHIFTS + [pltpu.SemaphoreType.DMA(())],
        compiler_params=params(2, 63),
        name="second_block",
    )(ext, count, x_first, x_last, cot, gain, beta, wqkv, qvb, bias, wp, ob, w1, b1, w2)


def in_steps(first, *shape, axis=0, buffers=2):
    def index(s):
        return tuple(jnp.clip(s - first, 0, 1) if n == axis else 0 for n in range(len(shape)))

    return pl.BlockSpec(shape, index, pipeline_mode=pl.Buffered(buffers))


def run_third(x, dy_first, dy_last, y, qw, pr, o16, mid, u, gain, beta, wqkv, wp, w1, w2, two):
    tokens = (CELLS, HALF, D)
    return pl.pallas_call(
        third_kernel,
        grid=(4,),
        out_shape=(jax.ShapeDtypeStruct(x.shape, bf16), GRADS, GRADS, jax.ShapeDtypeStruct(y.shape, bf16)),
        in_specs=[
            in_steps(2, *tokens, axis=1), ANY_SPEC, ANY_SPEC, ANY_SPEC, in_steps(2, *QW, buffers=1),
            in_steps(2, *PR, buffers=1), ANY_SPEC, in_steps(0, ROWS, D), ANY_SPEC,
            whole(gain.shape), whole(beta.shape), of_block(0, D, 3 * D), of_block(0, D, D), of_block(0, D, FF),
            of_block(0, FF, D), ANY_SPEC,
        ],
        out_specs=(in_steps(2, *tokens, axis=1), ANY_SPEC, ANY_SPEC, ANY_SPEC),
        scratch_shapes=[XS, VMEM((2,) + DOS.shape, f32)] + SMALLS + [VMEM((2, ROWS, D), f32)]
        + [VMEM((2, ROWS, width), bf16) for width in (D, D, FF, D, FF, D)]
        + [VMEM(GRADS.shape, bf16)] * 2 + exchange_scratch() * 2
        + [pltpu.SemaphoreType.DMA((2,)), pltpu.SemaphoreType.DMA((2, 2)), VMEM((2,) + PART.shape, bf16)] + SHIFTS,
        compiler_params=params(0, 63),
        name="first_backward",
    )(x, dy_first, dy_last, y, qw, pr, o16, mid, u, gain, beta, wqkv, wp, w1, w2, two)


def jobs():
    n_img, n_win = lax.axis_size("img"), lax.axis_size("win")
    bits = [("win", b) for b in range(1, n_win.bit_length() - 1)] + [("img", b) for b in range(n_img.bit_length() - 1)]
    pairs = [bits[n : n + 2] for n in range(0, len(bits), 2)]
    orders = [[[("win", 0)]] + pairs, [[("win", 0)]] + pairs[::-1]]
    out = []
    for group in range(3):
        out += [(1536 * group, 1024, orders[0]), (1536 * group + 1024, 512, orders[1])]
    return out + [(SLABS * D, SUMS - SLABS * D, orders[0])]


def plan_sizes(size, order):
    out = []
    for group in order:
        ways = 2 ** len(group)
        cut = ways if size % (16 * ways) == 0 else 1
        size //= cut
        out.append((ways, cut, size))
    return out


class Exchange:
    def __init__(self, buf, landing, send, recv, free):
        self.buf, self.landing, self.send, self.recv, self.free = buf, landing, send, recv, free
        index = {axis: lax.axis_index(axis) for axis in ("img", "win")}
        self.plans, land = [], 0
        for start, rows, order in jobs():
            plan = []
            for group, (ways, cut, size) in zip(order, plan_sizes(rows, order)):
                own = [(index[axis] // 2**bit) % 2 for axis, bit in group]
                peers = []
                for apart in range(1, ways):
                    to, piece = {}, 0
                    for n, (axis, bit) in enumerate(group):
                        here = own[n]
                        if apart >> n & 1:
                            to[axis] = to.get(axis, index[axis]) + 2**bit - 2 ** (bit + 1) * here
                            here = 1 - here
                        piece = piece + here * 2**n
                    peers.append((to, start + piece * size if cut > 1 else start, land))
                    land += size
                if cut > 1:
                    start = start + sum(here * 2**n for n, here in enumerate(own)) * size
                plan.append((start, size, cut, peers))
            self.plans.append(plan)
        self.bits = len(self.plans[0])
        self.stages = 2 * self.bits

    def peers(self):
        return [to for *_, peers in self.plans[0] for to, _, _ in peers]

    def copies(self, c, k):
        n = min(k, self.stages - 1 - k)
        keep, size, cut, peers = self.plans[c][n]
        if k >= self.bits and cut == 1:
            return []
        out = []
        for p, (to, give, land) in enumerate(peers):
            if k < self.bits:
                source, target = self.buf.at[pl.ds(pl.multiple_of(give, 16), size)], self.landing.at[pl.ds(land, size)]
            else:
                source = target = self.buf.at[pl.ds(pl.multiple_of(keep, 16), size)]
            out.append(
                pltpu.make_async_remote_copy(
                    source, target, self.send.at[c, k, p], self.recv.at[c, k, p], device_id=to, device_id_type=MESH
                )
            )
        return out

    def start(self, c, k):
        copies = self.copies(c, k)
        if copies and k >= self.bits:
            pl.semaphore_wait(self.free.at[c, self.stages - 1 - k], len(copies))
        for copy in copies:
            copy.start()

    def finish(self, c, k):
        for copy in self.copies(c, k):
            copy.wait()
        if k >= self.bits:
            return
        keep, size, cut, peers = self.plans[c][k]
        if cut > 1:
            for to, _, _ in peers:
                pl.semaphore_signal(self.free.at[c, k], inc=1, device_id=to, device_id_type=MESH)
        tile = max(t for t in (16, 32, 48, 64) if size % t == 0)

        def add(i, carry):
            here = pl.ds(pl.multiple_of(keep + i * tile, 16), tile)
            total = self.buf[here, :].astype(f32)
            for _, _, land in peers:
                total = total + self.landing[pl.ds(pl.multiple_of(land + i * tile, 16), tile), :].astype(f32)
            self.buf[here, :] = total.astype(bf16)
            return carry

        lax.fori_loop(0, size // tile, add, 0)

    def advance(self, which, k):
        for c in which:
            if 1 <= k <= self.stages:
                self.finish(c, k - 1)
            if k < self.stages:
                self.start(c, k)


def exchange_scratch():
    landing, most = 0, 0
    for _, rows, order in jobs():
        for ways, _, size in plan_sizes(rows, order):
            landing += size * (ways - 1)
            most = max(most, ways - 1)
    n, bits = len(jobs()), len(jobs()[0][2])
    dma = pltpu.SemaphoreType.DMA((n, 2 * bits, most))
    return [VMEM((landing, D), bf16), dma, dma, pltpu.SemaphoreType.REGULAR((n, bits))]


def finish_kernel(*refs):
    ins, outs = refs[:8], refs[8:]
    for n, out in enumerate(outs):
        for block in range(2):
            value = ins[2 * n + block][...].astype(f32)
            out[block] = value.T if n == 1 else value


def finish(grads_one, grads_two):
    slabs = [lambda j: (j, 0), lambda j: (4 + j, 0), lambda j: (8 + jnp.minimum(j, 2), 0), lambda j: (11, 0)]
    targets = [lambda j: (0, 0, j), lambda j: (0, j, 0), lambda j: (0, 0, jnp.minimum(j, 2)), lambda j: (0, 0, 0)]
    return pl.pallas_call(
        finish_kernel,
        grid=(4,),
        out_shape=tuple(jax.ShapeDtypeStruct((2,) + s, f32) for s in ((D, FF), (FF, D), (D, 3 * D), (D, D))),
        in_specs=[pl.BlockSpec((D, D), index) for index in slabs for _ in range(2)],
        out_specs=tuple(pl.BlockSpec((2, D, D), index) for index in targets),
        compiler_params=params(),
        name="finish_gradients",
    )(*[grads_one, grads_two] * 4)


def position_lookup():
    j = jnp.arange(KEYS)[:, None]
    i = jnp.arange(SLOT)[None, :]
    side = SIDE - 1
    index = (i // WINDOW - j // WINDOW + WINDOW - 1) * side + i % WINDOW - j % WINDOW + WINDOW - 1
    index = jnp.where((i < CELLS) & (j < CELLS), index, -1).reshape(-1)
    return (jnp.arange(side * side)[:, None] == index[None, :]).astype(f32)


def on_device(
    tokens, cotangent, crop_counts, crop_extent, norm_gain, norm_bias, qkv_weight, qv_bias, rel_table, proj_weight,
    out_bias, fc1_weight, fc1_bias, fc2_weight,
):
    crops = tokens.shape[0]
    x = tokens.reshape(crops, CELLS, D).transpose(1, 0, 2)
    cot = cotangent.reshape(crops, CELLS, D).transpose(1, 0, 2)
    lookup = position_lookup()
    highest = lax.Precision.HIGHEST
    bias = jnp.einsum("bkh,kp->bhp", rel_table, lookup, precision=highest) * LOG2E
    bias = bias.reshape(2, GROUPS, 4, KEYS, SLOT).transpose(0, 1, 3, 2, 4)
    bias = jnp.where(jnp.arange(KEYS)[:, None, None] < CELLS, bias, NEG).reshape(2, GROUPS, KEYS, 4 * SLOT)

    cells_of = lambda v: v.reshape(CELL + v.shape[1:])
    rows_of = lambda v: v.reshape((CELLS,) + v.shape[2:])
    x_first, x_last, cot_shifted, qw, pr, o16, mid, u = run_first(
        crop_extent, x, cells_of(cot), norm_gain, norm_bias, qkv_weight, qv_bias, bias, proj_weight, out_bias,
        fc1_weight, fc1_bias, fc2_weight,
    )
    y, dx_first, dx_last, grads_two = run_second(
        crop_extent, crop_counts, x_first, x_last, rows_of(cot_shifted), norm_gain, norm_bias, qkv_weight, qv_bias,
        bias, proj_weight, out_bias, fc1_weight, fc1_bias, fc2_weight,
    )
    dx, sum_one, sum_two, output = run_third(
        x, dx_first, dx_last, cells_of(y), qw, pr, o16, mid, u, norm_gain, norm_bias, qkv_weight, proj_weight,
        fc1_weight, fc2_weight, grads_two,
    )
    fc1, fc2, qkv, proj = finish(sum_one, sum_two)
    rows = jnp.stack([sum_one[SLABS * D :], sum_two[SLABS * D :]]).astype(f32)
    dbias = rows[:, SMALL : SMALL + TABLE, : 4 * SLOT].reshape(2, GROUPS, KEYS, 4, SLOT).transpose(0, 1, 3, 2, 4)
    table = jnp.einsum("hp,kp->kh", dbias.reshape(2 * HEADS, KEYS * SLOT), lookup, precision=highest)
    table = table.reshape(-1, 2, HEADS).transpose(1, 0, 2)
    back = lambda v: v.transpose(1, 0, 2).reshape(tokens.shape)
    return (
        back(rows_of(output)), back(dx), rows[:, 0:2], rows[:, 2:4], qkv, rows[:, 4:6], table, proj, rows[:, 6:8], fc1,
        rows[:, 8:12].reshape(2, FF), fc2,
    )


def solution(mesh):
    split = P("img", "win", None, None)
    return jax.shard_map(
        on_device,
        mesh=mesh,
        in_specs=(split, split, P("img"), P("img", None)) + (P(),) * 10,
        out_specs=(split, split) + (P(),) * 10,
        check_vma=False,
    )
```

```python
import jax
import jax.numpy as jnp
from jax import lax
from jax.experimental import pallas as pl
from jax.experimental.pallas import tpu as pltpu
from jax.sharding import PartitionSpec as P

D = 384
FF = 1536
HEADS = 12
HEAD_DIM = 32
WINDOW = 7
SHIFT = 3
CELLS = WINDOW * WINDOW
SIDE = 2 * WINDOW
HALF = 16
ROWS = CELLS * HALF
LANES = 128
GROUPS = 3
KEYS = 56
SLOT = 64
SLABS = 12
SMALL = 16
TABLE = GROUPS * KEYS
SUMS = SLABS * D + 256
GROUPED = ((0, 1), (2, 3), (4, 5, 6))
NEG = -1e30
LOG2E = 1.4426950408889634
SCALE = HEAD_DIM**-0.5
MESH = pl.DeviceIdType.MESH

bf16 = jnp.bfloat16
f32 = jnp.float32
VMEM = pltpu.VMEM


def mm(a, b):
    return lax.dot_general(a, b, (((1,), (0,)), ((), ())), preferred_element_type=f32)


def mm_bt(a, b):
    return lax.dot_general(a, b, (((1,), (1,)), ((), ())), preferred_element_type=f32)


def mm_at(a, b):
    return lax.dot_general(a, b, (((0,), (0,)), ((), ())), preferred_element_type=f32)


def norm(x):
    centred = x - jnp.mean(x, -1, keepdims=True)
    rstd = lax.rsqrt(jnp.mean(centred * centred, -1, keepdims=True) + 1e-5)
    return centred * rstd, rstd


def norm_back(xh, rstd, dn, gain):
    e = dn * gain
    mean_e = jnp.mean(e, -1, keepdims=True)
    mean_ex = jnp.mean(e * xh, -1, keepdims=True)
    dx = rstd * (e - mean_e - xh * mean_ex)
    return dx, jnp.sum(dn * xh, 0, keepdims=True), jnp.sum(dn, 0, keepdims=True)


def gelu(u):
    phi = 0.5 + 0.5 * lax.erf(u * 0.7071067811865476)
    return u * phi, phi


def gelu_slope(u, phi):
    return phi + u * jnp.exp2(u * u * (-0.5 * LOG2E)) * 0.3989422804014327


def spread(rows):
    head = lax.broadcasted_iota(jnp.int32, rows.shape, 1) // HEAD_DIM
    zero = jnp.zeros_like(rows)
    return jnp.concatenate([jnp.where(head == h, rows, zero) for h in range(4)], 0)


def gather_heads(rows):
    head = lax.broadcasted_iota(jnp.int32, (KEYS, LANES), 1) // HEAD_DIM
    out = rows[:KEYS]
    for h in range(1, 4):
        out = jnp.where(head == h, rows[SLOT * h : SLOT * h + KEYS], out)
    return out


def to_windows(ref, slot, part):
    parted = part.reshape(CELLS, 2, 8, LANES)
    for cg in range(2):
        ref[cg, slot, 0 : CELLS * 8, :] = parted[:, cg].reshape(CELLS * 8, LANES)


def from_windows(ref, slot):
    parts = [ref[cg, slot, 0 : CELLS * 8, :].reshape(CELLS, 1, 8, LANES) for cg in range(2)]
    return jnp.concatenate(parts, 1).reshape(ROWS, LANES)


def cells(shifted):
    win = lax.axis_index("win")
    j = lax.broadcasted_iota(jnp.int32, (KEYS, LANES), 0)
    i = lax.broadcasted_iota(jnp.int32, (KEYS, LANES), 1) % SLOT
    top, left = WINDOW * (win // 2), WINDOW * (win % 2)
    places = [top + j // WINDOW, left + j % WINDOW, top + i // WINDOW, left + i % WINDOW]
    if not shifted:
        return places, None
    region = [(v >= SIDE - WINDOW).astype(jnp.int32) + (v >= SIDE - SHIFT).astype(jnp.int32) for v in places]
    apart = (region[0] != region[2]) | (region[1] != region[3])
    moved = [jnp.where(v + SHIFT >= SIDE, v + SHIFT - SIDE, v + SHIFT) for v in places]
    return moved, jnp.where(apart, NEG, 0.0)


def forward(step, block, shifted, x, refs, keep_n1=None, keep_n2=None, keep_gelu=None, keep_u=None):
    (ext, gain, beta, wqkv, qvb, bias, wp, ob, w1, b1, w2, xs, qw, pr, os, o16, mid) = refs
    xh, _ = norm(x)
    n1 = (xh * gain[block, 0:1, :] + beta[block, 0:1, :]).astype(bf16)
    if keep_n1 is not None:
        keep_n1[step] = n1
    proj = mm(n1, wqkv[...])
    q = (proj[:, :D] + qvb[block, 0:1, :]) * (SCALE * LOG2E)
    k = proj[:, D : 2 * D]
    v = proj[:, 2 * D :] + qvb[block, 1:2, :]
    for g in range(GROUPS):
        cut = slice(LANES * g, LANES * (g + 1))
        to_windows(xs, g, q[:, cut])
        to_windows(xs, GROUPS + g, k[:, cut])
        to_windows(xs, 2 * GROUPS + g, v[:, cut])
    places, apart = cells(shifted)
    if apart is not None:
        apart = jnp.concatenate([apart, apart], 1)

    def windows(part, carry):
        masks = []
        for w in [8 * part + n for n in range(8)]:
            rows, cols = ext[0, step * HALF + w], ext[1, step * HALF + w]
            valid_j = (places[0] < rows) & (places[1] < cols)
            valid_i = (places[2] < rows) & (places[3] < cols)
            mask = jnp.where(valid_i == valid_j, 0.0, NEG)
            mask = jnp.concatenate([mask, mask], 1)
            masks.append(mask if apart is None else mask + apart)
        for g in range(GROUPS):
            for n in range(8):
                w = 8 * part + n
                qs, ks, vs = (xs[part, GROUPS * m + g, pl.ds(n, SLOT, stride=8), :].astype(bf16) for m in range(3))
                for m, value in enumerate((qs, ks, vs)):
                    qw[w, GROUPS * m + g] = value
                s = mm_bt(ks[:KEYS], spread(qs)) + bias[g] + masks[n]
                e = jnp.exp2(s - jnp.max(s, 0, keepdims=True))
                p = (e * (1.0 / jnp.sum(e, 0, keepdims=True))).astype(bf16)
                pr[w, g] = p
                os[part, g, pl.ds(n, KEYS, stride=8), :] = gather_heads(mm_at(p, vs[:KEYS]))
        return carry

    lax.fori_loop(0, 2, windows, 0)
    for g in range(GROUPS):
        o16[:, LANES * g : LANES * (g + 1)] = from_windows(os, g).astype(bf16)
    middle = x + (mm(o16[...], wp[...]) + ob[block, 0:1, :])
    mid[...] = middle
    xh2, _ = norm(middle)
    n2 = (xh2 * gain[block, 1:2, :] + beta[block, 1:2, :]).astype(bf16)
    if keep_n2 is not None:
        keep_n2[step] = n2
    y = middle + ob[block, 1:2, :]
    for part in range(3):
        cut = slice(512 * part, 512 * (part + 1))
        u = mm(n2, w1[:, cut]) + b1[block : block + 1, cut]
        if keep_u is not None:
            keep_u[:, cut] = u.astype(bf16)
        z, phi = gelu(u)
        z = z.astype(bf16)
        if keep_gelu is not None:
            keep_gelu[0][step, :, cut] = z
            keep_gelu[1][:, cut] = gelu_slope(u, phi).astype(bf16)
        y = y + mm(z, w2[cut, :])
    return y


def no_tick(point, when=True):
    pass


def mlp_back(step, block, mid, dy, refs, slope, keep_n2=None, beta=None, tick=no_tick):
    (gain, wp, w1, w2, dos, dm_all, du_all, da_all, small) = refs

    def add_small(row, value):
        small[row : row + 1, :] += value

    dm = dy.astype(bf16)
    dm_all[step] = dm
    add_small(7, jnp.sum(dm.astype(f32), 0, keepdims=True))
    sums = []
    for part in range(3):
        cut = slice(512 * part, 512 * (part + 1))
        du = (mm_bt(dm, w2[cut, :]) * slope(cut)).astype(bf16)
        du_all[step, :, cut] = du
        sums.append(jnp.sum(du.astype(f32), 0, keepdims=True))
        tick(part)
    sums = jnp.concatenate(sums, 1)
    for part in range(4):
        add_small(8 + part, sums[:, D * part : D * (part + 1)])
    dn2 = mm_bt(du_all[step], w1[...])
    tick(3)
    xh, rstd = norm(mid)
    if keep_n2 is not None:
        keep_n2[step] = (xh * gain[block, 1:2, :] + beta[block, 1:2, :]).astype(bf16)
    dx, dgain, dbeta = norm_back(xh, rstd, dn2, gain[block, 1:2, :])
    add_small(1, dgain)
    add_small(3, dbeta)
    dmid = dy + dx
    da = dmid.astype(bf16)
    da_all[step] = da
    add_small(6, jnp.sum(da.astype(f32), 0, keepdims=True))
    do = mm_bt(da, wp[...])
    for g in range(GROUPS):
        to_windows(dos, g, do[:, LANES * g : LANES * (g + 1)])
    tick(4)
    return dmid


def attention_back(step, block, x, dmid, refs, keep_n1=None, beta=None, tick=no_tick):
    (gain, wqkv, xs, qw, pr, dos, dp_all, small, dbias) = refs

    def add_small(row, value):
        small[row : row + 1, :] += value

    def windows_back(part, carry):
        units = [(n, g) for n in range(8) for g in range(GROUPS)]
        grad, scores = {}, {}
        for n, g in units:
            grad[n, g] = spread(dos[part, g, pl.ds(n, SLOT, stride=8), :].astype(bf16))
        dprobs = {(n, g): mm_bt(qw[8 * part + n, 2 * GROUPS + g][:KEYS], grad[n, g]) for n, g in units}
        for g in range(GROUPS):
            total = jnp.zeros((KEYS, 4 * SLOT), f32)
            for n in range(8):
                p = pr[8 * part + n, g].astype(f32)
                t = p * dprobs[n, g]
                ds = t - p * jnp.sum(t, 0, keepdims=True)
                total = total + ds
                scores[n, g] = ds.astype(bf16)
            dbias[g] += total
        for n, g in units:
            w, ds = 8 * part + n, scores[n, g]
            dv = mm(pr[w, g], grad[n, g])
            dk = mm(ds, spread(qw[w, g])) * (1.0 / LOG2E)
            dq = gather_heads(mm_at(ds, qw[w, GROUPS + g][:KEYS])) * SCALE
            for m, value in enumerate((dq, dk, dv)):
                xs[part, GROUPS * m + g, pl.ds(n, KEYS, stride=8), :] = value
        for n in range(4):
            tick(n, part == n // 2)
        return carry

    lax.fori_loop(0, 2, windows_back, 0)
    for n in range(3 * GROUPS):
        dp_all[step, :, LANES * n : LANES * (n + 1)] = from_windows(xs, n).astype(bf16)
    dp = dp_all[step, :, : 3 * D]
    add_small(4, jnp.sum(dp[:, :D].astype(f32), 0, keepdims=True))
    add_small(5, jnp.sum(dp[:, 2 * D :].astype(f32), 0, keepdims=True))
    dn1 = mm_bt(dp, wqkv[...])
    tick(4)
    xh, rstd = norm(x)
    if keep_n1 is not None:
        keep_n1[step] = (xh * gain[block, 0:1, :] + beta[block, 0:1, :]).astype(bf16)
    dx, dgain, dbeta = norm_back(xh, rstd, dn1, gain[block, 0:1, :])
    add_small(0, dgain)
    add_small(2, dbeta)
    tick(5)
    return dmid() + dx


def flat(ref, cut=slice(None)):
    return ref[:, :, cut].reshape(2 * ROWS, -1)


def put_slabs(out, first, value):
    for j in range(value.shape[1] // D):
        out[D * (first + j) : D * (first + j + 1), :] = value[:, D * j : D * (j + 1)].astype(bf16)


def fc_grads(n2, z, dm, du, out, tick=no_tick):
    for first, left, right in ((0, n2, du), (4, dm, z)):
        for j in range(2):
            put_slabs(out, first + 2 * j, mm_at(flat(left), flat(right, slice(768 * j, 768 * (j + 1)))))
        tick(first // 4)


def attention_grads(n1, o16, da, dp, out):
    put_slabs(out, 8, mm_at(flat(n1), flat(dp, slice(3 * D))))
    put_slabs(out, 11, mm_at(flat(o16), flat(da)))


def small_grads(small, dbias, out):
    base = SLABS * D
    out[base : base + SMALL, :] = small[...].astype(bf16)
    out[base + SMALL : SUMS, :] = jnp.zeros((SUMS - base - SMALL, D), bf16)
    out[base + SMALL : base + SMALL + TABLE, : 4 * SLOT] = dbias[...].reshape(TABLE, 4 * SLOT).astype(bf16)


KEEP = WINDOW - SHIFT
NEAR, FAR = slice(0, KEEP), slice(KEEP, WINDOW)
HERE, THERE = slice(SHIFT, WINDOW), slice(0, SHIFT)


def shift_peers():
    win = lax.axis_index("win")
    beside = 1 - 2 * (win % 2)
    below = 2 - 4 * (win // 2 % 2)
    return [{"win": win + beside}, {"win": win + below}, {"win": win + beside + below}]


def shift_copies(source, target, send, recv, back=False):
    plain = [(HERE, HERE), (HERE, THERE), (THERE, HERE), (THERE, THERE)]
    moved = [(NEAR, NEAR), (NEAR, FAR), (FAR, NEAR), (FAR, FAR)]
    if back:
        plain, moved = moved, plain
    out = [pltpu.make_async_copy(source.at[plain[0]], target.at[moved[0]], send.at[3])]
    for n, to in enumerate(shift_peers()):
        out.append(
            pltpu.make_async_remote_copy(
                source.at[plain[n + 1]], target.at[moved[n + 1]], send.at[n], recv.at[n], device_id=to, device_id_type=MESH
            )
        )
    return out


def start_all(copies):
    for copy in copies:
        copy.start()


def wait_all(copies):
    for copy in copies:
        copy.wait()


def greet(peers):
    barrier = pltpu.get_barrier_semaphore()
    for to in peers:
        pl.semaphore_signal(barrier, inc=1, device_id=to, device_id_type=MESH)
    pl.semaphore_wait(barrier, len(peers))


def first_kernel(
    ext, x_ref, cot, gain, beta, wqkv, qvb, bias, wp, ob, w1, b1, w2,
    y_shifted, y_last, cot_shifted, qw, pr, o16, mid, u_ref, xs, os, y_first, send, recv,
):
    step = pl.program_id(0)
    cot_copies = shift_copies(cot, cot_shifted, send.at[0], recv.at[0])
    y_copies = shift_copies(y_first, y_shifted, send.at[1], recv.at[1])

    @pl.when(step == 0)
    def _():
        greet(shift_peers())
        start_all(cot_copies)
        xs[...] = jnp.zeros_like(xs)

    x = x_ref[...].reshape(ROWS, D).astype(f32)
    y = forward(
        step, 0, False, x, (ext, gain, beta, wqkv, qvb, bias, wp, ob, w1, b1, w2, xs, qw, pr, os, o16, mid), keep_u=u_ref
    )
    y = y.astype(bf16).reshape(WINDOW, WINDOW, HALF, D)

    @pl.when(step == 0)
    def _():
        y_first[...] = y
        start_all(y_copies)

    @pl.when(step == 1)
    def _():
        y_last[...] = y
        wait_all(y_copies)
        wait_all(cot_copies)


def second_kernel(
    ext, count, x_first, x_last, cot_ref, gain, beta, wqkv, qvb, bias, wp, ob, w1, b1, w2,
    y_ref, dx_shifted, dx_last, grads,
    xs, qw, pr, os, mid, slope, dos, small, dbias, n1, n2, o16, z, dm, du, da, dp, x_both, dx_first, send, recv, local,
):
    step = pl.program_id(0)
    x_copies = shift_copies(x_last, x_both.at[1], send.at[0], recv.at[0])
    dx_copies = shift_copies(dx_first, dx_shifted, send.at[1], recv.at[1], back=True)

    @pl.when(step == 0)
    def _():
        load = pltpu.make_async_copy(x_first, x_both.at[0], local)
        load.start()
        greet(shift_peers())
        start_all(x_copies)
        load.wait()
        xs[...] = jnp.zeros_like(xs)
        dos[...] = jnp.zeros_like(dos)
        small[...] = jnp.zeros_like(small)
        dbias[...] = jnp.zeros_like(dbias)

    @pl.when(step == 1)
    def _():
        wait_all(x_copies)

    x = x_both[step].reshape(ROWS, D).astype(f32)
    live = lax.broadcasted_iota(jnp.int32, (CELLS, HALF, 1), 1) + step * HALF < count[0]
    y = forward(
        step, 1, True, x,
        (ext, gain, beta, wqkv, qvb, bias, wp, ob, w1, b1, w2, xs, qw, pr, os, o16.at[step], mid),
        n1, n2, (z, slope),
    )
    y_ref[...] = jnp.where(live, y.reshape(CELLS, HALF, D), 0.0).astype(bf16)
    dy = jnp.where(live, cot_ref[...].astype(f32), 0.0).reshape(ROWS, D)
    mid[...] = mlp_back(
        step, 1, mid[...], dy, (gain, wp, w1, w2, dos, dm, du, da, small), lambda cut: slope[:, cut].astype(f32)
    )
    dx = attention_back(
        step, 1, x, lambda: mid[...], (gain, wqkv, xs, qw, pr, dos, dp, small, dbias)
    )
    dx = dx.astype(bf16).reshape(WINDOW, WINDOW, HALF, D)

    @pl.when(step == 0)
    def _():
        dx_first[...] = dx
        start_all(dx_copies)

    @pl.when(step == 1)
    def _():
        dx_last[...] = dx
        fc_grads(n2, z, dm, du, grads)
        attention_grads(n1, o16, da, dp, grads)
        small_grads(small, dbias, grads)
        wait_all(dx_copies)


LAST = 24
PACE = {
    (0, 0): (4.2, 6.0, 13.5, 17.1, 21.7, 32.9, 50.5),
    (0, 1): (1.9, 3.9, 9.1, 12.7, 16.3, 31.4, 37.3),
    (0, 2): (2.6, 4.5, 10.1, 13.9, 20.1, 40.0, 52.1),
    (1, 0): (30.7, 33.8, 38.5, 44.6, 47.5, 59.9, 73.1),
    (1, 1): (13.1, 17.1, 29.9, 42.0, 56.9, 72.9, 95.6),
    (1, 2): (29.3, 30.4, 38.3, 39.8, 46.6, 57.1, 68.4),
}


def schedule(*exchanges):
    out = []
    for (which, group), places in PACE.items():
        exchange = exchanges[which]
        if exchange.stages + 1 != len(places):
            first = LAST + 1 if which and group == 2 else places[0]
            places = [first + 4 * k + 0.1 * group for k in range(exchange.stages + 1)]
        out += [(place, exchange, group, k) for k, place in enumerate(places)]
    return sorted(out, key=lambda item: item[0])


def third_kernel(
    x_ref, dy_first, dy_last, y_ref, qw, pr, o_ref, mid, u_ref, gain, beta, wqkv, wp, w1, w2, two_ref,
    dx_ref, one_out, two_out, y_out, small_out,
    xs, dos, small, dbias, dmid, n2, o16, z, dm, du, da,
    one, two, land_one, send_one, recv_one, free_one, land_two, send_two, recv_two, free_two, local, loads, dy_both, send, recv,
):
    step = pl.program_id(0)
    first = Exchange(one, land_one, send_one, recv_one, free_one)
    second = Exchange(two, land_two, send_two, recv_two, free_two)
    dy_copies = shift_copies(dy_last, dy_both.at[1], send.at[0], recv.at[0], back=True)
    y_copies = shift_copies(y_ref, y_out, send.at[1], recv.at[1], back=True)
    moves = [[] for _ in range(LAST + 1)]
    late = []
    for place, exchange, group, k in schedule(second, first):
        (moves[int(place)] if place < LAST + 1 else late).append((exchange, group, k))

    def tick(n):
        if n == 14:
            start_all(y_copies)
        for exchange, group, k in moves[n]:
            exchange.advance(GROUPED[group], k)

    def tick_at(steps, base, per_step):
        def ticker(point, when=True):
            for s in steps:
                pl.when((step == s) & when)(lambda s=s: tick(base + (s - steps[0]) * per_step + point))

        return ticker

    def kept(half):
        rows = pl.ds(half * ROWS, ROWS)
        return (
            pltpu.make_async_copy(u_ref.at[rows], z.at[half], loads.at[0, half]),
            pltpu.make_async_copy(o_ref.at[rows], o16.at[half], loads.at[1, half]),
        )

    @pl.when(step == 0)
    def _():
        load = pltpu.make_async_copy(two_ref, two, local.at[0])
        load.start()
        load_dy = pltpu.make_async_copy(dy_first, dy_both.at[0], local.at[1])
        load_dy.start()
        for half in range(2):
            start_all(kept(half))
        greet(second.peers() + shift_peers()[2:])
        start_all(dy_copies)
        xs[...] = jnp.zeros_like(xs)
        dos[...] = jnp.zeros_like(dos)
        small[...] = jnp.zeros_like(small)
        dbias[...] = jnp.zeros_like(dbias)
        load.wait()
        tick(0)
        load_dy.wait()

    for half in range(2):

        @pl.when(step == half)
        def _():
            wait_all(kept(half))
            if half:
                wait_all(dy_copies)

    @pl.when(step < 2)
    def _():
        def slope(cut):
            u = z[step, :, cut].astype(f32)
            value, phi = gelu(u)
            z[step, :, cut] = value.astype(bf16)
            return gelu_slope(u, phi)

        dmid[step] = mlp_back(
            step, 0, mid[...], dy_both[step].astype(f32).reshape(ROWS, D),
            (gain, wp, w1, w2, dos.at[step], dm, du, da, small), slope, n2, beta, tick_at((0, 1), 1, 5),
        )

    @pl.when(step == 1)
    def _():
        fc_grads(n2, z, dm, du, one, lambda point: tick(11 + point))

    @pl.when(step >= 2)
    def _():
        half = step - 2
        dx = attention_back(
            half, 0, x_ref[...].reshape(ROWS, D).astype(f32), lambda: dmid[half],
            (gain, wqkv, xs, qw, pr, dos.at[half], du, small, dbias), n2, beta, tick_at((2, 3), 13, 6),
        )
        dx_ref[...] = dx.astype(bf16).reshape(dx_ref.shape)

    @pl.when(step == 3)
    def _():
        attention_grads(n2, o16, da, du, one)
        small_grads(small, dbias, one)
        for n, (exchange, group, k) in enumerate(late):
            exchange.advance(GROUPED[group], k)
            if all(other is not second for other, _, _ in late[n + 1 :]) and (exchange is second or n == 0):
                store_two = pltpu.make_async_copy(two, two_out, local.at[0])
                store_two.start()
        store_one = pltpu.make_async_copy(one, one_out, local.at[1])
        store_one.start()
        tails = [
            pltpu.make_async_copy(ref.at[pl.ds(SLABS * D, SUMS - SLABS * D)], small_out.at[n], loads.at[0, n])
            for n, ref in enumerate((one, two))
        ]
        start_all(tails)
        wait_all(tails)
        wait_all(y_copies)
        store_one.wait()
        store_two.wait()


def whole(shape):
    return pl.BlockSpec(shape, lambda s: (0,) * len(shape), pipeline_mode=pl.Buffered(1))


def of_block(block, *shape):
    return pl.BlockSpec((None,) + shape, lambda s: (block,) + (0,) * len(shape), pipeline_mode=pl.Buffered(1))


def by_half(*shape, buffers=2):
    return pl.BlockSpec(shape, lambda s: (s,) + (0,) * (len(shape) - 1), pipeline_mode=pl.Buffered(buffers))


ANY_SPEC = pl.BlockSpec(memory_space=pl.ANY)
SMEM_SPEC = pl.BlockSpec(memory_space=pltpu.SMEM)
TOKEN_SPEC = pl.BlockSpec((CELLS, HALF, D), lambda s: (0, s, 0))
XS = VMEM((2, 3 * GROUPS, 8 * SLOT, LANES), f32)
DOS = VMEM((2, GROUPS, 8 * SLOT, LANES), f32)
QW = (HALF, 3 * GROUPS, SLOT, LANES)
PR = (HALF, GROUPS, KEYS, 4 * SLOT)


def params(collective_id=None, mib=61):
    return pltpu.CompilerParams(
        vmem_limit_bytes=mib * 2**20, dimension_semantics=("arbitrary",), collective_id=collective_id,
        has_side_effects=collective_id is not None,
    )


CELL = (WINDOW, WINDOW)
PART = jax.ShapeDtypeStruct(CELL + (HALF, D), bf16)
SHIFTS = [pltpu.SemaphoreType.DMA((2, 4)), pltpu.SemaphoreType.DMA((2, 4))]


def run_first(ext, x, cot, gain, beta, wqkv, qvb, bias, wp, ob, w1, b1, w2):
    crops = x.shape[1]
    return pl.pallas_call(
        first_kernel,
        grid=(2,),
        out_shape=(
            PART,
            PART,
            jax.ShapeDtypeStruct(cot.shape, bf16),
            jax.ShapeDtypeStruct((crops,) + QW[1:], bf16),
            jax.ShapeDtypeStruct((crops,) + PR[1:], bf16),
            jax.ShapeDtypeStruct((2 * ROWS, D), bf16),
            jax.ShapeDtypeStruct((2 * ROWS, D), f32),
            jax.ShapeDtypeStruct((2 * ROWS, FF), bf16),
        ),
        in_specs=[
            SMEM_SPEC, TOKEN_SPEC, ANY_SPEC, whole(gain.shape), whole(beta.shape), of_block(0, D, 3 * D), whole(qvb.shape),
            of_block(0, GROUPS, KEYS, 4 * SLOT), of_block(0, D, D), whole(ob.shape), of_block(0, D, FF),
            whole(b1.shape), of_block(0, FF, D),
        ],
        out_specs=(
            ANY_SPEC, whole(PART.shape), ANY_SPEC, by_half(*QW), by_half(*PR), by_half(ROWS, D), by_half(ROWS, D),
            by_half(ROWS, FF),
        ),
        scratch_shapes=[
            XS, VMEM((2, GROUPS, 8 * KEYS, LANES), f32), VMEM(PART.shape, bf16),
        ] + SHIFTS,
        compiler_params=params(1),
        name="first_forward",
    )(ext, x, cot, gain, beta, wqkv, qvb, bias, wp, ob, w1, b1, w2)


GRADS = jax.ShapeDtypeStruct((SUMS, D), bf16)
SMALLS = [VMEM((SMALL, D), f32), VMEM((GROUPS, KEYS, 4 * SLOT), f32)]


def run_second(ext, count, x_first, x_last, cot, gain, beta, wqkv, qvb, bias, wp, ob, w1, b1, w2):
    return pl.pallas_call(
        second_kernel,
        grid=(2,),
        out_shape=(jax.ShapeDtypeStruct(cot.shape, bf16), PART, PART, GRADS),
        in_specs=[
            SMEM_SPEC, SMEM_SPEC, ANY_SPEC, ANY_SPEC, TOKEN_SPEC, whole(gain.shape), whole(beta.shape), of_block(1, D, 3 * D),
            whole(qvb.shape), of_block(1, GROUPS, KEYS, 4 * SLOT), of_block(1, D, D), whole(ob.shape),
            of_block(1, D, FF), whole(b1.shape), of_block(1, FF, D),
        ],
        out_specs=(TOKEN_SPEC, ANY_SPEC, whole(PART.shape), whole(GRADS.shape)),
        scratch_shapes=[
            XS, VMEM(QW, bf16), VMEM(PR, bf16), VMEM((2, GROUPS, 8 * KEYS, LANES), f32),
            VMEM((ROWS, D), f32), VMEM((ROWS, FF), bf16), DOS,
        ] + SMALLS + [VMEM((2, ROWS, width), bf16) for width in (D, D, D, FF, D, FF, D, 3 * D)]
        + [VMEM((2,) + PART.shape, bf16), VMEM(PART.shape, bf16)] + SHIFTS + [pltpu.SemaphoreType.DMA(())],
        compiler_params=params(2, 63),
        name="second_block",
    )(ext, count, x_first, x_last, cot, gain, beta, wqkv, qvb, bias, wp, ob, w1, b1, w2)


def in_steps(first, *shape, axis=0, buffers=2):
    def index(s):
        return tuple(jnp.clip(s - first, 0, 1) if n == axis else 0 for n in range(len(shape)))

    return pl.BlockSpec(shape, index, pipeline_mode=pl.Buffered(buffers))


def run_third(x, dy_first, dy_last, y, qw, pr, o16, mid, u, gain, beta, wqkv, wp, w1, w2, two):
    tokens = (CELLS, HALF, D)
    return pl.pallas_call(
        third_kernel,
        grid=(4,),
        out_shape=(
            jax.ShapeDtypeStruct(x.shape, bf16), GRADS, GRADS, jax.ShapeDtypeStruct(y.shape, bf16),
            jax.ShapeDtypeStruct((2, SUMS - SLABS * D, D), bf16),
        ),
        in_specs=[
            in_steps(2, *tokens, axis=1), ANY_SPEC, ANY_SPEC, ANY_SPEC, in_steps(2, *QW, buffers=1),
            in_steps(2, *PR, buffers=1), ANY_SPEC, in_steps(0, ROWS, D), ANY_SPEC,
            whole(gain.shape), whole(beta.shape), of_block(0, D, 3 * D), of_block(0, D, D), of_block(0, D, FF),
            of_block(0, FF, D), ANY_SPEC,
        ],
        out_specs=(in_steps(2, *tokens, axis=1),) + (ANY_SPEC,) * 4,
        scratch_shapes=[XS, VMEM((2,) + DOS.shape, f32)] + SMALLS + [VMEM((2, ROWS, D), f32)]
        + [VMEM((2, ROWS, width), bf16) for width in (D, D, FF, D, FF, D)]
        + [VMEM(GRADS.shape, bf16)] * 2 + exchange_scratch() * 2
        + [pltpu.SemaphoreType.DMA((2,)), pltpu.SemaphoreType.DMA((2, 2)), VMEM((2,) + PART.shape, bf16)] + SHIFTS,
        compiler_params=params(0, 63),
        name="first_backward",
    )(x, dy_first, dy_last, y, qw, pr, o16, mid, u, gain, beta, wqkv, wp, w1, w2, two)


def jobs():
    n_img, n_win = lax.axis_size("img"), lax.axis_size("win")
    bits = [("win", b) for b in range(1, n_win.bit_length() - 1)] + [("img", b) for b in range(n_img.bit_length() - 1)]
    pairs = [bits[n : n + 2] for n in range(0, len(bits), 2)]
    orders = [[[("win", 0)]] + pairs, [[("win", 0)]] + pairs[::-1]]
    out = []
    for group in range(3):
        out += [(1536 * group, 1024, orders[0]), (1536 * group + 1024, 512, orders[1])]
    return out + [(SLABS * D, SUMS - SLABS * D, orders[0])]


def plan_sizes(size, order):
    out = []
    for group in order:
        ways = 2 ** len(group)
        cut = ways if size % (16 * ways) == 0 else 1
        size //= cut
        out.append((ways, cut, size))
    return out


class Exchange:
    def __init__(self, buf, landing, send, recv, free):
        self.buf, self.landing, self.send, self.recv, self.free = buf, landing, send, recv, free
        index = {axis: lax.axis_index(axis) for axis in ("img", "win")}
        self.plans, land = [], 0
        for start, rows, order in jobs():
            plan = []
            for group, (ways, cut, size) in zip(order, plan_sizes(rows, order)):
                own = [(index[axis] // 2**bit) % 2 for axis, bit in group]
                peers = []
                for apart in range(1, ways):
                    to, piece = {}, 0
                    for n, (axis, bit) in enumerate(group):
                        here = own[n]
                        if apart >> n & 1:
                            to[axis] = to.get(axis, index[axis]) + 2**bit - 2 ** (bit + 1) * here
                            here = 1 - here
                        piece = piece + here * 2**n
                    peers.append((to, start + piece * size if cut > 1 else start, land))
                    land += size
                if cut > 1:
                    start = start + sum(here * 2**n for n, here in enumerate(own)) * size
                plan.append((start, size, cut, peers))
            self.plans.append(plan)
        self.bits = len(self.plans[0])
        self.stages = 2 * self.bits

    def peers(self):
        return [to for *_, peers in self.plans[0] for to, _, _ in peers]

    def copies(self, c, k):
        n = min(k, self.stages - 1 - k)
        keep, size, cut, peers = self.plans[c][n]
        if k >= self.bits and cut == 1:
            return []
        out = []
        for p, (to, give, land) in enumerate(peers):
            if k < self.bits:
                source, target = self.buf.at[pl.ds(pl.multiple_of(give, 16), size)], self.landing.at[pl.ds(land, size)]
            else:
                source = target = self.buf.at[pl.ds(pl.multiple_of(keep, 16), size)]
            out.append(
                pltpu.make_async_remote_copy(
                    source, target, self.send.at[c, k, p], self.recv.at[c, k, p], device_id=to, device_id_type=MESH
                )
            )
        return out

    def start(self, c, k):
        copies = self.copies(c, k)
        if copies and k >= self.bits:
            pl.semaphore_wait(self.free.at[c, self.stages - 1 - k], len(copies))
        for copy in copies:
            copy.start()

    def finish(self, c, k):
        for copy in self.copies(c, k):
            copy.wait()
        if k >= self.bits:
            return
        keep, size, cut, peers = self.plans[c][k]
        if cut > 1:
            for to, _, _ in peers:
                pl.semaphore_signal(self.free.at[c, k], inc=1, device_id=to, device_id_type=MESH)
        tile = max(t for t in (16, 32, 48, 64) if size % t == 0)

        def add(i, carry):
            here = pl.ds(pl.multiple_of(keep + i * tile, 16), tile)
            total = self.buf[here, :].astype(f32)
            for _, _, land in peers:
                total = total + self.landing[pl.ds(pl.multiple_of(land + i * tile, 16), tile), :].astype(f32)
            self.buf[here, :] = total.astype(bf16)
            return carry

        lax.fori_loop(0, size // tile, add, 0)

    def advance(self, which, k):
        for c in which:
            if 1 <= k <= self.stages:
                self.finish(c, k - 1)
            if k < self.stages:
                self.start(c, k)


def exchange_scratch():
    landing, most = 0, 0
    for _, rows, order in jobs():
        for ways, _, size in plan_sizes(rows, order):
            landing += size * (ways - 1)
            most = max(most, ways - 1)
    n, bits = len(jobs()), len(jobs()[0][2])
    dma = pltpu.SemaphoreType.DMA((n, 2 * bits, most))
    return [VMEM((landing, D), bf16), dma, dma, pltpu.SemaphoreType.REGULAR((n, bits))]


def finish_kernel(*refs):
    ins, (small, *sources), outs, smalls, targets = refs[:8], refs[8:11], refs[11:15], refs[15:20], refs[20:22]
    step = pl.program_id(0)

    @pl.when(step == 0)
    def _():
        rows = small[:, :SMALL].astype(f32)
        for n, out in enumerate(smalls[:4]):
            out[...] = rows[:, 2 * n : 2 * n + 2]
        for n in range(4):
            smalls[4][:, D * n : D * (n + 1)] = rows[:, 8 + n]

    for source, target in zip(sources, targets):
        target[...] = source[...]

    @pl.when(step < 4)
    def _():
        for n, out in enumerate(outs):
            for block in range(2):
                value = ins[2 * n + block][...].astype(f32)
                out[block] = value.T if n == 1 else value


def finish(grads_one, grads_two, small, *passed):
    first = [lambda j: jnp.minimum(j, 3), lambda j: 4 + jnp.minimum(j, 3), lambda j: 8 + jnp.minimum(j, 2), lambda j: 11]
    places = [
        lambda j: (0, 0, jnp.minimum(j, 3)), lambda j: (0, jnp.minimum(j, 3), 0), lambda j: (0, 0, jnp.minimum(j, 2)),
        lambda j: (0, 0, 0),
    ]
    small_shapes = [(2, 2, D)] * 4 + [(2, FF)]
    tokens = pl.BlockSpec((WINDOW,) + passed[0].shape[1:], lambda j: (j, 0, 0))
    return pl.pallas_call(
        finish_kernel,
        grid=(WINDOW,),
        out_shape=tuple(
            jax.ShapeDtypeStruct(shape, f32)
            for shape in [(2, D, FF), (2, FF, D), (2, D, 3 * D), (2, D, D)] + small_shapes
        ) + tuple(jax.ShapeDtypeStruct(v.shape, v.dtype) for v in passed),
        in_specs=[pl.BlockSpec((D, D), lambda j, row=row: (row(j), 0)) for row in first for _ in range(2)]
        + [whole(small.shape)] + [tokens] * 2,
        out_specs=tuple(pl.BlockSpec((2, D, D), place) for place in places) + tuple(whole(v) for v in small_shapes)
        + (tokens,) * 2,
        compiler_params=params(),
        name="finish_gradients",
    )(*[grads_one, grads_two] * 4, small, *passed)


def position_lookup():
    j = jnp.arange(KEYS)[:, None]
    i = jnp.arange(SLOT)[None, :]
    side = SIDE - 1
    index = (i // WINDOW - j // WINDOW + WINDOW - 1) * side + i % WINDOW - j % WINDOW + WINDOW - 1
    index = jnp.where((i < CELLS) & (j < CELLS), index, -1).reshape(-1)
    return (jnp.arange(side * side)[:, None] == index[None, :]).astype(f32)


def on_device(
    tokens, cotangent, crop_counts, crop_extent, norm_gain, norm_bias, qkv_weight, qv_bias, rel_table, proj_weight,
    out_bias, fc1_weight, fc1_bias, fc2_weight,
):
    crops = tokens.shape[0]
    x = tokens.reshape(crops, CELLS, D).transpose(1, 0, 2)
    cot = cotangent.reshape(crops, CELLS, D).transpose(1, 0, 2)
    lookup = position_lookup()
    highest = lax.Precision.HIGHEST
    bias = jnp.einsum("bkh,kp->bhp", rel_table, lookup, precision=highest) * LOG2E
    bias = bias.reshape(2, GROUPS, 4, KEYS, SLOT).transpose(0, 1, 3, 2, 4)
    bias = jnp.where(jnp.arange(KEYS)[:, None, None] < CELLS, bias, NEG).reshape(2, GROUPS, KEYS, 4 * SLOT)

    cells_of = lambda v: v.reshape(CELL + v.shape[1:])
    rows_of = lambda v: v.reshape((CELLS,) + v.shape[2:])
    x_first, x_last, cot_shifted, qw, pr, o16, mid, u = run_first(
        crop_extent.T, x, cells_of(cot), norm_gain, norm_bias, qkv_weight, qv_bias, bias, proj_weight, out_bias,
        fc1_weight, fc1_bias, fc2_weight,
    )
    y, dx_first, dx_last, grads_two = run_second(
        crop_extent.T, crop_counts, x_first, x_last, rows_of(cot_shifted), norm_gain, norm_bias, qkv_weight, qv_bias,
        bias, proj_weight, out_bias, fc1_weight, fc1_bias, fc2_weight,
    )
    dx, sum_one, sum_two, output, small = run_third(
        x, dx_first, dx_last, cells_of(y), qw, pr, o16, mid, u, norm_gain, norm_bias, qkv_weight, proj_weight,
        fc1_weight, fc2_weight, grads_two,
    )
    fc1, fc2, qkv, proj, gains, biases, qv, outs, fc1_b, output, dx = finish(
        sum_one, sum_two, small, rows_of(output), dx
    )
    dbias = small[:, SMALL : SMALL + TABLE, : 4 * SLOT].astype(f32)
    dbias = dbias.reshape(2, GROUPS, KEYS, 4, SLOT).transpose(0, 1, 3, 2, 4)
    table = jnp.einsum("hp,kp->kh", dbias.reshape(2 * HEADS, KEYS * SLOT), lookup, precision=highest)
    table = table.reshape(-1, 2, HEADS).transpose(1, 0, 2)
    back = lambda v: v.transpose(1, 0, 2).reshape(tokens.shape)
    return back(output), back(dx), gains, biases, qkv, qv, table, proj, outs, fc1, fc1_b, fc2


def solution(mesh):
    split = P("img", "win", None, None)
    return jax.shard_map(
        on_device,
        mesh=mesh,
        in_specs=(split, split, P("img"), P("img", None)) + (P(),) * 10,
        out_specs=(split, split) + (P(),) * 10,
        check_vma=False,
    )
```

```python
import jax
import jax.numpy as jnp
from jax import lax
from jax.experimental import pallas as pl
from jax.experimental.pallas import tpu as pltpu
from jax.sharding import PartitionSpec as P

D = 384
FF = 1536
HEADS = 12
HEAD_DIM = 32
WINDOW = 7
SHIFT = 3
CELLS = WINDOW * WINDOW
SIDE = 2 * WINDOW
HALF = 16
ROWS = CELLS * HALF
LANES = 128
GROUPS = 3
KEYS = 56
SLOT = 64
SLABS = 12
SMALL = 16
TABLE = GROUPS * KEYS
SUMS = SLABS * D + 256
GROUPED = ((0, 1), (2, 3), (4, 5, 6))
NEG = -1e30
LOG2E = 1.4426950408889634
SCALE = HEAD_DIM**-0.5
MESH = pl.DeviceIdType.MESH

bf16 = jnp.bfloat16
f32 = jnp.float32
VMEM = pltpu.VMEM


def mm(a, b):
    return lax.dot_general(a, b, (((1,), (0,)), ((), ())), preferred_element_type=f32)


def mm_bt(a, b):
    return lax.dot_general(a, b, (((1,), (1,)), ((), ())), preferred_element_type=f32)


def mm_at(a, b):
    return lax.dot_general(a, b, (((0,), (0,)), ((), ())), preferred_element_type=f32)


def norm(x):
    centred = x - jnp.mean(x, -1, keepdims=True)
    rstd = lax.rsqrt(jnp.mean(centred * centred, -1, keepdims=True) + 1e-5)
    return centred * rstd, rstd


def norm_back(xh, rstd, dn, gain):
    e = dn * gain
    mean_e = jnp.mean(e, -1, keepdims=True)
    mean_ex = jnp.mean(e * xh, -1, keepdims=True)
    dx = rstd * (e - mean_e - xh * mean_ex)
    return dx, jnp.sum(dn * xh, 0, keepdims=True), jnp.sum(dn, 0, keepdims=True)


def gelu(u):
    phi = 0.5 + 0.5 * lax.erf(u * 0.7071067811865476)
    return u * phi, phi


def gelu_slope(u, phi):
    return phi + u * jnp.exp2(u * u * (-0.5 * LOG2E)) * 0.3989422804014327


def spread(rows):
    head = lax.broadcasted_iota(jnp.int32, rows.shape, 1) // HEAD_DIM
    zero = jnp.zeros_like(rows)
    return jnp.concatenate([jnp.where(head == h, rows, zero) for h in range(4)], 0)


def gather_heads(rows):
    head = lax.broadcasted_iota(jnp.int32, (KEYS, LANES), 1) // HEAD_DIM
    out = rows[:KEYS]
    for h in range(1, 4):
        out = jnp.where(head == h, rows[SLOT * h : SLOT * h + KEYS], out)
    return out


def to_windows(ref, slot, part):
    parted = part.reshape(CELLS, 2, 8, LANES)
    for cg in range(2):
        ref[cg, slot, 0 : CELLS * 8, :] = parted[:, cg].reshape(CELLS * 8, LANES)


def from_windows(ref, slot):
    parts = [ref[cg, slot, 0 : CELLS * 8, :].reshape(CELLS, 1, 8, LANES) for cg in range(2)]
    return jnp.concatenate(parts, 1).reshape(ROWS, LANES)


def cells(shifted):
    win = lax.axis_index("win")
    j = lax.broadcasted_iota(jnp.int32, (KEYS, LANES), 0)
    i = lax.broadcasted_iota(jnp.int32, (KEYS, LANES), 1) % SLOT
    top, left = WINDOW * (win // 2), WINDOW * (win % 2)
    places = [top + j // WINDOW, left + j % WINDOW, top + i // WINDOW, left + i % WINDOW]
    if not shifted:
        return places, None
    region = [(v >= SIDE - WINDOW).astype(jnp.int32) + (v >= SIDE - SHIFT).astype(jnp.int32) for v in places]
    apart = (region[0] != region[2]) | (region[1] != region[3])
    moved = [jnp.where(v + SHIFT >= SIDE, v + SHIFT - SIDE, v + SHIFT) for v in places]
    return moved, jnp.where(apart, NEG, 0.0)


def forward(step, block, shifted, x, refs, keep_n1=None, keep_n2=None, keep_gelu=None, keep_u=None):
    (ext, gain, beta, wqkv, qvb, bias, wp, ob, w1, b1, w2, xs, qw, pr, os, o16, mid) = refs
    xh, _ = norm(x)
    n1 = (xh * gain[block, 0:1, :] + beta[block, 0:1, :]).astype(bf16)
    if keep_n1 is not None:
        keep_n1[step] = n1
    proj = mm(n1, wqkv[...])
    q = (proj[:, :D] + qvb[block, 0:1, :]) * (SCALE * LOG2E)
    k = proj[:, D : 2 * D]
    v = proj[:, 2 * D :] + qvb[block, 1:2, :]
    for g in range(GROUPS):
        cut = slice(LANES * g, LANES * (g + 1))
        to_windows(xs, g, q[:, cut])
        to_windows(xs, GROUPS + g, k[:, cut])
        to_windows(xs, 2 * GROUPS + g, v[:, cut])
    places, apart = cells(shifted)
    if apart is not None:
        apart = jnp.concatenate([apart, apart], 1)

    def windows(part, carry):
        masks = []
        for w in [8 * part + n for n in range(8)]:
            rows, cols = ext[0, step * HALF + w], ext[1, step * HALF + w]
            valid_j = (places[0] < rows) & (places[1] < cols)
            valid_i = (places[2] < rows) & (places[3] < cols)
            mask = jnp.where(valid_i == valid_j, 0.0, NEG)
            mask = jnp.concatenate([mask, mask], 1)
            masks.append(mask if apart is None else mask + apart)
        for g in range(GROUPS):
            for n in range(8):
                w = 8 * part + n
                qs, ks, vs = (xs[part, GROUPS * m + g, pl.ds(n, SLOT, stride=8), :].astype(bf16) for m in range(3))
                for m, value in enumerate((qs, ks, vs)):
                    qw[w, GROUPS * m + g] = value
                s = mm_bt(ks[:KEYS], spread(qs)) + bias[g] + masks[n]
                e = jnp.exp2(s - jnp.max(s, 0, keepdims=True))
                p = (e * (1.0 / jnp.sum(e, 0, keepdims=True))).astype(bf16)
                pr[w, g] = p
                os[part, g, pl.ds(n, KEYS, stride=8), :] = gather_heads(mm_at(p, vs[:KEYS]))
        return carry

    lax.fori_loop(0, 2, windows, 0)
    for g in range(GROUPS):
        o16[:, LANES * g : LANES * (g + 1)] = from_windows(os, g).astype(bf16)
    middle = x + (mm(o16[...], wp[...]) + ob[block, 0:1, :])
    mid[...] = middle
    xh2, _ = norm(middle)
    n2 = (xh2 * gain[block, 1:2, :] + beta[block, 1:2, :]).astype(bf16)
    if keep_n2 is not None:
        keep_n2[step] = n2
    y = middle + ob[block, 1:2, :]
    for part in range(3):
        cut = slice(512 * part, 512 * (part + 1))
        u = mm(n2, w1[:, cut]) + b1[block : block + 1, cut]
        if keep_u is not None:
            keep_u[:, cut] = u.astype(bf16)
        z, phi = gelu(u)
        z = z.astype(bf16)
        if keep_gelu is not None:
            keep_gelu[0][step, :, cut] = z
            keep_gelu[1][:, cut] = gelu_slope(u, phi).astype(bf16)
        y = y + mm(z, w2[cut, :])
    return y


def no_tick(point, when=True):
    pass


def mlp_back(step, block, mid, dy, refs, slope, keep_n2=None, beta=None, tick=no_tick):
    (gain, wp, w1, w2, dos, dm_all, du_all, da_all, small) = refs

    def add_small(row, value):
        small[row : row + 1, :] += value

    dm = dy.astype(bf16)
    dm_all[step] = dm
    add_small(7, jnp.sum(dm.astype(f32), 0, keepdims=True))
    sums = []
    for part in range(3):
        cut = slice(512 * part, 512 * (part + 1))
        du = (mm_bt(dm, w2[cut, :]) * slope(cut)).astype(bf16)
        du_all[step, :, cut] = du
        sums.append(jnp.sum(du.astype(f32), 0, keepdims=True))
        tick(part)
    sums = jnp.concatenate(sums, 1)
    for part in range(4):
        add_small(8 + part, sums[:, D * part : D * (part + 1)])
    dn2 = mm_bt(du_all[step], w1[...])
    tick(3)
    xh, rstd = norm(mid)
    if keep_n2 is not None:
        keep_n2[step] = (xh * gain[block, 1:2, :] + beta[block, 1:2, :]).astype(bf16)
    dx, dgain, dbeta = norm_back(xh, rstd, dn2, gain[block, 1:2, :])
    add_small(1, dgain)
    add_small(3, dbeta)
    dmid = dy + dx
    da = dmid.astype(bf16)
    da_all[step] = da
    add_small(6, jnp.sum(da.astype(f32), 0, keepdims=True))
    do = mm_bt(da, wp[...])
    for g in range(GROUPS):
        to_windows(dos, g, do[:, LANES * g : LANES * (g + 1)])
    tick(4)
    return dmid


def attention_back(step, block, x, dmid, refs, keep_n1=None, beta=None, tick=no_tick):
    (gain, wqkv, xs, qw, pr, dos, dp_all, small, dbias) = refs

    def add_small(row, value):
        small[row : row + 1, :] += value

    def windows_back(part, carry):
        units = [(n, g) for n in range(8) for g in range(GROUPS)]
        grad, scores = {}, {}
        for n, g in units:
            grad[n, g] = spread(dos[part, g, pl.ds(n, SLOT, stride=8), :].astype(bf16))
        dprobs = {(n, g): mm_bt(qw[8 * part + n, 2 * GROUPS + g][:KEYS], grad[n, g]) for n, g in units}
        for g in range(GROUPS):
            total = jnp.zeros((KEYS, 4 * SLOT), f32)
            for n in range(8):
                p = pr[8 * part + n, g].astype(f32)
                t = p * dprobs[n, g]
                ds = t - p * jnp.sum(t, 0, keepdims=True)
                total = total + ds
                scores[n, g] = ds.astype(bf16)
            dbias[g] += total
        for n, g in units:
            w, ds = 8 * part + n, scores[n, g]
            dv = mm(pr[w, g], grad[n, g])
            dk = mm(ds, spread(qw[w, g])) * (1.0 / LOG2E)
            dq = gather_heads(mm_at(ds, qw[w, GROUPS + g][:KEYS])) * SCALE
            for m, value in enumerate((dq, dk, dv)):
                xs[part, GROUPS * m + g, pl.ds(n, KEYS, stride=8), :] = value
        for n in range(4):
            tick(n, part == n // 2)
        return carry

    lax.fori_loop(0, 2, windows_back, 0)
    for n in range(3 * GROUPS):
        dp_all[step, :, LANES * n : LANES * (n + 1)] = from_windows(xs, n).astype(bf16)
    dp = dp_all[step, :, : 3 * D]
    add_small(4, jnp.sum(dp[:, :D].astype(f32), 0, keepdims=True))
    add_small(5, jnp.sum(dp[:, 2 * D :].astype(f32), 0, keepdims=True))
    dn1 = mm_bt(dp, wqkv[...])
    tick(4)
    xh, rstd = norm(x)
    if keep_n1 is not None:
        keep_n1[step] = (xh * gain[block, 0:1, :] + beta[block, 0:1, :]).astype(bf16)
    dx, dgain, dbeta = norm_back(xh, rstd, dn1, gain[block, 0:1, :])
    add_small(0, dgain)
    add_small(2, dbeta)
    tick(5)
    return dmid() + dx


def flat(ref, cut=slice(None)):
    return ref[:, :, cut].reshape(2 * ROWS, -1)


def put_slabs(out, first, value):
    for j in range(value.shape[1] // D):
        out[D * (first + j) : D * (first + j + 1), :] = value[:, D * j : D * (j + 1)].astype(bf16)


def fc_grads(n2, z, dm, du, out, tick=no_tick):
    for first, left, right in ((0, n2, du), (4, dm, z)):
        for j in range(2):
            put_slabs(out, first + 2 * j, mm_at(flat(left), flat(right, slice(768 * j, 768 * (j + 1)))))
        tick(first // 4)


def attention_grads(n1, o16, da, dp, out):
    put_slabs(out, 8, mm_at(flat(n1), flat(dp, slice(3 * D))))
    put_slabs(out, 11, mm_at(flat(o16), flat(da)))


def small_grads(small, dbias, out):
    base = SLABS * D
    out[base : base + SMALL, :] = small[...].astype(bf16)
    out[base + SMALL : SUMS, :] = jnp.zeros((SUMS - base - SMALL, D), bf16)
    out[base + SMALL : base + SMALL + TABLE, : 4 * SLOT] = dbias[...].reshape(TABLE, 4 * SLOT).astype(bf16)


KEEP = WINDOW - SHIFT
NEAR, FAR = slice(0, KEEP), slice(KEEP, WINDOW)
HERE, THERE = slice(SHIFT, WINDOW), slice(0, SHIFT)


def shift_peers():
    win = lax.axis_index("win")
    beside = 1 - 2 * (win % 2)
    below = 2 - 4 * (win // 2 % 2)
    return [{"win": win + beside}, {"win": win + below}, {"win": win + beside + below}]


def shift_copies(source, target, send, recv, back=False):
    plain = [(HERE, HERE), (HERE, THERE), (THERE, HERE), (THERE, THERE)]
    moved = [(NEAR, NEAR), (NEAR, FAR), (FAR, NEAR), (FAR, FAR)]
    if back:
        plain, moved = moved, plain
    out = [pltpu.make_async_copy(source.at[plain[0]], target.at[moved[0]], send.at[3])]
    for n, to in enumerate(shift_peers()):
        out.append(
            pltpu.make_async_remote_copy(
                source.at[plain[n + 1]], target.at[moved[n + 1]], send.at[n], recv.at[n], device_id=to, device_id_type=MESH
            )
        )
    return out


def start_all(copies):
    for copy in copies:
        copy.start()


def wait_all(copies):
    for copy in copies:
        copy.wait()


def greet(peers):
    barrier = pltpu.get_barrier_semaphore()
    for to in peers:
        pl.semaphore_signal(barrier, inc=1, device_id=to, device_id_type=MESH)
    pl.semaphore_wait(barrier, len(peers))


def first_kernel(
    ext, x_ref, cot, gain, beta, wqkv, qvb, bias, wp, ob, w1, b1, w2,
    y_shifted, y_last, cot_shifted, qw, pr, o16, mid, u_ref, xs, os, y_first, send, recv,
):
    step = pl.program_id(0)
    cot_copies = shift_copies(cot, cot_shifted, send.at[0], recv.at[0])
    y_copies = shift_copies(y_first, y_shifted, send.at[1], recv.at[1])

    @pl.when(step == 0)
    def _():
        greet(shift_peers())
        start_all(cot_copies)
        xs[...] = jnp.zeros_like(xs)

    x = x_ref[...].reshape(ROWS, D).astype(f32)
    y = forward(
        step, 0, False, x, (ext, gain, beta, wqkv, qvb, bias, wp, ob, w1, b1, w2, xs, qw, pr, os, o16, mid), keep_u=u_ref
    )
    y = y.astype(bf16).reshape(WINDOW, WINDOW, HALF, D)

    @pl.when(step == 0)
    def _():
        y_first[...] = y
        start_all(y_copies)

    @pl.when(step == 1)
    def _():
        y_last[...] = y
        wait_all(y_copies)
        wait_all(cot_copies)


def second_kernel(
    ext, count, x_first, x_last, cot_ref, gain, beta, wqkv, qvb, bias, wp, ob, w1, b1, w2,
    y_shifted, y_last, dx_shifted, dx_last, grads,
    xs, qw, pr, os, mid, slope, dos, small, dbias, n1, n2, o16, z, dm, du, da, dp, x_both, dx_first, y_first, send, recv, local,
):
    step = pl.program_id(0)
    x_copies = shift_copies(x_last, x_both.at[1], send.at[0], recv.at[0])
    dx_copies = shift_copies(dx_first, dx_shifted, send.at[1], recv.at[1], back=True)
    y_copies = shift_copies(y_first, y_shifted, send.at[2], recv.at[2], back=True)

    @pl.when(step == 0)
    def _():
        load = pltpu.make_async_copy(x_first, x_both.at[0], local)
        load.start()
        greet(shift_peers())
        start_all(x_copies)
        load.wait()
        xs[...] = jnp.zeros_like(xs)
        dos[...] = jnp.zeros_like(dos)
        small[...] = jnp.zeros_like(small)
        dbias[...] = jnp.zeros_like(dbias)

    @pl.when(step == 1)
    def _():
        wait_all(x_copies)

    x = x_both[step].reshape(ROWS, D).astype(f32)
    live = lax.broadcasted_iota(jnp.int32, (CELLS, HALF, 1), 1) + step * HALF < count[0]
    y = forward(
        step, 1, True, x,
        (ext, gain, beta, wqkv, qvb, bias, wp, ob, w1, b1, w2, xs, qw, pr, os, o16.at[step], mid),
        n1, n2, (z, slope),
    )
    y = jnp.where(live, y.reshape(CELLS, HALF, D), 0.0).astype(bf16).reshape(WINDOW, WINDOW, HALF, D)

    @pl.when(step == 0)
    def _():
        y_first[...] = y
        start_all(y_copies)

    @pl.when(step == 1)
    def _():
        y_last[...] = y

    dy = jnp.where(live, cot_ref[...].astype(f32), 0.0).reshape(ROWS, D)
    mid[...] = mlp_back(
        step, 1, mid[...], dy, (gain, wp, w1, w2, dos, dm, du, da, small), lambda cut: slope[:, cut].astype(f32)
    )
    dx = attention_back(
        step, 1, x, lambda: mid[...], (gain, wqkv, xs, qw, pr, dos, dp, small, dbias)
    )
    dx = dx.astype(bf16).reshape(WINDOW, WINDOW, HALF, D)

    @pl.when(step == 0)
    def _():
        dx_first[...] = dx
        start_all(dx_copies)

    @pl.when(step == 1)
    def _():
        dx_last[...] = dx
        fc_grads(n2, z, dm, du, grads)
        attention_grads(n1, o16, da, dp, grads)
        small_grads(small, dbias, grads)
        wait_all(y_copies)
        wait_all(dx_copies)


LAST = 24
PACE = {
    (0, 0): (4.2, 6.0, 13.5, 17.1, 21.7, 32.9, 50.5),
    (0, 1): (1.9, 3.9, 9.1, 12.7, 16.3, 31.4, 37.3),
    (0, 2): (2.6, 4.5, 10.1, 13.9, 20.1, 40.0, 52.1),
    (1, 0): (30.7, 33.8, 38.5, 44.6, 47.5, 59.9, 73.1),
    (1, 1): (13.1, 17.1, 29.9, 42.0, 56.9, 72.9, 95.6),
    (1, 2): (29.3, 30.4, 38.3, 39.8, 46.6, 57.1, 68.4),
}


def schedule(*exchanges):
    out = []
    for (which, group), places in PACE.items():
        exchange = exchanges[which]
        if exchange.stages + 1 != len(places):
            first = LAST + 1 if which and group == 2 else places[0]
            places = [first + 4 * k + 0.1 * group for k in range(exchange.stages + 1)]
        out += [(place, exchange, group, k) for k, place in enumerate(places)]
    return sorted(out, key=lambda item: item[0])


def third_kernel(
    x_ref, dy_first, dy_last, y_ref, qw, pr, o_ref, mid, u_ref, gain, beta, wqkv, wp, w1, w2, two_ref,
    dx_ref, one_out, two_out, y_out, small_out,
    xs, dos, small, dbias, dmid, n2, o16, z, dm, du, da,
    one, two, land_one, send_one, recv_one, free_one, land_two, send_two, recv_two, free_two, local, loads, dy_both, send, recv,
):
    step = pl.program_id(0)
    first = Exchange(one, land_one, send_one, recv_one, free_one)
    second = Exchange(two, land_two, send_two, recv_two, free_two)
    dy_copies = shift_copies(dy_last, dy_both.at[1], send.at[0], recv.at[0], back=True)
    y_copies = shift_copies(y_ref, y_out, send.at[1], recv.at[1], back=True)
    moves = [[] for _ in range(LAST + 1)]
    late = []
    for place, exchange, group, k in schedule(second, first):
        (moves[int(place)] if place < LAST + 1 else late).append((exchange, group, k))

    def tick(n):
        if n == 14:
            start_all(y_copies)
        for exchange, group, k in moves[n]:
            exchange.advance(GROUPED[group], k)

    def tick_at(steps, base, per_step):
        def ticker(point, when=True):
            for s in steps:
                pl.when((step == s) & when)(lambda s=s: tick(base + (s - steps[0]) * per_step + point))

        return ticker

    def kept(half):
        rows = pl.ds(half * ROWS, ROWS)
        return (
            pltpu.make_async_copy(u_ref.at[rows], z.at[half], loads.at[0, half]),
            pltpu.make_async_copy(o_ref.at[rows], o16.at[half], loads.at[1, half]),
        )

    @pl.when(step == 0)
    def _():
        load = pltpu.make_async_copy(two_ref, two, local.at[0])
        load.start()
        load_dy = pltpu.make_async_copy(dy_first, dy_both.at[0], local.at[1])
        load_dy.start()
        for half in range(2):
            start_all(kept(half))
        greet(second.peers() + shift_peers()[2:])
        start_all(dy_copies)
        xs[...] = jnp.zeros_like(xs)
        dos[...] = jnp.zeros_like(dos)
        small[...] = jnp.zeros_like(small)
        dbias[...] = jnp.zeros_like(dbias)
        load.wait()
        tick(0)
        load_dy.wait()

    for half in range(2):

        @pl.when(step == half)
        def _():
            wait_all(kept(half))
            if half:
                wait_all(dy_copies)

    @pl.when(step < 2)
    def _():
        def slope(cut):
            u = z[step, :, cut].astype(f32)
            value, phi = gelu(u)
            z[step, :, cut] = value.astype(bf16)
            return gelu_slope(u, phi)

        dmid[step] = mlp_back(
            step, 0, mid[...], dy_both[step].astype(f32).reshape(ROWS, D),
            (gain, wp, w1, w2, dos.at[step], dm, du, da, small), slope, n2, beta, tick_at((0, 1), 1, 5),
        )

    @pl.when(step == 1)
    def _():
        fc_grads(n2, z, dm, du, one, lambda point: tick(11 + point))

    @pl.when(step >= 2)
    def _():
        half = step - 2
        dx = attention_back(
            half, 0, x_ref[...].reshape(ROWS, D).astype(f32), lambda: dmid[half],
            (gain, wqkv, xs, qw, pr, dos.at[half], du, small, dbias), n2, beta, tick_at((2, 3), 13, 6),
        )
        dx_ref[...] = dx.astype(bf16).reshape(dx_ref.shape)

    @pl.when(step == 3)
    def _():
        attention_grads(n2, o16, da, du, one)
        small_grads(small, dbias, one)
        for n, (exchange, group, k) in enumerate(late):
            exchange.advance(GROUPED[group], k)
            if all(other is not second for other, _, _ in late[n + 1 :]) and (exchange is second or n == 0):
                store_two = pltpu.make_async_copy(two, two_out, local.at[0])
                store_two.start()
        store_one = pltpu.make_async_copy(one, one_out, local.at[1])
        store_one.start()
        tails = [
            pltpu.make_async_copy(ref.at[pl.ds(SLABS * D, SUMS - SLABS * D)], small_out.at[n], loads.at[0, n])
            for n, ref in enumerate((one, two))
        ]
        start_all(tails)
        wait_all(tails)
        wait_all(y_copies)
        store_one.wait()
        store_two.wait()


def whole(shape):
    return pl.BlockSpec(shape, lambda s: (0,) * len(shape), pipeline_mode=pl.Buffered(1))


def of_block(block, *shape):
    return pl.BlockSpec((None,) + shape, lambda s: (block,) + (0,) * len(shape), pipeline_mode=pl.Buffered(1))


def by_half(*shape, buffers=2):
    return pl.BlockSpec(shape, lambda s: (s,) + (0,) * (len(shape) - 1), pipeline_mode=pl.Buffered(buffers))


ANY_SPEC = pl.BlockSpec(memory_space=pl.ANY)
SMEM_SPEC = pl.BlockSpec(memory_space=pltpu.SMEM)
TOKEN_SPEC = pl.BlockSpec((CELLS, HALF, D), lambda s: (0, s, 0))
XS = VMEM((2, 3 * GROUPS, 8 * SLOT, LANES), f32)
DOS = VMEM((2, GROUPS, 8 * SLOT, LANES), f32)
QW = (HALF, 3 * GROUPS, SLOT, LANES)
PR = (HALF, GROUPS, KEYS, 4 * SLOT)


def params(collective_id=None, mib=61):
    return pltpu.CompilerParams(
        vmem_limit_bytes=mib * 2**20, dimension_semantics=("arbitrary",), collective_id=collective_id,
        has_side_effects=collective_id is not None,
    )


CELL = (WINDOW, WINDOW)
PART = jax.ShapeDtypeStruct(CELL + (HALF, D), bf16)
SHIFTS = [pltpu.SemaphoreType.DMA((3, 4)), pltpu.SemaphoreType.DMA((3, 4))]


def run_first(ext, x, cot, gain, beta, wqkv, qvb, bias, wp, ob, w1, b1, w2):
    crops = x.shape[1]
    return pl.pallas_call(
        first_kernel,
        grid=(2,),
        out_shape=(
            PART,
            PART,
            jax.ShapeDtypeStruct(cot.shape, bf16),
            jax.ShapeDtypeStruct((crops,) + QW[1:], bf16),
            jax.ShapeDtypeStruct((crops,) + PR[1:], bf16),
            jax.ShapeDtypeStruct((2 * ROWS, D), bf16),
            jax.ShapeDtypeStruct((2 * ROWS, D), f32),
            jax.ShapeDtypeStruct((2 * ROWS, FF), bf16),
        ),
        in_specs=[
            SMEM_SPEC, TOKEN_SPEC, ANY_SPEC, whole(gain.shape), whole(beta.shape), of_block(0, D, 3 * D), whole(qvb.shape),
            of_block(0, GROUPS, KEYS, 4 * SLOT), of_block(0, D, D), whole(ob.shape), of_block(0, D, FF),
            whole(b1.shape), of_block(0, FF, D),
        ],
        out_specs=(
            ANY_SPEC, whole(PART.shape), ANY_SPEC, by_half(*QW), by_half(*PR), by_half(ROWS, D), by_half(ROWS, D),
            by_half(ROWS, FF),
        ),
        scratch_shapes=[
            XS, VMEM((2, GROUPS, 8 * KEYS, LANES), f32), VMEM(PART.shape, bf16),
        ] + SHIFTS,
        compiler_params=params(1),
        name="first_forward",
    )(ext, x, cot, gain, beta, wqkv, qvb, bias, wp, ob, w1, b1, w2)


GRADS = jax.ShapeDtypeStruct((SUMS, D), bf16)
SMALLS = [VMEM((SMALL, D), f32), VMEM((GROUPS, KEYS, 4 * SLOT), f32)]


def run_second(ext, count, x_first, x_last, cot, gain, beta, wqkv, qvb, bias, wp, ob, w1, b1, w2):
    return pl.pallas_call(
        second_kernel,
        grid=(2,),
        out_shape=(PART, PART, PART, PART, GRADS),
        in_specs=[
            SMEM_SPEC, SMEM_SPEC, ANY_SPEC, ANY_SPEC, TOKEN_SPEC, whole(gain.shape), whole(beta.shape), of_block(1, D, 3 * D),
            whole(qvb.shape), of_block(1, GROUPS, KEYS, 4 * SLOT), of_block(1, D, D), whole(ob.shape),
            of_block(1, D, FF), whole(b1.shape), of_block(1, FF, D),
        ],
        out_specs=(ANY_SPEC, whole(PART.shape), ANY_SPEC, whole(PART.shape), whole(GRADS.shape)),
        scratch_shapes=[
            XS, VMEM(QW, bf16), VMEM(PR, bf16), VMEM((2, GROUPS, 8 * KEYS, LANES), f32),
            VMEM((ROWS, D), f32), VMEM((ROWS, FF), bf16), DOS,
        ] + SMALLS + [VMEM((2, ROWS, width), bf16) for width in (D, D, D, FF, D, FF, D, 3 * D)]
        + [VMEM((2,) + PART.shape, bf16), VMEM(PART.shape, bf16), VMEM(PART.shape, bf16)] + SHIFTS
        + [pltpu.SemaphoreType.DMA(())],
        compiler_params=params(2, 63),
        name="second_block",
    )(ext, count, x_first, x_last, cot, gain, beta, wqkv, qvb, bias, wp, ob, w1, b1, w2)


def in_steps(first, *shape, axis=0, buffers=2):
    def index(s):
        return tuple(jnp.clip(s - first, 0, 1) if n == axis else 0 for n in range(len(shape)))

    return pl.BlockSpec(shape, index, pipeline_mode=pl.Buffered(buffers))


def run_third(x, dy_first, dy_last, y, qw, pr, o16, mid, u, gain, beta, wqkv, wp, w1, w2, two):
    tokens = (CELLS, HALF, D)
    return pl.pallas_call(
        third_kernel,
        grid=(4,),
        out_shape=(
            jax.ShapeDtypeStruct(x.shape, bf16), GRADS, GRADS, jax.ShapeDtypeStruct(y.shape, bf16),
            jax.ShapeDtypeStruct((2, SUMS - SLABS * D, D), bf16),
        ),
        in_specs=[
            in_steps(2, *tokens, axis=1), ANY_SPEC, ANY_SPEC, ANY_SPEC, in_steps(2, *QW, buffers=1),
            in_steps(2, *PR, buffers=1), ANY_SPEC, in_steps(0, ROWS, D), ANY_SPEC,
            whole(gain.shape), whole(beta.shape), of_block(0, D, 3 * D), of_block(0, D, D), of_block(0, D, FF),
            of_block(0, FF, D), ANY_SPEC,
        ],
        out_specs=(in_steps(2, *tokens, axis=1),) + (ANY_SPEC,) * 4,
        scratch_shapes=[XS, VMEM((2,) + DOS.shape, f32)] + SMALLS + [VMEM((2, ROWS, D), f32)]
        + [VMEM((2, ROWS, width), bf16) for width in (D, D, FF, D, FF, D)]
        + [VMEM(GRADS.shape, bf16)] * 2 + exchange_scratch() * 2
        + [pltpu.SemaphoreType.DMA((2,)), pltpu.SemaphoreType.DMA((2, 2)), VMEM((2,) + PART.shape, bf16)] + SHIFTS,
        compiler_params=params(0, 63),
        name="first_backward",
    )(x, dy_first, dy_last, y, qw, pr, o16, mid, u, gain, beta, wqkv, wp, w1, w2, two)


def jobs():
    n_img, n_win = lax.axis_size("img"), lax.axis_size("win")
    bits = [("win", b) for b in range(1, n_win.bit_length() - 1)] + [("img", b) for b in range(n_img.bit_length() - 1)]
    pairs = [bits[n : n + 2] for n in range(0, len(bits), 2)]
    orders = [[[("win", 0)]] + pairs, [[("win", 0)]] + pairs[::-1]]
    out = []
    for group in range(3):
        out += [(1536 * group, 1024, orders[0]), (1536 * group + 1024, 512, orders[1])]
    return out + [(SLABS * D, SUMS - SLABS * D, orders[0])]


def plan_sizes(size, order):
    out = []
    for group in order:
        ways = 2 ** len(group)
        cut = ways if size % (16 * ways) == 0 else 1
        size //= cut
        out.append((ways, cut, size))
    return out


class Exchange:
    def __init__(self, buf, landing, send, recv, free):
        self.buf, self.landing, self.send, self.recv, self.free = buf, landing, send, recv, free
        index = {axis: lax.axis_index(axis) for axis in ("img", "win")}
        self.plans, land = [], 0
        for start, rows, order in jobs():
            plan = []
            for group, (ways, cut, size) in zip(order, plan_sizes(rows, order)):
                own = [(index[axis] // 2**bit) % 2 for axis, bit in group]
                peers = []
                for apart in range(1, ways):
                    to, piece = {}, 0
                    for n, (axis, bit) in enumerate(group):
                        here = own[n]
                        if apart >> n & 1:
                            to[axis] = to.get(axis, index[axis]) + 2**bit - 2 ** (bit + 1) * here
                            here = 1 - here
                        piece = piece + here * 2**n
                    peers.append((to, start + piece * size if cut > 1 else start, land))
                    land += size
                if cut > 1:
                    start = start + sum(here * 2**n for n, here in enumerate(own)) * size
                plan.append((start, size, cut, peers))
            self.plans.append(plan)
        self.bits = len(self.plans[0])
        self.stages = 2 * self.bits

    def peers(self):
        return [to for *_, peers in self.plans[0] for to, _, _ in peers]

    def copies(self, c, k):
        n = min(k, self.stages - 1 - k)
        keep, size, cut, peers = self.plans[c][n]
        if k >= self.bits and cut == 1:
            return []
        out = []
        for p, (to, give, land) in enumerate(peers):
            if k < self.bits:
                source, target = self.buf.at[pl.ds(pl.multiple_of(give, 16), size)], self.landing.at[pl.ds(land, size)]
            else:
                source = target = self.buf.at[pl.ds(pl.multiple_of(keep, 16), size)]
            out.append(
                pltpu.make_async_remote_copy(
                    source, target, self.send.at[c, k, p], self.recv.at[c, k, p], device_id=to, device_id_type=MESH
                )
            )
        return out

    def start(self, c, k):
        copies = self.copies(c, k)
        if copies and k >= self.bits:
            pl.semaphore_wait(self.free.at[c, self.stages - 1 - k], len(copies))
        for copy in copies:
            copy.start()

    def finish(self, c, k):
        for copy in self.copies(c, k):
            copy.wait()
        if k >= self.bits:
            return
        keep, size, cut, peers = self.plans[c][k]
        if cut > 1:
            for to, _, _ in peers:
                pl.semaphore_signal(self.free.at[c, k], inc=1, device_id=to, device_id_type=MESH)
        tile = max(t for t in (16, 32, 48, 64) if size % t == 0)

        def add(i, carry):
            here = pl.ds(pl.multiple_of(keep + i * tile, 16), tile)
            total = self.buf[here, :].astype(f32)
            for _, _, land in peers:
                total = total + self.landing[pl.ds(pl.multiple_of(land + i * tile, 16), tile), :].astype(f32)
            self.buf[here, :] = total.astype(bf16)
            return carry

        lax.fori_loop(0, size // tile, add, 0)

    def advance(self, which, k):
        for c in which:
            if 1 <= k <= self.stages:
                self.finish(c, k - 1)
            if k < self.stages:
                self.start(c, k)


def exchange_scratch():
    landing, most = 0, 0
    for _, rows, order in jobs():
        for ways, _, size in plan_sizes(rows, order):
            landing += size * (ways - 1)
            most = max(most, ways - 1)
    n, bits = len(jobs()), len(jobs()[0][2])
    dma = pltpu.SemaphoreType.DMA((n, 2 * bits, most))
    return [VMEM((landing, D), bf16), dma, dma, pltpu.SemaphoreType.REGULAR((n, bits))]


def finish_kernel(*refs):
    ins, (small, *parts, dx), outs, smalls = refs[:8], refs[8:12], refs[12:16], refs[16:21]
    y_out, dx_out = refs[21:]
    step = pl.program_id(0)

    @pl.when(step == 0)
    def _():
        rows = small[:, :SMALL].astype(f32)
        for n, out in enumerate(smalls[:4]):
            out[...] = rows[:, 2 * n : 2 * n + 2]
        for n in range(4):
            smalls[4][:, D * n : D * (n + 1)] = rows[:, 8 + n]

    for n, part in enumerate(parts):
        y_out[:, HALF * n : HALF * (n + 1)] = part[...]
    dx_out[...] = dx[...]

    @pl.when(step < 4)
    def _():
        for n, out in enumerate(outs):
            for block in range(2):
                value = ins[2 * n + block][...].astype(f32)
                out[block] = value.T if n == 1 else value


def finish(grads_one, grads_two, small, y_first, y_last, dx):
    first = [lambda j: jnp.minimum(j, 3), lambda j: 4 + jnp.minimum(j, 3), lambda j: 8 + jnp.minimum(j, 2), lambda j: 11]
    places = [
        lambda j: (0, 0, jnp.minimum(j, 3)), lambda j: (0, jnp.minimum(j, 3), 0), lambda j: (0, 0, jnp.minimum(j, 2)),
        lambda j: (0, 0, 0),
    ]
    small_shapes = [(2, 2, D)] * 4 + [(2, FF)]
    tokens, part = (pl.BlockSpec((WINDOW,) + v.shape[1:], lambda j: (j, 0, 0)) for v in (dx, y_first))
    return pl.pallas_call(
        finish_kernel,
        grid=(WINDOW,),
        out_shape=tuple(
            jax.ShapeDtypeStruct(shape, f32)
            for shape in [(2, D, FF), (2, FF, D), (2, D, 3 * D), (2, D, D)] + small_shapes
        ) + (jax.ShapeDtypeStruct(dx.shape, bf16),) * 2,
        in_specs=[pl.BlockSpec((D, D), lambda j, row=row: (row(j), 0)) for row in first for _ in range(2)]
        + [whole(small.shape), part, part, tokens],
        out_specs=tuple(pl.BlockSpec((2, D, D), place) for place in places) + tuple(whole(v) for v in small_shapes)
        + (tokens,) * 2,
        compiler_params=params(),
        name="finish_gradients",
    )(*[grads_one, grads_two] * 4, small, y_first, y_last, dx)


def position_lookup():
    j = jnp.arange(KEYS)[:, None]
    i = jnp.arange(SLOT)[None, :]
    side = SIDE - 1
    index = (i // WINDOW - j // WINDOW + WINDOW - 1) * side + i % WINDOW - j % WINDOW + WINDOW - 1
    index = jnp.where((i < CELLS) & (j < CELLS), index, -1).reshape(-1)
    return (jnp.arange(side * side)[:, None] == index[None, :]).astype(f32)


def on_device(
    tokens, cotangent, crop_counts, crop_extent, norm_gain, norm_bias, qkv_weight, qv_bias, rel_table, proj_weight,
    out_bias, fc1_weight, fc1_bias, fc2_weight,
):
    crops = tokens.shape[0]
    x = tokens.reshape(crops, CELLS, D).transpose(1, 0, 2)
    cot = cotangent.reshape(crops, CELLS, D).transpose(1, 0, 2)
    lookup = position_lookup()
    highest = lax.Precision.HIGHEST
    bias = jnp.einsum("bkh,kp->bhp", rel_table, lookup, precision=highest) * LOG2E
    bias = bias.reshape(2, GROUPS, 4, KEYS, SLOT).transpose(0, 1, 3, 2, 4)
    bias = jnp.where(jnp.arange(KEYS)[:, None, None] < CELLS, bias, NEG).reshape(2, GROUPS, KEYS, 4 * SLOT)

    cells_of = lambda v: v.reshape(CELL + v.shape[1:])
    rows_of = lambda v: v.reshape((CELLS,) + v.shape[2:])
    x_first, x_last, cot_shifted, qw, pr, o16, mid, u = run_first(
        crop_extent.T, x, cells_of(cot), norm_gain, norm_bias, qkv_weight, qv_bias, bias, proj_weight, out_bias,
        fc1_weight, fc1_bias, fc2_weight,
    )
    y_first, y_last, dx_first, dx_last, grads_two = run_second(
        crop_extent.T, crop_counts, x_first, x_last, rows_of(cot_shifted), norm_gain, norm_bias, qkv_weight, qv_bias,
        bias, proj_weight, out_bias, fc1_weight, fc1_bias, fc2_weight,
    )
    dx, sum_one, sum_two, y_last, small = run_third(
        x, dx_first, dx_last, y_last, qw, pr, o16, mid, u, norm_gain, norm_bias, qkv_weight, proj_weight,
        fc1_weight, fc2_weight, grads_two,
    )
    fc1, fc2, qkv, proj, gains, biases, qv, outs, fc1_b, output, dx = finish(
        sum_one, sum_two, small, rows_of(y_first), rows_of(y_last), dx
    )
    dbias = small[:, SMALL : SMALL + TABLE, : 4 * SLOT].astype(f32)
    dbias = dbias.reshape(2, GROUPS, KEYS, 4, SLOT).transpose(0, 1, 3, 2, 4)
    table = jnp.einsum("hp,kp->kh", dbias.reshape(2 * HEADS, KEYS * SLOT), lookup, precision=highest)
    table = table.reshape(-1, 2, HEADS).transpose(1, 0, 2)
    back = lambda v: v.transpose(1, 0, 2).reshape(tokens.shape)
    return back(output), back(dx), gains, biases, qkv, qv, table, proj, outs, fc1, fc1_b, fc2


def solution(mesh):
    split = P("img", "win", None, None)
    return jax.shard_map(
        on_device,
        mesh=mesh,
        in_specs=(split, split, P("img"), P("img", None)) + (P(),) * 10,
        out_specs=(split, split) + (P(),) * 10,
        check_vma=False,
    )
```

```python
import jax
import jax.numpy as jnp
from jax import lax
from jax.experimental import pallas as pl
from jax.experimental.pallas import tpu as pltpu
from jax.sharding import PartitionSpec as P

D = 384
FF = 1536
HEADS = 12
HEAD_DIM = 32
WINDOW = 7
SHIFT = 3
CELLS = WINDOW * WINDOW
SIDE = 2 * WINDOW
HALF = 16
ROWS = CELLS * HALF
LANES = 128
GROUPS = 3
KEYS = 56
SLOT = 64
SLABS = 12
SMALL = 16
TABLE = GROUPS * KEYS
SUMS = SLABS * D + 256
GROUPED = ((1, 0), (3, 2), (5, 4, 6))
NEG = -1e30
LOG2E = 1.4426950408889634
SCALE = HEAD_DIM**-0.5
MESH = pl.DeviceIdType.MESH

bf16 = jnp.bfloat16
f32 = jnp.float32
VMEM = pltpu.VMEM


def mm(a, b):
    return lax.dot_general(a, b, (((1,), (0,)), ((), ())), preferred_element_type=f32)


def mm_bt(a, b):
    return lax.dot_general(a, b, (((1,), (1,)), ((), ())), preferred_element_type=f32)


def mm_at(a, b):
    return lax.dot_general(a, b, (((0,), (0,)), ((), ())), preferred_element_type=f32)


def norm(x):
    centred = x - jnp.mean(x, -1, keepdims=True)
    rstd = lax.rsqrt(jnp.mean(centred * centred, -1, keepdims=True) + 1e-5)
    return centred * rstd, rstd


def norm_back(xh, rstd, dn, gain):
    e = dn * gain
    mean_e = jnp.mean(e, -1, keepdims=True)
    mean_ex = jnp.mean(e * xh, -1, keepdims=True)
    dx = rstd * (e - mean_e - xh * mean_ex)
    return dx, jnp.sum(dn * xh, 0, keepdims=True), jnp.sum(dn, 0, keepdims=True)


def gelu(u):
    phi = 0.5 + 0.5 * lax.erf(u * 0.7071067811865476)
    return u * phi, phi


def gelu_slope(u, phi):
    return phi + u * jnp.exp2(u * u * (-0.5 * LOG2E)) * 0.3989422804014327


def spread(rows):
    head = lax.broadcasted_iota(jnp.int32, rows.shape, 1) // HEAD_DIM
    zero = jnp.zeros_like(rows)
    return jnp.concatenate([jnp.where(head == h, rows, zero) for h in range(4)], 0)


def gather_heads(rows):
    head = lax.broadcasted_iota(jnp.int32, (KEYS, LANES), 1) // HEAD_DIM
    out = rows[:KEYS]
    for h in range(1, 4):
        out = jnp.where(head == h, rows[SLOT * h : SLOT * h + KEYS], out)
    return out


def to_windows(ref, slot, part):
    parted = part.reshape(CELLS, 2, 8, LANES)
    for cg in range(2):
        ref[cg, slot, 0 : CELLS * 8, :] = parted[:, cg].reshape(CELLS * 8, LANES)


def from_windows(ref, slot):
    parts = [ref[cg, slot, 0 : CELLS * 8, :].reshape(CELLS, 1, 8, LANES) for cg in range(2)]
    return jnp.concatenate(parts, 1).reshape(ROWS, LANES)


def cells(shifted):
    win = lax.axis_index("win")
    j = lax.broadcasted_iota(jnp.int32, (KEYS, LANES), 0)
    i = lax.broadcasted_iota(jnp.int32, (KEYS, LANES), 1) % SLOT
    top, left = WINDOW * (win // 2), WINDOW * (win % 2)
    places = [top + j // WINDOW, left + j % WINDOW, top + i // WINDOW, left + i % WINDOW]
    if not shifted:
        return places, None
    region = [(v >= SIDE - WINDOW).astype(jnp.int32) + (v >= SIDE - SHIFT).astype(jnp.int32) for v in places]
    apart = (region[0] != region[2]) | (region[1] != region[3])
    moved = [jnp.where(v + SHIFT >= SIDE, v + SHIFT - SIDE, v + SHIFT) for v in places]
    return moved, jnp.where(apart, NEG, 0.0)


def forward(step, block, shifted, x, refs, keep_n1=None, keep_n2=None, keep_gelu=None, keep_u=None):
    (ext, gain, beta, wqkv, qvb, bias, wp, ob, w1, b1, w2, xs, qw, pr, os, o16, mid) = refs
    xh, _ = norm(x)
    n1 = (xh * gain[block, 0:1, :] + beta[block, 0:1, :]).astype(bf16)
    if keep_n1 is not None:
        keep_n1[step] = n1
    proj = mm(n1, wqkv[...])
    q = (proj[:, :D] + qvb[block, 0:1, :]) * (SCALE * LOG2E)
    k = proj[:, D : 2 * D]
    v = proj[:, 2 * D :] + qvb[block, 1:2, :]
    for g in range(GROUPS):
        cut = slice(LANES * g, LANES * (g + 1))
        to_windows(xs, g, q[:, cut])
        to_windows(xs, GROUPS + g, k[:, cut])
        to_windows(xs, 2 * GROUPS + g, v[:, cut])
    places, apart = cells(shifted)
    if apart is not None:
        apart = jnp.concatenate([apart, apart], 1)

    def windows(part, carry):
        masks = []
        for w in [8 * part + n for n in range(8)]:
            rows, cols = ext[0, step * HALF + w], ext[1, step * HALF + w]
            valid_j = (places[0] < rows) & (places[1] < cols)
            valid_i = (places[2] < rows) & (places[3] < cols)
            mask = jnp.where(valid_i == valid_j, 0.0, NEG)
            mask = jnp.concatenate([mask, mask], 1)
            masks.append(mask if apart is None else mask + apart)
        for g in range(GROUPS):
            for n in range(8):
                w = 8 * part + n
                qs, ks, vs = (xs[part, GROUPS * m + g, pl.ds(n, SLOT, stride=8), :].astype(bf16) for m in range(3))
                for m, value in enumerate((qs, ks, vs)):
                    qw[w, GROUPS * m + g] = value
                s = mm_bt(ks[:KEYS], spread(qs)) + bias[g] + masks[n]
                e = jnp.exp2(s - jnp.max(s, 0, keepdims=True))
                p = (e * (1.0 / jnp.sum(e, 0, keepdims=True))).astype(bf16)
                pr[w, g] = p
                os[part, g, pl.ds(n, KEYS, stride=8), :] = gather_heads(mm_at(p, vs[:KEYS]))
        return carry

    lax.fori_loop(0, 2, windows, 0)
    for g in range(GROUPS):
        o16[:, LANES * g : LANES * (g + 1)] = from_windows(os, g).astype(bf16)
    middle = x + (mm(o16[...], wp[...]) + ob[block, 0:1, :])
    mid[...] = middle
    xh2, _ = norm(middle)
    n2 = (xh2 * gain[block, 1:2, :] + beta[block, 1:2, :]).astype(bf16)
    if keep_n2 is not None:
        keep_n2[step] = n2
    y = middle + ob[block, 1:2, :]
    for part in range(3):
        cut = slice(512 * part, 512 * (part + 1))
        u = mm(n2, w1[:, cut]) + b1[block : block + 1, cut]
        if keep_u is not None:
            keep_u[:, cut] = u.astype(bf16)
        z, phi = gelu(u)
        z = z.astype(bf16)
        if keep_gelu is not None:
            keep_gelu[0][step, :, cut] = z
            keep_gelu[1][:, cut] = gelu_slope(u, phi).astype(bf16)
        y = y + mm(z, w2[cut, :])
    return y


def no_tick(point, when=True):
    pass


def mlp_back(step, block, mid, dy, refs, slope, keep_n2=None, beta=None, tick=no_tick):
    (gain, wp, w1, w2, dos, dm_all, du_all, da_all, small) = refs

    def add_small(row, value):
        small[row : row + 1, :] += value

    dm = dy.astype(bf16)
    dm_all[step] = dm
    add_small(7, jnp.sum(dm.astype(f32), 0, keepdims=True))
    sums = []
    for part in range(3):
        cut = slice(512 * part, 512 * (part + 1))
        du = (mm_bt(dm, w2[cut, :]) * slope(cut)).astype(bf16)
        du_all[step, :, cut] = du
        sums.append(jnp.sum(du.astype(f32), 0, keepdims=True))
        tick(part)
    sums = jnp.concatenate(sums, 1)
    for part in range(4):
        add_small(8 + part, sums[:, D * part : D * (part + 1)])
    dn2 = mm_bt(du_all[step], w1[...])
    tick(3)
    xh, rstd = norm(mid)
    if keep_n2 is not None:
        keep_n2[step] = (xh * gain[block, 1:2, :] + beta[block, 1:2, :]).astype(bf16)
    dx, dgain, dbeta = norm_back(xh, rstd, dn2, gain[block, 1:2, :])
    add_small(1, dgain)
    add_small(3, dbeta)
    dmid = dy + dx
    da = dmid.astype(bf16)
    da_all[step] = da
    add_small(6, jnp.sum(da.astype(f32), 0, keepdims=True))
    do = mm_bt(da, wp[...])
    for g in range(GROUPS):
        to_windows(dos, g, do[:, LANES * g : LANES * (g + 1)])
    tick(4)
    return dmid


def attention_back(step, block, x, dmid, refs, keep_n1=None, beta=None, tick=no_tick):
    (gain, wqkv, xs, qw, pr, dos, dp_all, small, dbias) = refs

    def add_small(row, value):
        small[row : row + 1, :] += value

    def windows_back(part, carry):
        units = [(n, g) for n in range(8) for g in range(GROUPS)]
        grad, scores = {}, {}
        for n, g in units:
            grad[n, g] = spread(dos[part, g, pl.ds(n, SLOT, stride=8), :].astype(bf16))
        dprobs = {(n, g): mm_bt(qw[8 * part + n, 2 * GROUPS + g][:KEYS], grad[n, g]) for n, g in units}
        for g in range(GROUPS):
            total = jnp.zeros((KEYS, 4 * SLOT), f32)
            for n in range(8):
                p = pr[8 * part + n, g].astype(f32)
                t = p * dprobs[n, g]
                ds = t - p * jnp.sum(t, 0, keepdims=True)
                total = total + ds
                scores[n, g] = ds.astype(bf16)
            dbias[g] += total
        for n, g in units:
            w, ds = 8 * part + n, scores[n, g]
            dv = mm(pr[w, g], grad[n, g])
            dk = mm(ds, spread(qw[w, g])) * (1.0 / LOG2E)
            dq = gather_heads(mm_at(ds, qw[w, GROUPS + g][:KEYS])) * SCALE
            for m, value in enumerate((dq, dk, dv)):
                xs[part, GROUPS * m + g, pl.ds(n, KEYS, stride=8), :] = value
        for n in range(4):
            tick(n, part == n // 2)
        return carry

    lax.fori_loop(0, 2, windows_back, 0)
    for n in range(3 * GROUPS):
        dp_all[step, :, LANES * n : LANES * (n + 1)] = from_windows(xs, n).astype(bf16)
    dp = dp_all[step, :, : 3 * D]
    add_small(4, jnp.sum(dp[:, :D].astype(f32), 0, keepdims=True))
    add_small(5, jnp.sum(dp[:, 2 * D :].astype(f32), 0, keepdims=True))
    dn1 = mm_bt(dp, wqkv[...])
    tick(4)
    xh, rstd = norm(x)
    if keep_n1 is not None:
        keep_n1[step] = (xh * gain[block, 0:1, :] + beta[block, 0:1, :]).astype(bf16)
    dx, dgain, dbeta = norm_back(xh, rstd, dn1, gain[block, 0:1, :])
    add_small(0, dgain)
    add_small(2, dbeta)
    tick(5)
    return dmid() + dx


def flat(ref, cut=slice(None)):
    return ref[:, :, cut].reshape(2 * ROWS, -1)


def put_slabs(out, first, value):
    for j in range(value.shape[1] // D):
        out[D * (first + j) : D * (first + j + 1), :] = value[:, D * j : D * (j + 1)].astype(bf16)


def fc_grads(n2, z, dm, du, out, tick=no_tick):
    for first, left, right in ((0, n2, du), (4, dm, z)):
        for j in range(2):
            put_slabs(out, first + 2 * j, mm_at(flat(left), flat(right, slice(768 * j, 768 * (j + 1)))))
        tick(first // 4)


def attention_grads(n1, o16, da, dp, out):
    put_slabs(out, 8, mm_at(flat(n1), flat(dp, slice(3 * D))))
    put_slabs(out, 11, mm_at(flat(o16), flat(da)))


def small_grads(small, dbias, out):
    base = SLABS * D
    out[base : base + SMALL, :] = small[...].astype(bf16)
    out[base + SMALL : SUMS, :] = jnp.zeros((SUMS - base - SMALL, D), bf16)
    out[base + SMALL : base + SMALL + TABLE, : 4 * SLOT] = dbias[...].reshape(TABLE, 4 * SLOT).astype(bf16)


KEEP = WINDOW - SHIFT
NEAR, FAR = slice(0, KEEP), slice(KEEP, WINDOW)
HERE, THERE = slice(SHIFT, WINDOW), slice(0, SHIFT)


def shift_peers():
    win = lax.axis_index("win")
    beside = 1 - 2 * (win % 2)
    below = 2 - 4 * (win // 2 % 2)
    return [{"win": win + beside}, {"win": win + below}, {"win": win + beside + below}]


def shift_copies(source, target, send, recv, back=False):
    plain = [(HERE, HERE), (HERE, THERE), (THERE, HERE), (THERE, THERE)]
    moved = [(NEAR, NEAR), (NEAR, FAR), (FAR, NEAR), (FAR, FAR)]
    if back:
        plain, moved = moved, plain
    out = [pltpu.make_async_copy(source.at[plain[0]], target.at[moved[0]], send.at[3])]
    for n, to in enumerate(shift_peers()):
        out.append(
            pltpu.make_async_remote_copy(
                source.at[plain[n + 1]], target.at[moved[n + 1]], send.at[n], recv.at[n], device_id=to, device_id_type=MESH
            )
        )
    return out


def start_all(copies):
    for copy in copies:
        copy.start()


def wait_all(copies):
    for copy in copies:
        copy.wait()


def greet(peers):
    barrier = pltpu.get_barrier_semaphore()
    for to in peers:
        pl.semaphore_signal(barrier, inc=1, device_id=to, device_id_type=MESH)
    pl.semaphore_wait(barrier, len(peers))


def first_kernel(
    ext, x_ref, cot, gain, beta, wqkv, qvb, bias, wp, ob, w1, b1, w2,
    y_shifted, y_last, cot_shifted, qw, pr, o16, mid, u_ref, xs, os, y_first, send, recv,
):
    step = pl.program_id(0)
    cot_copies = shift_copies(cot, cot_shifted, send.at[0], recv.at[0])
    y_copies = shift_copies(y_first, y_shifted, send.at[1], recv.at[1])

    @pl.when(step == 0)
    def _():
        greet(shift_peers())
        start_all(cot_copies)
        xs[...] = jnp.zeros_like(xs)

    x = x_ref[...].reshape(ROWS, D).astype(f32)
    y = forward(
        step, 0, False, x, (ext, gain, beta, wqkv, qvb, bias, wp, ob, w1, b1, w2, xs, qw, pr, os, o16, mid), keep_u=u_ref
    )
    y = y.astype(bf16).reshape(WINDOW, WINDOW, HALF, D)

    @pl.when(step == 0)
    def _():
        y_first[...] = y
        start_all(y_copies)

    @pl.when(step == 1)
    def _():
        y_last[...] = y
        wait_all(y_copies)
        wait_all(cot_copies)


def second_kernel(
    ext, count, x_first, x_last, cot_ref, gain, beta, wqkv, qvb, bias, wp, ob, w1, b1, w2,
    y_shifted, y_last, dx_shifted, dx_last, grads,
    xs, qw, pr, os, mid, slope, dos, small, dbias, n1, n2, o16, z, dm, du, da, dp, x_both, dx_first, y_first, send, recv, local,
):
    step = pl.program_id(0)
    x_copies = shift_copies(x_last, x_both.at[1], send.at[0], recv.at[0])
    dx_copies = shift_copies(dx_first, dx_shifted, send.at[1], recv.at[1], back=True)
    y_copies = shift_copies(y_first, y_shifted, send.at[2], recv.at[2], back=True)

    @pl.when(step == 0)
    def _():
        load = pltpu.make_async_copy(x_first, x_both.at[0], local)
        load.start()
        greet(shift_peers())
        start_all(x_copies)
        load.wait()
        xs[...] = jnp.zeros_like(xs)
        dos[...] = jnp.zeros_like(dos)
        small[...] = jnp.zeros_like(small)
        dbias[...] = jnp.zeros_like(dbias)

    @pl.when(step == 1)
    def _():
        wait_all(x_copies)

    x = x_both[step].reshape(ROWS, D).astype(f32)
    live = lax.broadcasted_iota(jnp.int32, (CELLS, HALF, 1), 1) + step * HALF < count[0]
    y = forward(
        step, 1, True, x,
        (ext, gain, beta, wqkv, qvb, bias, wp, ob, w1, b1, w2, xs, qw, pr, os, o16.at[step], mid),
        n1, n2, (z, slope),
    )
    y = jnp.where(live, y.reshape(CELLS, HALF, D), 0.0).astype(bf16).reshape(WINDOW, WINDOW, HALF, D)

    @pl.when(step == 0)
    def _():
        y_first[...] = y
        start_all(y_copies)

    @pl.when(step == 1)
    def _():
        y_last[...] = y

    dy = jnp.where(live, cot_ref[...].astype(f32), 0.0).reshape(ROWS, D)
    mid[...] = mlp_back(
        step, 1, mid[...], dy, (gain, wp, w1, w2, dos, dm, du, da, small), lambda cut: slope[:, cut].astype(f32)
    )
    dx = attention_back(
        step, 1, x, lambda: mid[...], (gain, wqkv, xs, qw, pr, dos, dp, small, dbias)
    )
    dx = dx.astype(bf16).reshape(WINDOW, WINDOW, HALF, D)

    @pl.when(step == 0)
    def _():
        dx_first[...] = dx
        start_all(dx_copies)

    @pl.when(step == 1)
    def _():
        dx_last[...] = dx
        fc_grads(n2, z, dm, du, grads)
        attention_grads(n1, o16, da, dp, grads)
        small_grads(small, dbias, grads)
        wait_all(y_copies)
        wait_all(dx_copies)


LAST = 24
PACE = {
    (0, 0): (4.2, 6.0, 13.5, 17.1, 21.7, 32.9, 50.5),
    (0, 1): (1.9, 3.9, 9.1, 12.7, 16.3, 31.4, 37.3),
    (0, 2): (2.6, 4.5, 10.1, 13.9, 20.1, 40.0, 52.1),
    (1, 0): (30.7, 33.8, 38.5, 44.6, 47.5, 59.9, 73.1),
    (1, 1): (13.1, 17.1, 29.9, 42.0, 56.9, 72.9, 95.6),
    (1, 2): (29.3, 30.4, 38.3, 39.8, 46.6, 57.1, 68.4),
}


def schedule(*exchanges):
    out = []
    for (which, group), places in PACE.items():
        exchange = exchanges[which]
        if exchange.stages + 1 != len(places):
            first = LAST + 1 if which and group == 2 else places[0]
            places = [first + 4 * k + 0.1 * group for k in range(exchange.stages + 1)]
        out += [(place, exchange, group, k) for k, place in enumerate(places)]
    return sorted(out, key=lambda item: item[0])


def third_kernel(
    x_ref, dy_first, dy_last, y_ref, qw, pr, o_ref, mid, u_ref, gain, beta, wqkv, wp, w1, w2, two_ref,
    dx_ref, one_out, two_out, y_out, small_out,
    xs, dos, small, dbias, dmid, n2, o16, z, dm, du, da,
    one, two, land_one, send_one, recv_one, free_one, land_two, send_two, recv_two, free_two, local, loads, dy_both, send, recv,
):
    step = pl.program_id(0)
    first = Exchange(one, land_one, send_one, recv_one, free_one)
    second = Exchange(two, land_two, send_two, recv_two, free_two)
    dy_copies = shift_copies(dy_last, dy_both.at[1], send.at[0], recv.at[0], back=True)
    y_copies = shift_copies(y_ref, y_out, send.at[1], recv.at[1], back=True)
    moves = [[] for _ in range(LAST + 1)]
    late = []
    for place, exchange, group, k in schedule(second, first):
        (moves[int(place)] if place < LAST + 1 else late).append((exchange, group, k))

    def tick(n):
        if n == 14:
            start_all(y_copies)
        for exchange, group, k in moves[n]:
            exchange.advance(GROUPED[group], k)

    def tick_at(steps, base, per_step):
        def ticker(point, when=True):
            for s in steps:
                pl.when((step == s) & when)(lambda s=s: tick(base + (s - steps[0]) * per_step + point))

        return ticker

    def kept(half):
        rows = pl.ds(half * ROWS, ROWS)
        return (
            pltpu.make_async_copy(u_ref.at[rows], z.at[half], loads.at[0, half]),
            pltpu.make_async_copy(o_ref.at[rows], o16.at[half], loads.at[1, half]),
        )

    @pl.when(step == 0)
    def _():
        load = pltpu.make_async_copy(two_ref, two, local.at[0])
        load.start()
        load_dy = pltpu.make_async_copy(dy_first, dy_both.at[0], local.at[1])
        load_dy.start()
        for half in range(2):
            start_all(kept(half))
        greet(second.peers() + shift_peers()[2:])
        start_all(dy_copies)
        xs[...] = jnp.zeros_like(xs)
        dos[...] = jnp.zeros_like(dos)
        small[...] = jnp.zeros_like(small)
        dbias[...] = jnp.zeros_like(dbias)
        load.wait()
        tick(0)
        load_dy.wait()

    for half in range(2):

        @pl.when(step == half)
        def _():
            wait_all(kept(half))
            if half:
                wait_all(dy_copies)

    @pl.when(step < 2)
    def _():
        def slope(cut):
            u = z[step, :, cut].astype(f32)
            value, phi = gelu(u)
            z[step, :, cut] = value.astype(bf16)
            return gelu_slope(u, phi)

        dmid[step] = mlp_back(
            step, 0, mid[...], dy_both[step].astype(f32).reshape(ROWS, D),
            (gain, wp, w1, w2, dos.at[step], dm, du, da, small), slope, n2, beta, tick_at((0, 1), 1, 5),
        )

    @pl.when(step == 1)
    def _():
        fc_grads(n2, z, dm, du, one, lambda point: tick(11 + point))

    @pl.when(step >= 2)
    def _():
        half = step - 2
        dx = attention_back(
            half, 0, x_ref[...].reshape(ROWS, D).astype(f32), lambda: dmid[half],
            (gain, wqkv, xs, qw, pr, dos.at[half], du, small, dbias), n2, beta, tick_at((2, 3), 13, 6),
        )
        dx_ref[...] = dx.astype(bf16).reshape(dx_ref.shape)

    @pl.when(step == 3)
    def _():
        attention_grads(n2, o16, da, du, one)
        small_grads(small, dbias, one)
        for n, (exchange, group, k) in enumerate(late):
            exchange.advance(GROUPED[group], k)
            if all(other is not second for other, _, _ in late[n + 1 :]) and (exchange is second or n == 0):
                store_two = pltpu.make_async_copy(two, two_out, local.at[0])
                store_two.start()
        store_one = pltpu.make_async_copy(one, one_out, local.at[1])
        store_one.start()
        tails = [
            pltpu.make_async_copy(ref.at[pl.ds(SLABS * D, SUMS - SLABS * D)], small_out.at[n], loads.at[0, n])
            for n, ref in enumerate((one, two))
        ]
        start_all(tails)
        wait_all(tails)
        wait_all(y_copies)
        store_one.wait()
        store_two.wait()


def whole(shape):
    return pl.BlockSpec(shape, lambda s: (0,) * len(shape), pipeline_mode=pl.Buffered(1))


def of_block(block, *shape):
    return pl.BlockSpec((None,) + shape, lambda s: (block,) + (0,) * len(shape), pipeline_mode=pl.Buffered(1))


def by_half(*shape, buffers=2):
    return pl.BlockSpec(shape, lambda s: (s,) + (0,) * (len(shape) - 1), pipeline_mode=pl.Buffered(buffers))


ANY_SPEC = pl.BlockSpec(memory_space=pl.ANY)
SMEM_SPEC = pl.BlockSpec(memory_space=pltpu.SMEM)
TOKEN_SPEC = pl.BlockSpec((CELLS, HALF, D), lambda s: (0, s, 0))
XS = VMEM((2, 3 * GROUPS, 8 * SLOT, LANES), f32)
DOS = VMEM((2, GROUPS, 8 * SLOT, LANES), f32)
QW = (HALF, 3 * GROUPS, SLOT, LANES)
PR = (HALF, GROUPS, KEYS, 4 * SLOT)


def params(collective_id=None, mib=61):
    return pltpu.CompilerParams(
        vmem_limit_bytes=mib * 2**20, dimension_semantics=("arbitrary",), collective_id=collective_id,
        has_side_effects=collective_id is not None,
    )


CELL = (WINDOW, WINDOW)
PART = jax.ShapeDtypeStruct(CELL + (HALF, D), bf16)
SHIFTS = [pltpu.SemaphoreType.DMA((3, 4)), pltpu.SemaphoreType.DMA((3, 4))]


def run_first(ext, x, cot, gain, beta, wqkv, qvb, bias, wp, ob, w1, b1, w2):
    crops = x.shape[1]
    return pl.pallas_call(
        first_kernel,
        grid=(2,),
        out_shape=(
            PART,
            PART,
            jax.ShapeDtypeStruct(cot.shape, bf16),
            jax.ShapeDtypeStruct((crops,) + QW[1:], bf16),
            jax.ShapeDtypeStruct((crops,) + PR[1:], bf16),
            jax.ShapeDtypeStruct((2 * ROWS, D), bf16),
            jax.ShapeDtypeStruct((2 * ROWS, D), f32),
            jax.ShapeDtypeStruct((2 * ROWS, FF), bf16),
        ),
        in_specs=[
            SMEM_SPEC, TOKEN_SPEC, ANY_SPEC, whole(gain.shape), whole(beta.shape), of_block(0, D, 3 * D), whole(qvb.shape),
            of_block(0, GROUPS, KEYS, 4 * SLOT), of_block(0, D, D), whole(ob.shape), of_block(0, D, FF),
            whole(b1.shape), of_block(0, FF, D),
        ],
        out_specs=(
            ANY_SPEC, whole(PART.shape), ANY_SPEC, by_half(*QW), by_half(*PR), by_half(ROWS, D), by_half(ROWS, D),
            by_half(ROWS, FF),
        ),
        scratch_shapes=[
            XS, VMEM((2, GROUPS, 8 * KEYS, LANES), f32), VMEM(PART.shape, bf16),
        ] + SHIFTS,
        compiler_params=params(1),
        name="first_forward",
    )(ext, x, cot, gain, beta, wqkv, qvb, bias, wp, ob, w1, b1, w2)


GRADS = jax.ShapeDtypeStruct((SUMS, D), bf16)
SMALLS = [VMEM((SMALL, D), f32), VMEM((GROUPS, KEYS, 4 * SLOT), f32)]


def run_second(ext, count, x_first, x_last, cot, gain, beta, wqkv, qvb, bias, wp, ob, w1, b1, w2):
    return pl.pallas_call(
        second_kernel,
        grid=(2,),
        out_shape=(PART, PART, PART, PART, GRADS),
        in_specs=[
            SMEM_SPEC, SMEM_SPEC, ANY_SPEC, ANY_SPEC, TOKEN_SPEC, whole(gain.shape), whole(beta.shape), of_block(1, D, 3 * D),
            whole(qvb.shape), of_block(1, GROUPS, KEYS, 4 * SLOT), of_block(1, D, D), whole(ob.shape),
            of_block(1, D, FF), whole(b1.shape), of_block(1, FF, D),
        ],
        out_specs=(ANY_SPEC, whole(PART.shape), ANY_SPEC, whole(PART.shape), whole(GRADS.shape)),
        scratch_shapes=[
            XS, VMEM(QW, bf16), VMEM(PR, bf16), VMEM((2, GROUPS, 8 * KEYS, LANES), f32),
            VMEM((ROWS, D), f32), VMEM((ROWS, FF), bf16), DOS,
        ] + SMALLS + [VMEM((2, ROWS, width), bf16) for width in (D, D, D, FF, D, FF, D, 3 * D)]
        + [VMEM((2,) + PART.shape, bf16), VMEM(PART.shape, bf16), VMEM(PART.shape, bf16)] + SHIFTS
        + [pltpu.SemaphoreType.DMA(())],
        compiler_params=params(2, 63),
        name="second_block",
    )(ext, count, x_first, x_last, cot, gain, beta, wqkv, qvb, bias, wp, ob, w1, b1, w2)


def in_steps(first, *shape, axis=0, buffers=2):
    def index(s):
        return tuple(jnp.clip(s - first, 0, 1) if n == axis else 0 for n in range(len(shape)))

    return pl.BlockSpec(shape, index, pipeline_mode=pl.Buffered(buffers))


def run_third(x, dy_first, dy_last, y, qw, pr, o16, mid, u, gain, beta, wqkv, wp, w1, w2, two):
    tokens = (CELLS, HALF, D)
    return pl.pallas_call(
        third_kernel,
        grid=(4,),
        out_shape=(
            jax.ShapeDtypeStruct(x.shape, bf16), GRADS, GRADS, jax.ShapeDtypeStruct(y.shape, bf16),
            jax.ShapeDtypeStruct((2, SUMS - SLABS * D, D), bf16),
        ),
        in_specs=[
            in_steps(2, *tokens, axis=1), ANY_SPEC, ANY_SPEC, ANY_SPEC, in_steps(2, *QW, buffers=1),
            in_steps(2, *PR, buffers=1), ANY_SPEC, in_steps(0, ROWS, D), ANY_SPEC,
            whole(gain.shape), whole(beta.shape), of_block(0, D, 3 * D), of_block(0, D, D), of_block(0, D, FF),
            of_block(0, FF, D), ANY_SPEC,
        ],
        out_specs=(in_steps(2, *tokens, axis=1),) + (ANY_SPEC,) * 4,
        scratch_shapes=[XS, VMEM((2,) + DOS.shape, f32)] + SMALLS + [VMEM((2, ROWS, D), f32)]
        + [VMEM((2, ROWS, width), bf16) for width in (D, D, FF, D, FF, D)]
        + [VMEM(GRADS.shape, bf16)] * 2 + exchange_scratch() * 2
        + [pltpu.SemaphoreType.DMA((2,)), pltpu.SemaphoreType.DMA((2, 2)), VMEM((2,) + PART.shape, bf16)] + SHIFTS,
        compiler_params=params(0, 63),
        name="first_backward",
    )(x, dy_first, dy_last, y, qw, pr, o16, mid, u, gain, beta, wqkv, wp, w1, w2, two)


def jobs():
    n_img, n_win = lax.axis_size("img"), lax.axis_size("win")
    bits = [("win", b) for b in range(1, n_win.bit_length() - 1)] + [("img", b) for b in range(n_img.bit_length() - 1)]
    pairs = [bits[n : n + 2] for n in range(0, len(bits), 2)]
    orders = [[[("win", 0)]] + pairs, [[("win", 0)]] + pairs[::-1]]
    out = []
    for group in range(3):
        out += [(1536 * group, 1024, orders[0]), (1536 * group + 1024, 512, orders[1])]
    return out + [(SLABS * D, SUMS - SLABS * D, orders[0])]


def plan_sizes(size, order):
    out = []
    for group in order:
        ways = 2 ** len(group)
        cut = ways if size % (16 * ways) == 0 else 1
        size //= cut
        out.append((ways, cut, size))
    return out


class Exchange:
    def __init__(self, buf, landing, send, recv, free):
        self.buf, self.landing, self.send, self.recv, self.free = buf, landing, send, recv, free
        index = {axis: lax.axis_index(axis) for axis in ("img", "win")}
        self.plans, land = [], 0
        for start, rows, order in jobs():
            plan = []
            for group, (ways, cut, size) in zip(order, plan_sizes(rows, order)):
                own = [(index[axis] // 2**bit) % 2 for axis, bit in group]
                peers = []
                for apart in range(1, ways):
                    to, piece = {}, 0
                    for n, (axis, bit) in enumerate(group):
                        here = own[n]
                        if apart >> n & 1:
                            to[axis] = to.get(axis, index[axis]) + 2**bit - 2 ** (bit + 1) * here
                            here = 1 - here
                        piece = piece + here * 2**n
                    peers.append((to, start + piece * size if cut > 1 else start, land))
                    land += size
                if cut > 1:
                    start = start + sum(here * 2**n for n, here in enumerate(own)) * size
                plan.append((start, size, cut, peers))
            self.plans.append(plan)
        self.bits = len(self.plans[0])
        self.stages = 2 * self.bits

    def peers(self):
        return [to for *_, peers in self.plans[0] for to, _, _ in peers]

    def copies(self, c, k):
        n = min(k, self.stages - 1 - k)
        keep, size, cut, peers = self.plans[c][n]
        if k >= self.bits and cut == 1:
            return []
        out = []
        for p, (to, give, land) in enumerate(peers):
            if k < self.bits:
                source, target = self.buf.at[pl.ds(pl.multiple_of(give, 16), size)], self.landing.at[pl.ds(land, size)]
            else:
                source = target = self.buf.at[pl.ds(pl.multiple_of(keep, 16), size)]
            out.append(
                pltpu.make_async_remote_copy(
                    source, target, self.send.at[c, k, p], self.recv.at[c, k, p], device_id=to, device_id_type=MESH
                )
            )
        return out

    def start(self, c, k):
        copies = self.copies(c, k)
        if copies and k >= self.bits:
            pl.semaphore_wait(self.free.at[c, self.stages - 1 - k], len(copies))
        for copy in copies:
            copy.start()

    def finish(self, c, k):
        for copy in self.copies(c, k):
            copy.wait()
        if k >= self.bits:
            return
        keep, size, cut, peers = self.plans[c][k]
        if cut > 1:
            for to, _, _ in peers:
                pl.semaphore_signal(self.free.at[c, k], inc=1, device_id=to, device_id_type=MESH)
        tile = max(t for t in (16, 32, 48, 64) if size % t == 0)

        def add(i, carry):
            here = pl.ds(pl.multiple_of(keep + i * tile, 16), tile)
            total = self.buf[here, :].astype(f32)
            for _, _, land in peers:
                total = total + self.landing[pl.ds(pl.multiple_of(land + i * tile, 16), tile), :].astype(f32)
            self.buf[here, :] = total.astype(bf16)
            return carry

        lax.fori_loop(0, size // tile, add, 0)

    def advance(self, which, k):
        for c in which:
            if 1 <= k <= self.stages:
                self.finish(c, k - 1)
            if k < self.stages:
                self.start(c, k)


def exchange_scratch():
    landing, most = 0, 0
    for _, rows, order in jobs():
        for ways, _, size in plan_sizes(rows, order):
            landing += size * (ways - 1)
            most = max(most, ways - 1)
    n, bits = len(jobs()), len(jobs()[0][2])
    dma = pltpu.SemaphoreType.DMA((n, 2 * bits, most))
    return [VMEM((landing, D), bf16), dma, dma, pltpu.SemaphoreType.REGULAR((n, bits))]


def finish_kernel(*refs):
    ins, (small, *parts, dx), outs, smalls = refs[:8], refs[8:12], refs[12:16], refs[16:21]
    y_out, dx_out = refs[21:]
    step = pl.program_id(0)

    @pl.when(step == 0)
    def _():
        rows = small[:, :SMALL].astype(f32)
        for n, out in enumerate(smalls[:4]):
            out[...] = rows[:, 2 * n : 2 * n + 2]
        for n in range(4):
            smalls[4][:, D * n : D * (n + 1)] = rows[:, 8 + n]

    for n, part in enumerate(parts):
        y_out[:, HALF * n : HALF * (n + 1)] = part[...]
    dx_out[...] = dx[...]

    @pl.when(step < 4)
    def _():
        for n, out in enumerate(outs):
            for block in range(2):
                value = ins[2 * n + block][...].astype(f32)
                out[block] = value.T if n == 1 else value


def finish(grads_one, grads_two, small, y_first, y_last, dx):
    first = [lambda j: jnp.minimum(j, 3), lambda j: 4 + jnp.minimum(j, 3), lambda j: 8 + jnp.minimum(j, 2), lambda j: 11]
    places = [
        lambda j: (0, 0, jnp.minimum(j, 3)), lambda j: (0, jnp.minimum(j, 3), 0), lambda j: (0, 0, jnp.minimum(j, 2)),
        lambda j: (0, 0, 0),
    ]
    small_shapes = [(2, 2, D)] * 4 + [(2, FF)]
    tokens, part = (pl.BlockSpec((WINDOW,) + v.shape[1:], lambda j: (j, 0, 0)) for v in (dx, y_first))
    return pl.pallas_call(
        finish_kernel,
        grid=(WINDOW,),
        out_shape=tuple(
            jax.ShapeDtypeStruct(shape, f32)
            for shape in [(2, D, FF), (2, FF, D), (2, D, 3 * D), (2, D, D)] + small_shapes
        ) + (jax.ShapeDtypeStruct(dx.shape, bf16),) * 2,
        in_specs=[pl.BlockSpec((D, D), lambda j, row=row: (row(j), 0)) for row in first for _ in range(2)]
        + [whole(small.shape), part, part, tokens],
        out_specs=tuple(pl.BlockSpec((2, D, D), place) for place in places) + tuple(whole(v) for v in small_shapes)
        + (tokens,) * 2,
        compiler_params=params(),
        name="finish_gradients",
    )(*[grads_one, grads_two] * 4, small, y_first, y_last, dx)


def position_lookup():
    j = jnp.arange(KEYS)[:, None]
    i = jnp.arange(SLOT)[None, :]
    side = SIDE - 1
    index = (i // WINDOW - j // WINDOW + WINDOW - 1) * side + i % WINDOW - j % WINDOW + WINDOW - 1
    index = jnp.where((i < CELLS) & (j < CELLS), index, -1).reshape(-1)
    return (jnp.arange(side * side)[:, None] == index[None, :]).astype(f32)


def on_device(
    tokens, cotangent, crop_counts, crop_extent, norm_gain, norm_bias, qkv_weight, qv_bias, rel_table, proj_weight,
    out_bias, fc1_weight, fc1_bias, fc2_weight,
):
    crops = tokens.shape[0]
    x = tokens.reshape(crops, CELLS, D).transpose(1, 0, 2)
    cot = cotangent.reshape(crops, CELLS, D).transpose(1, 0, 2)
    lookup = position_lookup()
    highest = lax.Precision.HIGHEST
    bias = jnp.einsum("bkh,kp->bhp", rel_table, lookup, precision=highest) * LOG2E
    bias = bias.reshape(2, GROUPS, 4, KEYS, SLOT).transpose(0, 1, 3, 2, 4)
    bias = jnp.where(jnp.arange(KEYS)[:, None, None] < CELLS, bias, NEG).reshape(2, GROUPS, KEYS, 4 * SLOT)

    cells_of = lambda v: v.reshape(CELL + v.shape[1:])
    rows_of = lambda v: v.reshape((CELLS,) + v.shape[2:])
    x_first, x_last, cot_shifted, qw, pr, o16, mid, u = run_first(
        crop_extent.T, x, cells_of(cot), norm_gain, norm_bias, qkv_weight, qv_bias, bias, proj_weight, out_bias,
        fc1_weight, fc1_bias, fc2_weight,
    )
    y_first, y_last, dx_first, dx_last, grads_two = run_second(
        crop_extent.T, crop_counts, x_first, x_last, rows_of(cot_shifted), norm_gain, norm_bias, qkv_weight, qv_bias,
        bias, proj_weight, out_bias, fc1_weight, fc1_bias, fc2_weight,
    )
    dx, sum_one, sum_two, y_last, small = run_third(
        x, dx_first, dx_last, y_last, qw, pr, o16, mid, u, norm_gain, norm_bias, qkv_weight, proj_weight,
        fc1_weight, fc2_weight, grads_two,
    )
    fc1, fc2, qkv, proj, gains, biases, qv, outs, fc1_b, output, dx = finish(
        sum_one, sum_two, small, rows_of(y_first), rows_of(y_last), dx
    )
    dbias = small[:, SMALL : SMALL + TABLE, : 4 * SLOT].astype(f32)
    dbias = dbias.reshape(2, GROUPS, KEYS, 4, SLOT).transpose(0, 1, 3, 2, 4)
    table = jnp.einsum("hp,kp->kh", dbias.reshape(2 * HEADS, KEYS * SLOT), lookup, precision=highest)
    table = table.reshape(-1, 2, HEADS).transpose(1, 0, 2)
    back = lambda v: v.transpose(1, 0, 2).reshape(tokens.shape)
    return back(output), back(dx), gains, biases, qkv, qv, table, proj, outs, fc1, fc1_b, fc2


def solution(mesh):
    split = P("img", "win", None, None)
    return jax.shard_map(
        on_device,
        mesh=mesh,
        in_specs=(split, split, P("img"), P("img", None)) + (P(),) * 10,
        out_specs=(split, split) + (P(),) * 10,
        check_vma=False,
    )
```
